32 devices in a mesh: rep: 8 (over z, y), shard: 4 (over x, core).
Axes of the slice: x: 2, y: 2, z: 4, core: 2. Of those that a mesh axis runs over, the one named last changes fastest.
Arguments:
- tokens: bfloat16 [64, 384, 768], P(('rep', 'shard')), may hold values from -6 to 6
- ln1_gain: bfloat16 [768], P('shard'), may hold values from 0.099609375 to 1.8984375
- ln1_bias: bfloat16 [768], P('shard'), may hold values from -4 to 4
- qkv_weight: bfloat16 [768, 2304], P('shard'), may hold values from -0.21875 to 0.21875
- query_bias: bfloat16 [768], P('shard'), may hold values from -6 to 6
- value_bias: bfloat16 [768], P('shard'), may hold values from -6 to 6
- out_weight: bfloat16 [768, 768], P('shard'), may hold values from -0.625 to 0.625
- out_bias: bfloat16 [768], P('shard'), may hold values from -6 to 6
- ln2_gain: bfloat16 [768], P('shard'), may hold values from 0.099609375 to 1.8984375
- ln2_bias: bfloat16 [768], P('shard'), may hold values from -4 to 4
- fc1_weight: bfloat16 [768, 3072], P('shard'), may hold values from -0.21875 to 0.21875
- fc1_bias: bfloat16 [3072], P('shard'), may hold values from -6 to 6
- fc2_weight: bfloat16 [3072, 768], P('shard'), may hold values from -0.21875 to 0.21875
- fc2_bias: bfloat16 [768], P('shard'), may hold values from -6 to 6
- cotangent: bfloat16 [64, 384, 768], P(('rep', 'shard')), may hold values from -6 to 6
Outputs:
- output: bfloat16 [64, 384, 768], P(('rep', 'shard'))
- in_grad: bfloat16 [64, 384, 768], P(('rep', 'shard'))
- grad_ln1_gain: float32 [768], P('shard')
- grad_ln1_bias: float32 [768], P('shard')
- grad_qkv_weight: float32 [768, 2304], P('shard')
- grad_query_bias: float32 [768], P('shard')
- grad_value_bias: float32 [768], P('shard')
- grad_out_weight: float32 [768, 768], P('shard')
- grad_out_bias: float32 [768], P('shard')
- grad_ln2_gain: float32 [768], P('shard')
- grad_ln2_bias: float32 [768], P('shard')
- grad_fc1_weight: float32 [768, 3072], P('shard')
- grad_fc1_bias: float32 [3072], P('shard')
- grad_fc2_weight: float32 [3072, 768], P('shard')
- grad_fc2_bias: float32 [768], P('shard')
The draws below stay inside these ranges and needn't reach their ends.
All inputs are finite; a program needn't handle non-finite values.
Results may differ from the reference program's by a relative error of at most 0.017.
Values may be sent and summed in bfloat16 or wider, within the bound.
No kernel may reach another device: no remote copies, remote signals or barrier semaphores. Data moves between devices by JAX's collectives and lax.ppermute only.
A program may use at most 192 MiB of HBM per device.

```python
import math
import jax
import jax.numpy as jnp
from jax import lax

D = 768
HEADS = 12
HEAD = 64
FF = 3072
LEN = 384
SEQS = 64


def levels(rng, shape, shards, least, largest):
    def one(dim, parts):
        steps = jax.random.uniform(jax.random.fold_in(jax.random.fold_in(rng, 6), dim), (parts,), jnp.float32, least / len(shards), largest / len(shards))
        return jnp.repeat(jnp.exp(steps), shape[dim] // parts).reshape((-1,) + (1,) * (len(shape) - dim - 1))

    loudness = one(*shards[0])
    for cut in shards[1:]:
        loudness = loudness * one(*cut)
    return loudness


def scatter_about(key, shape, scale, reach, split=(), dtype=jnp.bfloat16):
    array = scale * jax.random.normal(key, shape, jnp.float32)
    if split:
        array = array * levels(key, shape, split, -0.22, 0.18)
    return jnp.clip(array, -reach, reach).astype(dtype)


def setup_inputs(seed: int = 0) -> dict:
    streams_of = jax.random.split(jax.random.key(seed), 16)
    tokens = scatter_about(streams_of[0], (SEQS, LEN, D), 1.0, 6.0, ((0, 32),))
    ln1_gain = jnp.clip(1.0 + 0.18 * jax.random.normal(streams_of[1], (D,), jnp.float32), 0.099609375, 1.8984375).astype(jnp.bfloat16)
    ln1_bias = scatter_about(streams_of[2], (D,), 0.3, 4.0, ((0, 4),))
    qkv_weight = scatter_about(streams_of[3], (D, 3 * D), D ** -0.5, 0.21875, ((0, 4),))
    query_bias = scatter_about(streams_of[4], (D,), 0.5, 6.0, ((0, 4),))
    value_bias = scatter_about(streams_of[5], (D,), 0.5, 6.0, ((0, 4),))
    out_weight = scatter_about(streams_of[6], (D, D), (D // 8) ** -0.5, 0.625, ((0, 4),))
    out_bias = scatter_about(streams_of[7], (D,), 0.5, 6.0, ((0, 4),))
    ln2_gain = jnp.clip(1.0 + 0.18 * jax.random.normal(streams_of[8], (D,), jnp.float32), 0.099609375, 1.8984375).astype(jnp.bfloat16)
    ln2_bias = scatter_about(streams_of[9], (D,), 0.3, 4.0, ((0, 4),))
    fc1_weight = scatter_about(streams_of[10], (D, FF), D ** -0.5, 0.21875, ((0, 4),))
    fc1_bias = scatter_about(streams_of[11], (FF,), 0.5, 6.0, ((0, 4),))
    fc2_weight = scatter_about(streams_of[12], (FF, D), (FF // 4) ** -0.5, 0.21875, ((0, 4),))
    fc2_bias = scatter_about(streams_of[13], (D,), 0.5, 6.0, ((0, 4),))
    cotangent = scatter_about(streams_of[14], (SEQS, LEN, D), 1.0, 6.0, ((0, 32),))
    return dict(tokens=tokens, ln1_gain=ln1_gain, ln1_bias=ln1_bias, qkv_weight=qkv_weight, query_bias=query_bias, value_bias=value_bias, out_weight=out_weight, out_bias=out_bias, ln2_gain=ln2_gain, ln2_bias=ln2_bias, fc1_weight=fc1_weight, fc1_bias=fc1_bias, fc2_weight=fc2_weight, fc2_bias=fc2_bias, cotangent=cotangent)


@jax.custom_vjp
def low(v):
    return lax.optimization_barrier(v.astype(jnp.bfloat16)).astype(jnp.float32)

@jax.custom_vjp
def low_back(v):
    return v

def low_keep(v):
    return (low(v), None)

def low_pass(kept, grad):
    return (grad,)

def back_keep(v):
    return (v, None)

def back_low(kept, grad):
    return (low(grad),)
low.defvjp(low_keep, low_pass)
low_back.defvjp(back_keep, back_low)
EPSILON = 1e-05
HIGHEST = lax.Precision.HIGHEST

def normalize(values, scaling, offset):
    average = lax.optimization_barrier(jnp.mean(values, axis=-1, keepdims=True))
    centred = values - average
    spread = lax.optimization_barrier(jnp.mean(centred * centred, axis=-1, keepdims=True))
    return centred * lax.rsqrt(spread + EPSILON) * scaling + offset

def matmul(left, right):
    return jnp.dot(left, right, precision=HIGHEST, preferred_element_type=jnp.float32)

def decoder_layer(params, inputs):
    ln1_gain, ln1_bias, qkv_weight, query_bias, value_bias, out_weight, out_bias, ln2_gain, ln2_bias, fc1_weight, fc1_bias, fc2_weight, fc2_bias = params
    count = inputs.shape[0]
    rows_flat = inputs.reshape(count * LEN, D)
    first = low(normalize(rows_flat, ln1_gain, ln1_bias))
    packed = matmul(first, qkv_weight)
    query = low_back(low(packed[:, :D] + query_bias))
    keys = low_back(low(packed[:, D:2 * D]))
    values = low_back(low(packed[:, 2 * D:] + value_bias))
    shape4 = (count, LEN, HEADS, HEAD)
    scores_raw = jnp.einsum('sqhd,skhd->shqk', query.reshape(shape4), keys.reshape(shape4), precision=HIGHEST)
    scores = low_back(scores_raw * (1.0 / math.sqrt(HEAD)))
    causal = jnp.arange(LEN)[:, None] >= jnp.arange(LEN)[None, :]
    masked = jnp.where(causal, scores, -1e+30)
    probs = low(jax.nn.softmax(masked, axis=-1))
    mixed = jnp.einsum('shqk,skhd->sqhd', probs, values.reshape(shape4), precision=HIGHEST)
    heads_out = low_back(low(mixed.reshape(count * LEN, D)))
    hidden = rows_flat + low_back(matmul(heads_out, out_weight) + out_bias)
    second = low(normalize(hidden, ln2_gain, ln2_bias))
    pre_act = low_back(matmul(second, fc1_weight) + fc1_bias)
    activated = low(jax.nn.gelu(pre_act, approximate=True))
    result = hidden + low_back(matmul(activated, fc2_weight) + fc2_bias)
    return result.reshape(inputs.shape)

def reference(tokens, ln1_gain, ln1_bias, qkv_weight, query_bias, value_bias, out_weight, out_bias, ln2_gain, ln2_bias, fc1_weight, fc1_bias, fc2_weight, fc2_bias, cotangent):
    params = tuple((piece.astype(jnp.float32) for piece in (ln1_gain, ln1_bias, qkv_weight, query_bias, value_bias, out_weight, out_bias, ln2_gain, ln2_bias, fc1_weight, fc1_bias, fc2_weight, fc2_bias)))
    groups = SEQS // 8
    inputs = tokens.astype(jnp.float32).reshape(groups, 8, LEN, D)
    upstream = cotangent.astype(jnp.float32).reshape(groups, 8, LEN, D)
    zeros = tuple((jnp.zeros_like(piece) for piece in params))

    def advance(summed, couple):
        inside, incoming = couple
        result, puller = jax.vjp(decoder_layer, params, inside)
        grad_params, grad_inputs = puller(incoming)
        summed = tuple((first + second for first, second in zip(summed, grad_params)))
        return (summed, (result.astype(jnp.bfloat16), grad_inputs.astype(jnp.bfloat16)))
    summed, (results, grad_inputs) = lax.scan(advance, zeros, (inputs, upstream))
    return (results.reshape(SEQS, LEN, D), grad_inputs.reshape(SEQS, LEN, D), summed[0], summed[1], summed[2], summed[3], summed[4], summed[5], summed[6], summed[7], summed[8], summed[9], summed[10], summed[11], summed[12])
```

```python
from functools import partial
import math

import jax
import jax.numpy as jnp
from jax import lax
from jax.experimental import pallas as pl
from jax.experimental.pallas import tpu as pltpu
from jax.sharding import PartitionSpec as P

HEAD = 64
EPSILON = 1e-05
F32 = jnp.float32
BF16 = jnp.bfloat16
LIMIT = 56 * 1024 * 1024
TANH_SCALE = math.sqrt(2.0 / math.pi)


def dot_nn(left, right):
    return jnp.dot(left, right, preferred_element_type=F32)


def dot_nt(left, right):
    return lax.dot_general(left, right, (((1,), (1,)), ((), ())), preferred_element_type=F32)


def dot_tn(left, right):
    return lax.dot_general(left, right, (((0,), (0,)), ((), ())), preferred_element_type=F32)


def whole(shape):
    return pl.BlockSpec(shape, lambda *_: (0,) * len(shape))


HBM = pl.BlockSpec(memory_space=pl.ANY)
ROW_XOR = (0, 2, 1, 3)


def weight_copies(info, pieces, target, sems):
    me, half = info[0], info[1]
    block = pieces[0].shape[0]
    part = block // 2
    rows = (
        me * block,
        (me ^ 1) * block,
        (me ^ 2) * block + half * part,
        (me ^ 2) * block + (1 - half) * part,
        (me ^ 3) * block + half * part,
        (me ^ 3) * block + (1 - half) * part,
    )
    copies = []
    for index, (piece, row) in enumerate(zip(pieces, rows)):
        size = piece.shape[0]
        row = pl.multiple_of(row, 16)
        copies.append(
            pltpu.make_async_copy(piece, target.at[pl.ds(row, size), :], sems.at[index])
        )
    return copies


def norm_parts(values):
    average = jnp.mean(values, axis=-1, keepdims=True)
    centred = values - average
    inverse = lax.rsqrt(jnp.mean(centred * centred, axis=-1, keepdims=True) + EPSILON)
    return centred * inverse, inverse


def triangle(block):
    return lax.broadcasted_iota(jnp.int32, (block, block), 0) <= lax.broadcasted_iota(
        jnp.int32, (block, block), 1
    )


def attend_kernel(length, info, tok, vec, *refs):
    pieces, (first, packed, mixed, logsum), (weight, sems) = refs[:6], refs[6:10], refs[10:]
    rows, width = tok.shape
    copies = weight_copies(info, pieces, weight, sems)
    for copy in copies:
        copy.start()

    def norm_step(i, _):
        at = pl.ds(pl.multiple_of(i * 128, 128), 128)
        white, _inverse = norm_parts(tok[at, :].astype(F32))
        first[at, :] = (white * vec[0:1, :] + vec[1:2, :]).astype(BF16)
        return 0

    lax.fori_loop(0, rows // 128, norm_step, 0)
    for copy in copies:
        copy.wait()

    for part in range(3):
        def project(i, _, part=part):
            at = pl.ds(pl.multiple_of(i * 256, 256), 256)
            to = pl.ds(pl.multiple_of(part * width + i * 256, 256), 256)
            value = dot_nn(first[...], weight[:, to])
            if part == 0:
                value = (value + vec[2:3, at]).astype(BF16) * jnp.asarray(HEAD**-0.5, BF16)
            elif part == 2:
                value = (value + vec[3:4, at]).astype(BF16)
            else:
                value = value.astype(BF16)
            packed[:, to] = value
            return 0

        lax.fori_loop(0, width // 256, project, 0)

    pairs = width // 128
    blocks = length // 128
    keep = triangle(128)

    def pair_step(it, _):
        base = (it // pairs) * length
        column = (it % pairs) * 128
        at = pl.ds(pl.multiple_of(base, 128), length)
        query = packed[at, pl.ds(pl.multiple_of(column, 128), 128)]
        key = packed[at, pl.ds(pl.multiple_of(width + column, 128), 128)]
        value = packed[at, pl.ds(pl.multiple_of(2 * width + column, 128), 128)]
        lane = lax.broadcasted_iota(jnp.int32, query.shape, 1)
        halves = []
        for head in range(2):
            masked = jnp.where((lane < HEAD) == (head == 0), query, jnp.zeros_like(query))
            scores = [
                dot_nt(key[kb * 128 : (kb + 1) * 128], masked[kb * 128 :]) for kb in range(blocks)
            ]
            outs = []
            for qb in range(blocks):
                tiles = [
                    scores[kb][:, (qb - kb) * 128 : (qb - kb + 1) * 128] for kb in range(qb + 1)
                ]
                tiles[qb] = jnp.where(keep, tiles[qb], -1e30)
                highest = tiles[0]
                for tile in tiles[1:]:
                    highest = jnp.maximum(highest, tile)
                highest = jnp.max(highest, axis=0, keepdims=True)
                expo = [jnp.exp(tile - highest) for tile in tiles]
                total = expo[0]
                for tile in expo[1:]:
                    total = total + tile
                total = jnp.sum(total, axis=0, keepdims=True)
                scale = 1.0 / total
                probs = jnp.concatenate([(tile * scale).astype(BF16) for tile in expo], axis=0)
                outs.append(dot_tn(value[: (qb + 1) * 128], probs))
                logsum[it * 2 + head, 0:1, qb * 128 : (qb + 1) * 128] = highest + jnp.log(total)
            halves.append(outs)
        for qb in range(blocks):
            both = jnp.concatenate([halves[0][qb][:HEAD], halves[1][qb][HEAD:]], axis=0)
            mixed[
                pl.ds(pl.multiple_of(base + qb * 128, 128), 128),
                pl.ds(pl.multiple_of(column, 128), 128),
            ] = both.T.astype(BF16)
        return 0

    lax.fori_loop(0, (rows // length) * pairs, pair_step, 0)


def attend(info, tok, vec, pieces, length):
    rows, width = tok.shape
    groups = (rows // length) * (width // HEAD)
    return pl.pallas_call(
        partial(attend_kernel, length),
        in_specs=[pl.BlockSpec(memory_space=pltpu.SMEM)]
        + [pl.BlockSpec(memory_space=pltpu.VMEM)] * 2
        + [HBM] * 6,
        out_specs=[pl.BlockSpec(memory_space=pltpu.VMEM)] * 4,
        out_shape=[
            jax.ShapeDtypeStruct((rows, width), BF16),
            jax.ShapeDtypeStruct((rows, 3 * width), BF16),
            jax.ShapeDtypeStruct((rows, width), BF16),
            jax.ShapeDtypeStruct((groups, 1, length), F32),
        ],
        scratch_shapes=[pltpu.VMEM((width, 3 * width), BF16), pltpu.SemaphoreType.DMA((6,))],
        compiler_params=pltpu.CompilerParams(vmem_limit_bytes=LIMIT),
        cost_estimate=pl.CostEstimate(
            flops=2 * rows * width * 3 * width * 3, bytes_accessed=12000000, transcendentals=0
        ),
        name="attend",
    )(info, tok, vec, *pieces)


def feed_kernel(info, mixed, tok, vec, bias, *refs):
    out_pieces, fc1_pieces = refs[:6], refs[6:12]
    hidden, second, act, slope = refs[12:16]
    out_w, fc1_w, sems = refs[16:]
    step = pl.program_id(0)
    rows, width = tok.shape
    chunk = act.shape[1]

    @pl.when(step == 0)
    def _():
        out_copies = weight_copies(info, out_pieces, out_w, sems.at[0])
        fc1_copies = weight_copies(info, fc1_pieces, fc1_w, sems.at[1])
        for copy in out_copies + fc1_copies:
            copy.start()
        for copy in out_copies:
            copy.wait()

        def norm_step(i, _):
            at = pl.ds(pl.multiple_of(i * 256, 256), 256)
            value = tok[at, :].astype(F32) + dot_nn(mixed[at, :], out_w[...]) + vec[4:5, :]
            hidden[at, :] = value
            white, _inverse = norm_parts(value)
            second[at, :] = (white * vec[5:6, :] + vec[6:7, :]).astype(BF16)
            return 0

        lax.fori_loop(0, rows // 256, norm_step, 0)
        for copy in fc1_copies:
            copy.wait()

    columns = pl.ds(pl.multiple_of(step * chunk, chunk), chunk)

    def gelu_step(i, _):
        at = pl.ds(pl.multiple_of(i * 256, 256), 256)
        u = dot_nn(second[at, :], fc1_w[:, columns]) + bias[...]
        square = u * u
        t = jnp.tanh(u * (TANH_SCALE + (TANH_SCALE * 0.044715) * square))
        left = 0.5 + 0.5 * t
        act[at, :] = (u * left).astype(BF16)
        inner = TANH_SCALE + (3 * TANH_SCALE * 0.044715) * square
        slope[at, :] = (left + u * (0.5 - 0.5 * t * t) * inner).astype(BF16)
        return 0

    lax.fori_loop(0, rows // 256, gelu_step, 0)


def feed(info, mixed, tok, vec, bias, out_pieces, fc1_pieces):
    rows, width = tok.shape
    ff = bias.shape[1]
    chunk = 512
    return pl.pallas_call(
        feed_kernel,
        grid=(ff // chunk,),
        in_specs=[
            pl.BlockSpec(memory_space=pltpu.SMEM),
            whole((rows, width)),
            whole((rows, width)),
            whole(vec.shape),
            pl.BlockSpec((1, chunk), lambda j: (0, j)),
        ]
        + [HBM] * 12,
        out_specs=[
            whole((rows, width)),
            whole((rows, width)),
            pl.BlockSpec((rows, chunk), lambda j: (0, j)),
            pl.BlockSpec((rows, chunk), lambda j: (0, j)),
        ],
        out_shape=[
            jax.ShapeDtypeStruct((rows, width), F32),
            jax.ShapeDtypeStruct((rows, width), BF16),
            jax.ShapeDtypeStruct((rows, ff), BF16),
            jax.ShapeDtypeStruct((rows, ff), BF16),
        ],
        scratch_shapes=[
            pltpu.VMEM((width, width), BF16),
            pltpu.VMEM((width, ff), BF16),
            pltpu.SemaphoreType.DMA((2, 6)),
        ],
        compiler_params=pltpu.CompilerParams(
            vmem_limit_bytes=LIMIT, dimension_semantics=("arbitrary",)
        ),
        cost_estimate=pl.CostEstimate(
            flops=2 * rows * width * (width + ff) * 2, bytes_accessed=20000000, transcendentals=0
        ),
        name="feed",
    )(info, mixed, tok, vec, bias, *out_pieces, *fc1_pieces)


def down_grad_kernel(info, act, dy, send, keep, sums):
    step = pl.program_id(0)

    @pl.when(step == 0)
    def _():
        sums[...] = jnp.sum(dy[...].astype(F32), axis=0, keepdims=True)

    grad = dot_tn(act[...], dy[...]).astype(BF16)

    @pl.when(step < 6)
    def _():
        send[0] = grad

    @pl.when(step >= 6)
    def _():
        keep[0] = grad


def down_grad(info, act, dy):
    rows, width = dy.shape
    ff = act.shape[1]
    block = ff // 4
    chunk = block // 3

    def act_at(i, info):
        turn = i // 3
        owner = info[0] ^ ((turn & 1) * 2 + (1 - turn // 2))
        return (0, owner * 3 + i % 3)

    def send_at(i, info):
        i = jnp.minimum(i, 5)
        return (i // 3, i % 3, 0)

    def keep_at(i, info):
        i = jnp.maximum(i - 6, 0)
        return (i // 3, i % 3, 0)

    return pl.pallas_call(
        down_grad_kernel,
        grid_spec=pltpu.PrefetchScalarGridSpec(
            num_scalar_prefetch=1,
            grid=(12,),
            in_specs=[pl.BlockSpec((rows, chunk), act_at), whole((rows, width))],
            out_specs=[
                pl.BlockSpec((1, chunk, width), send_at),
                pl.BlockSpec((1, chunk, width), keep_at),
                whole((1, width)),
            ],
        ),
        out_shape=[
            jax.ShapeDtypeStruct((2, block, width), BF16),
            jax.ShapeDtypeStruct((2, block, width), BF16),
            jax.ShapeDtypeStruct((1, width), F32),
        ],
        compiler_params=pltpu.CompilerParams(
            vmem_limit_bytes=LIMIT, dimension_semantics=("arbitrary",)
        ),
        cost_estimate=pl.CostEstimate(
            flops=2 * rows * width * ff * 2, bytes_accessed=10000000, transcendentals=0
        ),
        name="down_grad",
    )(info, act, dy)


def transpose_by_owner(info, source, target):
    block = source.shape[1] // 4
    for owner in range(4):
        turned = source[:, owner * block : (owner + 1) * block].T
        near = owner ^ info[0]
        slot = (near & 1) * 2 + near // 2
        target[pl.ds(pl.multiple_of(slot * block, 16), block), :] = turned


def norm_grad_rows(values, incoming, gain):
    white, inverse = norm_parts(values)
    scaled = incoming * gain
    inner = (
        scaled
        - jnp.mean(scaled, axis=-1, keepdims=True)
        - white * jnp.mean(scaled * white, axis=-1, keepdims=True)
    )
    return (
        inner * inverse,
        jnp.sum(incoming * white, axis=0, keepdims=True),
        jnp.sum(incoming, axis=0, keepdims=True),
    )


def up_grad_kernel(info, slope, dy, second, hidden, vec, *refs):
    fc1_pieces, fc2_pieces = refs[:6], refs[6:12]
    keep, send, grad_hidden, branch, sums, bias_sums = refs[12:18]
    fc1_w, fc2_w, turned, grad_second, sems = refs[18:]
    step = pl.program_id(0)
    rows, width = dy.shape
    chunk = slope.shape[1]

    @pl.when(step == 0)
    def _():
        fc2_copies = weight_copies(info, fc2_pieces, fc2_w, sems.at[0])
        fc1_copies = weight_copies(info, fc1_pieces, fc1_w, sems.at[1])
        for copy in fc2_copies + fc1_copies:
            copy.start()
        transpose_by_owner(info, second, turned)
        for copy in fc2_copies + fc1_copies:
            copy.wait()

    columns = pl.ds(pl.multiple_of(step * chunk, chunk), chunk)
    grad_act = dot_nt(dy[...], fc2_w[columns, :])
    grad_pre = (grad_act * slope[...].astype(F32)).astype(BF16)
    bias_sums[...] = jnp.sum(grad_pre.astype(F32), axis=0, keepdims=True)
    grad = dot_nn(turned[...], grad_pre).astype(BF16).reshape(4, width // 4, chunk)
    keep[...] = grad[:2]
    send[...] = grad[2:]
    part = dot_nt(grad_pre, fc1_w[:, columns])

    @pl.when(step == 0)
    def _():
        grad_second[...] = part

    @pl.when(step > 0)
    def _():
        grad_second[...] += part

    @pl.when(step == pl.num_programs(0) - 1)
    def _():
        def norm_step(i, carry):
            at = pl.ds(pl.multiple_of(i * 128, 128), 128)
            through, gains, biases = norm_grad_rows(hidden[at, :], grad_second[at, :], vec[5:6, :])
            value = dy[at, :].astype(F32) + through
            grad_hidden[at, :] = value
            rounded = value.astype(BF16)
            branch[at, :] = rounded
            return (
                carry[0] + gains,
                carry[1] + biases,
                carry[2] + jnp.sum(rounded.astype(F32), axis=0, keepdims=True),
            )

        zero = jnp.zeros((1, width), F32)
        gains, biases, outs = lax.fori_loop(0, rows // 128, norm_step, (zero, zero, zero))
        sums[0:1, :] = gains
        sums[1:2, :] = biases
        sums[2:3, :] = outs


def up_grad(info, slope, dy, second, hidden, vec, fc1_pieces, fc2_pieces):
    rows, width = dy.shape
    ff = slope.shape[1]
    chunk = 512
    return pl.pallas_call(
        up_grad_kernel,
        grid=(ff // chunk,),
        in_specs=[
            pl.BlockSpec(memory_space=pltpu.SMEM),
            pl.BlockSpec((rows, chunk), lambda j: (0, j)),
            whole((rows, width)),
            whole((rows, width)),
            whole((rows, width)),
            whole(vec.shape),
        ]
        + [HBM] * 12,
        out_specs=[
            pl.BlockSpec((2, width // 4, chunk), lambda j: (0, 0, j)),
            pl.BlockSpec((2, width // 4, chunk), lambda j: (0, 0, j)),
            whole((rows, width)),
            whole((rows, width)),
            whole((3, width)),
            pl.BlockSpec((1, chunk), lambda j: (0, j)),
        ],
        out_shape=[
            jax.ShapeDtypeStruct((2, width // 4, ff), BF16),
            jax.ShapeDtypeStruct((2, width // 4, ff), BF16),
            jax.ShapeDtypeStruct((rows, width), F32),
            jax.ShapeDtypeStruct((rows, width), BF16),
            jax.ShapeDtypeStruct((3, width), F32),
            jax.ShapeDtypeStruct((1, ff), F32),
        ],
        scratch_shapes=[
            pltpu.VMEM((width, ff), BF16),
            pltpu.VMEM((ff, width), BF16),
            pltpu.VMEM((width, rows), BF16),
            pltpu.VMEM((rows, width), F32),
            pltpu.SemaphoreType.DMA((2, 6)),
        ],
        compiler_params=pltpu.CompilerParams(
            vmem_limit_bytes=LIMIT, dimension_semantics=("arbitrary",)
        ),
        cost_estimate=pl.CostEstimate(
            flops=2 * rows * width * ff * 6, bytes_accessed=30000000, transcendentals=0
        ),
        name="up_grad",
    )(info, slope, dy, second, hidden, vec, *fc1_pieces, *fc2_pieces)


def attend_grad_kernel(length, info, branch, mixed, first, packed, logsum, *refs):
    pieces = refs[:6]
    keep, send, grad_packed, sums = refs[6:10]
    weight, grad_mixed, turned, sems = refs[10:]
    rows, width = branch.shape
    copies = weight_copies(info, pieces, weight, sems)
    for copy in copies:
        copy.start()
    for copy in copies:
        copy.wait()

    def mixed_step(i, _):
        at = pl.ds(pl.multiple_of(i * 256, 256), 256)
        grad_mixed[at, :] = dot_nt(branch[at, :], weight[...]).astype(BF16)
        return 0

    lax.fori_loop(0, rows // 256, mixed_step, 0)

    pairs = width // 128
    blocks = length // 128
    causal = triangle(128)

    def pair_step(it, _):
        base = (it // pairs) * length
        column = (it % pairs) * 128
        at = pl.ds(pl.multiple_of(base, 128), length)
        at_query = pl.ds(pl.multiple_of(column, 128), 128)
        at_key = pl.ds(pl.multiple_of(width + column, 128), 128)
        at_value = pl.ds(pl.multiple_of(2 * width + column, 128), 128)
        query, key, value = packed[at, at_query], packed[at, at_key], packed[at, at_value]
        incoming = grad_mixed[at, at_query]
        lane = lax.broadcasted_iota(jnp.int32, query.shape, 1)
        results = []
        for head in range(2):
            here = (lane < HEAD) == (head == 0)
            query_h = jnp.where(here, query, jnp.zeros_like(query))
            incoming_h = jnp.where(here, incoming, jnp.zeros_like(incoming))
            probs, grads = [], []
            for kb in range(blocks):
                rows_k = slice(kb * 128, (kb + 1) * 128)
                scores = dot_nt(key[rows_k], query_h[kb * 128 :])
                stats = logsum[it * 2 + head, 0:1, kb * 128 :]
                expo = jnp.exp(scores - stats)
                diagonal = jnp.where(causal, expo[:, :128], 0.0)
                if kb < blocks - 1:
                    expo = jnp.concatenate([diagonal, expo[:, 128:]], axis=1)
                else:
                    expo = diagonal
                probs.append(expo)
                grads.append(dot_nt(value[rows_k], incoming_h[kb * 128 :]))
            inner = []
            for qb in range(blocks):
                total = None
                for kb in range(qb + 1):
                    cut = slice((qb - kb) * 128, (qb - kb + 1) * 128)
                    term = probs[kb][:, cut] * grads[kb][:, cut]
                    total = term if total is None else total + term
                inner.append(jnp.sum(total, axis=0, keepdims=True))
            inner = jnp.concatenate(inner, axis=1)
            score_grads = [
                (probs[kb] * (grads[kb] - inner[:, kb * 128 :])).astype(BF16)
                for kb in range(blocks)
            ]
            grad_values = [
                dot_nn(probs[kb].astype(BF16), incoming[kb * 128 :]) for kb in range(blocks)
            ]
            grad_keys = [dot_nn(score_grads[kb], query[kb * 128 :]) for kb in range(blocks)]
            grad_query = []
            for qb in range(blocks):
                tiles = [
                    score_grads[kb][:, (qb - kb) * 128 : (qb - kb + 1) * 128]
                    for kb in range(qb + 1)
                ]
                grad_query.append(dot_tn(key[: (qb + 1) * 128], jnp.concatenate(tiles, axis=0)))
            results.append((grad_values, grad_keys, grad_query))
        left = lax.broadcasted_iota(jnp.int32, (128, 128), 1) < HEAD
        for b in range(blocks):
            to = pl.ds(pl.multiple_of(base + b * 128, 128), 128)
            grad_packed[to, at_value] = jnp.where(left, results[0][0][b], results[1][0][b]).astype(
                BF16
            )
            grad_packed[to, at_key] = jnp.where(left, results[0][1][b], results[1][1][b]).astype(
                BF16
            )
            both = jnp.concatenate([results[0][2][b][:HEAD], results[1][2][b][HEAD:]], axis=0)
            grad_packed[to, at_query] = (both.T * HEAD**-0.5).astype(BF16)
        return 0

    lax.fori_loop(0, (rows // length) * pairs, pair_step, 0)

    def weight_grad(source, source_at, target_at):
        grad = dot_nn(turned[...], source[:, source_at]).astype(BF16).reshape(4, width // 4, 256)
        keep[:, :, target_at] = grad[:2]
        send[:, :, target_at] = grad[2:]

    transpose_by_owner(info, mixed, turned)

    def out_step(i, _):
        weight_grad(
            branch,
            pl.ds(pl.multiple_of(i * 256, 256), 256),
            pl.ds(pl.multiple_of(3 * width + i * 256, 256), 256),
        )
        return 0

    lax.fori_loop(0, width // 256, out_step, 0)
    transpose_by_owner(info, first, turned)

    def packed_step(i, _):
        at = pl.ds(pl.multiple_of(i * 256, 256), 256)
        weight_grad(grad_packed, at, at)
        sums[:, at] = jnp.sum(grad_packed[:, at].astype(F32), axis=0, keepdims=True)
        return 0

    lax.fori_loop(0, 3 * width // 256, packed_step, 0)


def attend_grad(info, branch, mixed, first, packed, logsum, pieces, length):
    rows, width = branch.shape
    return pl.pallas_call(
        partial(attend_grad_kernel, length),
        in_specs=[pl.BlockSpec(memory_space=pltpu.SMEM)]
        + [pl.BlockSpec(memory_space=pltpu.VMEM)] * 5
        + [HBM] * 6,
        out_specs=[pl.BlockSpec(memory_space=pltpu.VMEM)] * 4,
        out_shape=[
            jax.ShapeDtypeStruct((2, width // 4, 4 * width), BF16),
            jax.ShapeDtypeStruct((2, width // 4, 4 * width), BF16),
            jax.ShapeDtypeStruct((rows, 3 * width), BF16),
            jax.ShapeDtypeStruct((1, 3 * width), F32),
        ],
        scratch_shapes=[
            pltpu.VMEM((width, width), BF16),
            pltpu.VMEM((rows, width), BF16),
            pltpu.VMEM((width, rows), BF16),
            pltpu.SemaphoreType.DMA((6,)),
        ],
        compiler_params=pltpu.CompilerParams(vmem_limit_bytes=LIMIT),
        cost_estimate=pl.CostEstimate(
            flops=2 * rows * width * 4 * width * 6, bytes_accessed=20000000, transcendentals=0
        ),
        name="attend_grad",
    )(info, branch, mixed, first, packed, logsum, *pieces)


def input_grad_kernel(info, grad_packed, tok, grad_hidden, vec, *refs):
    pieces, (in_grad, sums), (weight, sems) = refs[:6], refs[6:8], refs[8:]
    rows, width = tok.shape
    step = pl.program_id(0)

    @pl.when(step == 0)
    def _():
        copies = weight_copies(info, pieces, weight, sems)
        for copy in copies:
            copy.start()
        sums[...] = jnp.zeros_like(sums)
        for copy in copies:
            copy.wait()

    grad_first = dot_nt(grad_packed[...], weight[...])
    through, gains, biases = norm_grad_rows(tok[...].astype(F32), grad_first, vec[0:1, :])
    in_grad[...] = (grad_hidden[...] + through).astype(BF16)
    sums[0:1, :] += gains
    sums[1:2, :] += biases


def input_grad(info, grad_packed, tok, grad_hidden, vec, pieces):
    rows, width = tok.shape
    block = 256
    return pl.pallas_call(
        input_grad_kernel,
        grid=(rows // block,),
        in_specs=[
            pl.BlockSpec(memory_space=pltpu.SMEM),
            pl.BlockSpec((block, 3 * width), lambda i: (i, 0)),
            pl.BlockSpec((block, width), lambda i: (i, 0)),
            pl.BlockSpec((block, width), lambda i: (i, 0)),
            whole(vec.shape),
        ]
        + [HBM] * 6,
        out_specs=[pl.BlockSpec((block, width), lambda i: (i, 0)), whole((2, width))],
        out_shape=[
            jax.ShapeDtypeStruct((rows, width), BF16),
            jax.ShapeDtypeStruct((2, width), F32),
        ],
        scratch_shapes=[pltpu.VMEM((width, 3 * width), BF16), pltpu.SemaphoreType.DMA((6,))],
        compiler_params=pltpu.CompilerParams(
            vmem_limit_bytes=LIMIT, dimension_semantics=("arbitrary",)
        ),
        cost_estimate=pl.CostEstimate(
            flops=2 * rows * width * 3 * width * 2, bytes_accessed=14000000, transcendentals=0
        ),
        name="input_grad",
    )(info, grad_packed, tok, grad_hidden, vec, *pieces)


def output_kernel(info, act, hidden, vec, *refs):
    pieces, (out,), (weight, sems) = refs[:6], refs[6:7], refs[7:]

    @pl.when(pl.program_id(0) == 0)
    def _():
        copies = weight_copies(info, pieces, weight, sems)
        for copy in copies:
            copy.start()
        for copy in copies:
            copy.wait()

    out[...] = (hidden[...] + dot_nn(act[...], weight[...]) + vec[7:8, :]).astype(BF16)


def output_rows(info, act, hidden, vec, pieces):
    rows, width = hidden.shape
    ff = act.shape[1]
    block = 256
    return pl.pallas_call(
        output_kernel,
        grid=(rows // block,),
        in_specs=[
            pl.BlockSpec(memory_space=pltpu.SMEM),
            pl.BlockSpec((block, ff), lambda i: (i, 0)),
            pl.BlockSpec((block, width), lambda i: (i, 0)),
            whole(vec.shape),
        ]
        + [HBM] * 6,
        out_specs=pl.BlockSpec((block, width), lambda i: (i, 0)),
        out_shape=jax.ShapeDtypeStruct((rows, width), BF16),
        scratch_shapes=[pltpu.VMEM((ff, width), BF16), pltpu.SemaphoreType.DMA((6,))],
        compiler_params=pltpu.CompilerParams(
            vmem_limit_bytes=LIMIT, dimension_semantics=("arbitrary",)
        ),
        cost_estimate=pl.CostEstimate(
            flops=2 * rows * width * ff * 2, bytes_accessed=14000000, transcendentals=0
        ),
        name="output_rows",
    )(info, act, hidden, vec, *pieces)


def swap(value, axis, size, bit):
    return lax.ppermute(value, axis, [(i, i ^ bit) for i in range(size)])


def gather_weight(block, reps, half):
    part = block.shape[0] // 2
    mine = lax.dynamic_slice_in_dim(block, half * part, part, 0)
    far_a = swap(mine, "shard", 4, 2)
    far_b = swap(far_a, "rep", reps, 1)
    return (
        block,
        swap(block, "shard", 4, 1),
        far_a,
        far_b,
        swap(far_a, "shard", 4, 1),
        swap(far_b, "shard", 4, 1),
    )


def halves(terms, bit, axis=0):
    size = terms[0].shape[axis] // 2

    def cut(start):
        total = None
        for term in terms:
            piece = lax.dynamic_slice_in_dim(term, start, size, axis).astype(F32)
            total = piece if total is None else total + piece
        return total.astype(BF16)

    return cut(bit * size), cut((1 - bit) * size)


def reduce_chunk(keep, send, me, rep, reps):
    got = swap(send, "shard", 4, 1)
    far = (keep[1].astype(F32) + got[1].astype(F32)).astype(BF16)
    far = swap(far, "shard", 4, 2)
    terms = [keep[0], got[0], far]
    bits = reps.bit_length() - 1
    for level in range(bits):
        mine, other = halves(terms, (rep >> level) & 1)
        terms = [mine, swap(other, "rep", reps, 1 << level)]
    total = sum(term.astype(F32) for term in terms).astype(BF16)
    for level in reversed(range(bits)):
        other = swap(total, "rep", reps, 1 << level)
        bit = (rep >> level) & 1
        total = jnp.where(
            bit == 0,
            jnp.concatenate([total, other], axis=0),
            jnp.concatenate([other, total], axis=0),
        )
    return total.astype(F32)


def sum_small(value, reps):
    value = value + swap(value, "shard", 4, 1)
    value = value + swap(value, "shard", 4, 2)
    bit = 1
    while bit < reps:
        value = value + swap(value, "rep", reps, bit)
        bit *= 2
    return value


def on_device(
    reps,
    tokens,
    ln1_gain,
    ln1_bias,
    qkv_weight,
    query_bias,
    value_bias,
    out_weight,
    out_bias,
    ln2_gain,
    ln2_bias,
    fc1_weight,
    fc1_bias,
    fc2_weight,
    fc2_bias,
    cotangent,
):
    seqs_here, length, width = tokens.shape
    rows = seqs_here * length
    me = lax.axis_index("shard").astype(jnp.int32)
    rep = lax.axis_index("rep").astype(jnp.int32)
    half = rep & 1
    info = jnp.stack([me, half])

    small = jnp.concatenate(
        [
            ln1_gain,
            ln1_bias,
            query_bias,
            value_bias,
            out_bias,
            ln2_gain,
            ln2_bias,
            fc2_bias,
            fc1_bias,
        ]
    ).reshape(1, -1)
    pair = jnp.concatenate([small, swap(small, "shard", 4, 1)], axis=0)
    near = jnp.concatenate([pair, swap(pair, "shard", 4, 2)], axis=0)
    near = jnp.where((me & 1) == 0, near, near[jnp.array([1, 0, 3, 2])])
    near = jnp.where((me & 2) == 0, near, near[jnp.array([2, 3, 0, 1])]).astype(F32)
    share = width // 4
    vec = near[:, : 8 * share].reshape(4, 8, share).transpose(1, 0, 2).reshape(8, width)
    bias = near[:, 8 * share :].reshape(1, -1)

    qkv = gather_weight(qkv_weight, reps, half)
    out = gather_weight(out_weight, reps, half)
    fc1 = gather_weight(fc1_weight, reps, half)
    fc2 = gather_weight(fc2_weight, reps, half)

    tok = tokens.reshape(rows, width)
    dy = cotangent.reshape(rows, width)
    first, packed, mixed, logsum = attend(info, tok, vec, qkv, length)
    hidden, second, act, slope = feed(info, mixed, tok, vec, bias, out, fc1)
    send2, keep2, sums_dy = down_grad(info, act, dy)
    keep1, send1, grad_hidden, branch, sums_ln2, sums_fc1 = up_grad(
        info, slope, dy, second, hidden, vec, fc1, fc2
    )
    keep0, send0, grad_packed, sums_packed = attend_grad(
        info, branch, mixed, first, packed, logsum, out, length
    )
    in_grad, sums_ln1 = input_grad(info, grad_packed, tok, grad_hidden, vec, qkv)
    output = output_rows(info, act, hidden, vec, fc2)

    total2 = reduce_chunk(keep2, send2, me, rep, reps)
    total1 = reduce_chunk(keep1, send1, me, rep, reps)
    total0 = reduce_chunk(keep0, send0, me, rep, reps)

    sums = jnp.concatenate(
        [
            sums_ln1,
            sums_packed.reshape(3, width),
            sums_ln2,
            sums_dy,
            sums_fc1.reshape(4, width),
        ],
        axis=0,
    )
    sums = sum_small(sums, reps)
    mine = lax.dynamic_slice_in_dim(sums, me * share, share, 1)
    fc1b = lax.dynamic_slice_in_dim(sums, 9 + me, 1, 0).reshape(width)
    return (
        output.reshape(tokens.shape),
        in_grad.reshape(tokens.shape),
        mine[0],
        mine[1],
        total0[:, : 3 * width],
        mine[2],
        mine[4],
        total0[:, 3 * width :],
        mine[7],
        mine[5],
        mine[6],
        total1,
        fc1b,
        total2,
        mine[8],
    )


def solution(mesh):
    spread = P(("rep", "shard"), None, None)
    matrix = P("shard", None)
    vector = P("shard")
    return jax.shard_map(
        partial(on_device, mesh.shape["rep"]),
        mesh=mesh,
        in_specs=(
            spread, vector, vector, matrix, vector, vector, matrix, vector,
            vector, vector, matrix, vector, matrix, vector, spread,
        ),
        out_specs=(
            spread, spread, vector, vector, matrix, vector, vector, matrix,
            vector, vector, vector, matrix, vector, matrix, vector,
        ),
        check_vma=False,
    )
```

```python
from functools import partial
import math

import jax
import jax.numpy as jnp
from jax import lax
from jax.experimental import pallas as pl
from jax.experimental.pallas import tpu as pltpu
from jax.sharding import PartitionSpec as P

HEAD = 64
EPSILON = 1e-05
F32 = jnp.float32
BF16 = jnp.bfloat16
LIMIT = 56 * 1024 * 1024
TANH_SCALE = math.sqrt(2.0 / math.pi)


def dot_nn(left, right):
    return jnp.dot(left, right, preferred_element_type=F32)


def dot_nt(left, right):
    return lax.dot_general(left, right, (((1,), (1,)), ((), ())), preferred_element_type=F32)


def dot_tn(left, right):
    return lax.dot_general(left, right, (((0,), (0,)), ((), ())), preferred_element_type=F32)


def whole(shape):
    return pl.BlockSpec(shape, lambda *_: (0,) * len(shape))


HBM = pl.BlockSpec(memory_space=pl.ANY)
VMEM = pl.BlockSpec(memory_space=pltpu.VMEM)
SMEM = pl.BlockSpec(memory_space=pltpu.SMEM)


def run(body, name, inputs, outputs, scratch=(), deps=(), grid=(), cost=1):
    count, hidden_inputs = len(inputs), len(deps)
    given = len(outputs)

    def kernel(*refs):
        first = True
        for axis in range(len(grid)):
            first = first & (pl.program_id(axis) == 0)
        token = refs[count + hidden_inputs + given]

        @pl.when(first)
        def _():
            token[0] = 0

        ins = refs[:count]
        outs = refs[count + hidden_inputs : count + hidden_inputs + given]
        body(*ins, *outs, *refs[count + hidden_inputs + given + 1 :])

    return pl.pallas_call(
        kernel,
        grid=grid,
        in_specs=[spec for _, spec in inputs] + [HBM] * hidden_inputs,
        out_specs=[spec for _, _, spec in outputs] + [SMEM],
        out_shape=[jax.ShapeDtypeStruct(shape, dtype) for shape, dtype, _ in outputs]
        + [jax.ShapeDtypeStruct((1,), jnp.int32)],
        scratch_shapes=list(scratch),
        compiler_params=pltpu.CompilerParams(
            vmem_limit_bytes=LIMIT,
            dimension_semantics=("arbitrary",) * len(grid) if grid else None,
        ),
        cost_estimate=pl.CostEstimate(flops=cost, bytes_accessed=cost, transcendentals=0),
        name=name,
    )(*[value for value, _ in inputs], *deps)


def weight_copies(info, pieces, target, sems):
    me, half = info[0], info[1]
    block = pieces[0].shape[0]
    part = block // 2
    rows = (
        me * block,
        (me ^ 1) * block,
        (me ^ 2) * block + half * part,
        (me ^ 2) * block + (1 - half) * part,
        (me ^ 3) * block + half * part,
        (me ^ 3) * block + (1 - half) * part,
    )
    copies = []
    for index, (piece, row) in enumerate(zip(pieces, rows)):
        size = piece.shape[0]
        row = pl.multiple_of(row, 16)
        copies.append(
            pltpu.make_async_copy(piece, target.at[pl.ds(row, size), :], sems.at[index])
        )
    return copies


def norm_parts(values):
    average = jnp.mean(values, axis=-1, keepdims=True)
    centred = values - average
    inverse = lax.rsqrt(jnp.mean(centred * centred, axis=-1, keepdims=True) + EPSILON)
    return centred * inverse, inverse


def triangle(block):
    return lax.broadcasted_iota(jnp.int32, (block, block), 0) <= lax.broadcasted_iota(
        jnp.int32, (block, block), 1
    )


def transpose_by_owner(info, source, target):
    block = source.shape[1] // 4
    for owner in range(4):
        turned = source[:, owner * block : (owner + 1) * block].T
        near = owner ^ info[0]
        slot = (near & 1) * 2 + near // 2
        target[pl.ds(pl.multiple_of(slot * block, 16), block), :] = turned


def norm_grad_rows(values, incoming, gain):
    white, inverse = norm_parts(values)
    scaled = incoming * gain
    inner = (
        scaled
        - jnp.mean(scaled, axis=-1, keepdims=True)
        - white * jnp.mean(scaled * white, axis=-1, keepdims=True)
    )
    return (
        inner * inverse,
        jnp.sum(incoming * white, axis=0, keepdims=True),
        jnp.sum(incoming, axis=0, keepdims=True),
    )


def copy_by_owner(me, source, target):
    block = source.shape[0] // 4
    for slot in range(4):
        owner = me ^ ((slot & 1) * 2 + slot // 2)
        target[slot * block : (slot + 1) * block, :] = source[
            pl.ds(pl.multiple_of(owner * block, 16), block), :
        ]


def project_kernel(info, tok, vec, *refs):
    pieces, (packed, turned, weight), (white_first, sems) = refs[:6], refs[6:9], refs[9:]
    rows, width = tok.shape
    copies = weight_copies(info, pieces, weight, sems)
    for copy in copies:
        copy.start()

    def norm_step(i, _):
        at = pl.ds(pl.multiple_of(i * 128, 128), 128)
        white, _inverse = norm_parts(tok[at, :].astype(F32))
        white_first[at, :] = (white * vec[0:1, :] + vec[1:2, :]).astype(BF16)
        return 0

    lax.fori_loop(0, rows // 128, norm_step, 0)
    transpose_by_owner(info, white_first, turned)
    for copy in copies:
        copy.wait()
    side = width // 2
    for part in range(3):
        value = dot_nn(white_first[...], weight[:, part * width : (part + 1) * width])
        if part == 0:
            value = (value + vec[2:3, :]).astype(BF16) * jnp.asarray(HEAD**-0.5, BF16)
        elif part == 2:
            value = (value + vec[3:4, :]).astype(BF16)
        else:
            value = value.astype(BF16)
        packed[:, part * side : (part + 1) * side] = value[:, :side]
        packed[:, (3 + part) * side : (4 + part) * side] = value[:, side:]


def project(info, tok, vec, pieces, deps):
    rows, width = tok.shape
    return run(
        project_kernel,
        "project",
        [(info, SMEM), (tok, VMEM), (vec, VMEM)] + [(piece, HBM) for piece in pieces],
        [
            ((rows, 3 * width), BF16, VMEM),
            ((width, rows), BF16, VMEM),
            ((width, 3 * width), BF16, VMEM),
        ],
        [pltpu.VMEM((rows, width), BF16), pltpu.SemaphoreType.DMA((6,))],
        deps,
    )


def attend_kernel(length, packed, mixed, mixed_turned, logsum):
    side = packed.shape[1] // 3
    blocks = length // 128
    keep = triangle(128)

    def pair_step(pair, _):
        column = pair * 128
        query = packed[:, pl.ds(pl.multiple_of(column, 128), 128)]
        key = packed[:, pl.ds(pl.multiple_of(side + column, 128), 128)]
        value = packed[:, pl.ds(pl.multiple_of(2 * side + column, 128), 128)]
        lane = lax.broadcasted_iota(jnp.int32, query.shape, 1)
        halves = []
        for head in range(2):
            masked = jnp.where((lane < HEAD) == (head == 0), query, jnp.zeros_like(query))
            scores = [
                dot_nt(key[kb * 128 : (kb + 1) * 128], masked[kb * 128 :]) for kb in range(blocks)
            ]
            outs = []
            for qb in range(blocks):
                tiles = [
                    scores[kb][:, (qb - kb) * 128 : (qb - kb + 1) * 128] for kb in range(qb + 1)
                ]
                tiles[qb] = jnp.where(keep, tiles[qb], -1e30)
                highest = tiles[0]
                for tile in tiles[1:]:
                    highest = jnp.maximum(highest, tile)
                highest = jnp.max(highest, axis=0, keepdims=True)
                expo = [jnp.exp(tile - highest) for tile in tiles]
                total = expo[0]
                for tile in expo[1:]:
                    total = total + tile
                total = jnp.sum(total, axis=0, keepdims=True)
                scale = 1.0 / total
                probs = jnp.concatenate([(tile * scale).astype(BF16) for tile in expo], axis=0)
                outs.append(dot_tn(value[: (qb + 1) * 128], probs))
                logsum[0, pair * 2 + head, 0:1, qb * 128 : (qb + 1) * 128] = highest + jnp.log(
                    total
                )
            halves.append(outs)
        at = pl.ds(pl.multiple_of(column, 128), 128)
        for qb in range(blocks):
            both = jnp.concatenate([halves[0][qb][:HEAD], halves[1][qb][HEAD:]], axis=0)
            both = both.astype(BF16)
            mixed_turned[at, qb * 128 : (qb + 1) * 128] = both
            mixed[qb * 128 : (qb + 1) * 128, at] = both.T
        return 0

    lax.fori_loop(0, side // 128, pair_step, 0)


def attend(packed, length, deps):
    rows, columns = packed.shape
    width, seqs = columns // 3, rows // length
    side = width // 2
    heads = side // HEAD
    return run(
        partial(attend_kernel, length),
        "attend",
        [(packed, pl.BlockSpec((length, 3 * side), lambda s, g: (s, g)))],
        [
            ((rows, width), BF16, pl.BlockSpec((length, side), lambda s, g: (s, g))),
            ((width, rows), BF16, pl.BlockSpec((side, length), lambda s, g: (g, s))),
            (
                (seqs, 2 * heads, 1, length),
                F32,
                pl.BlockSpec((1, heads, 1, length), lambda s, g: (s, g, 0, 0)),
            ),
        ],
        deps=deps,
        grid=(seqs, 2),
    )


def feed_kernel(info, mixed, tok, vec, bias, *refs):
    out_pieces, fc1_pieces = refs[:6], refs[6:12]
    hidden, second_turned, act, slope, out_w, fc1_out, second, fc1_w, sems, out_sem = refs[12:]
    step = pl.program_id(0)
    rows, width = tok.shape
    chunk = act.shape[1]
    keep_fc1 = pltpu.make_async_copy(fc1_w, fc1_out, out_sem)

    @pl.when(step == 0)
    def _():
        out_copies = weight_copies(info, out_pieces, out_w, sems.at[0])
        fc1_copies = weight_copies(info, fc1_pieces, fc1_w, sems.at[1])
        for copy in out_copies + fc1_copies:
            copy.start()
        for copy in out_copies:
            copy.wait()

        def norm_step(i, _):
            at = pl.ds(pl.multiple_of(i * 256, 256), 256)
            value = tok[at, :].astype(F32) + dot_nn(mixed[at, :], out_w[...]) + vec[4:5, :]
            hidden[at, :] = value
            white, _inverse = norm_parts(value)
            second[at, :] = (white * vec[5:6, :] + vec[6:7, :]).astype(BF16)
            return 0

        lax.fori_loop(0, rows // 256, norm_step, 0)
        transpose_by_owner(info, second, second_turned)
        for copy in fc1_copies:
            copy.wait()
        keep_fc1.start()

    columns = pl.ds(pl.multiple_of(step * chunk, chunk), chunk)
    u = dot_nn(second[...], fc1_w[:, columns]) + bias[...]
    square = u * u
    t = jnp.tanh(u * (TANH_SCALE + (TANH_SCALE * 0.044715) * square))
    left = 0.5 + 0.5 * t
    act[...] = (u * left).astype(BF16)
    inner = 0.5 * TANH_SCALE + (1.5 * TANH_SCALE * 0.044715) * square
    slope[...] = (left + (u - u * t * t) * inner).astype(BF16)

    @pl.when(step == pl.num_programs(0) - 1)
    def _():
        keep_fc1.wait()


def feed(info, mixed, tok, vec, bias, out_pieces, fc1_pieces, deps):
    rows, width = tok.shape
    ff = bias.shape[1]
    chunk = 256
    by_column = pl.BlockSpec((rows, chunk), lambda j: (0, j))
    return run(
        feed_kernel,
        "feed",
        [
            (info, SMEM),
            (mixed, whole((rows, width))),
            (tok, whole((rows, width))),
            (vec, whole(vec.shape)),
            (bias, pl.BlockSpec((1, chunk), lambda j: (0, j))),
        ]
        + [(piece, HBM) for piece in out_pieces + fc1_pieces],
        [
            ((rows, width), F32, whole((rows, width))),
            ((width, rows), BF16, whole((width, rows))),
            ((rows, ff), BF16, by_column),
            ((rows, ff), BF16, by_column),
            ((width, width), BF16, whole((width, width))),
            ((width, ff), BF16, HBM),
        ],
        [
            pltpu.VMEM((rows, width), BF16),
            pltpu.VMEM((width, ff), BF16),
            pltpu.SemaphoreType.DMA((2, 6)),
            pltpu.SemaphoreType.DMA,
        ],
        deps,
        (ff // chunk,),
    )


def down_grad_kernel(info, act, dy, *refs):
    pieces, (send, keep, sums, weight, sems) = refs[:6], refs[6:]
    step = pl.program_id(0)
    copies = weight_copies(info, pieces, weight, sems)

    @pl.when(step == 0)
    def _():
        for copy in copies:
            copy.start()
        sums[...] = jnp.sum(dy[...].astype(F32), axis=0, keepdims=True)

    block = send.shape[1]
    owner = info[0] ^ ((step & 1) * 2 + (1 - step // 2))
    mine = act[:, pl.ds(pl.multiple_of(owner * block, 128), block)]
    grad = dot_nn(mine.T, dy[...]).astype(BF16)

    @pl.when(step < 2)
    def _():
        send[0] = grad

    @pl.when(step >= 2)
    def _():
        keep[0] = grad

    @pl.when(step == 3)
    def _():
        for copy in copies:
            copy.wait()


def down_grad(info, act, dy, pieces, deps):
    rows, width = dy.shape
    ff = act.shape[1]
    block = ff // 4
    return run(
        down_grad_kernel,
        "down_grad",
        [(info, SMEM), (act, whole((rows, ff))), (dy, whole((rows, width)))]
        + [(piece, HBM) for piece in pieces],
        [
            (
                (2, block, width),
                BF16,
                pl.BlockSpec((1, block, width), lambda i: (jnp.minimum(i, 1), 0, 0)),
            ),
            (
                (2, block, width),
                BF16,
                pl.BlockSpec((1, block, width), lambda i: (jnp.maximum(i - 2, 0), 0, 0)),
            ),
            ((1, width), F32, whole((1, width))),
            ((ff, width), BF16, HBM),
        ],
        [pltpu.SemaphoreType.DMA((6,))],
        deps,
        (4,),
    )


def up_grad_kernel(last, slope, dy, second_turned, fc1_w, fc2_w, *refs):
    if last:
        earlier, hidden, vec = refs[:3]
        keep, send, bias_sums, grad_hidden, branch, sums, total = refs[3:]
    else:
        keep, send, bias_sums, total = refs
    step = pl.program_id(0)
    rows, width = dy.shape
    grad_act = dot_nt(dy[...], fc2_w[...])
    grad_pre = (grad_act * slope[...].astype(F32)).astype(BF16)
    bias_sums[...] = jnp.sum(grad_pre.astype(F32), axis=0, keepdims=True)
    grad = dot_nn(second_turned[...], grad_pre).astype(BF16)
    for slot in range(2):
        keep[slot] = grad[slot * (width // 4) : (slot + 1) * (width // 4)]
        send[slot] = grad[(slot + 2) * (width // 4) : (slot + 3) * (width // 4)]
    part = dot_nt(grad_pre, fc1_w[...])

    @pl.when(step == 0)
    def _():
        total[...] = (earlier[...] + part) if last else part

    @pl.when(step > 0)
    def _():
        total[...] += part

    if not last:
        return

    @pl.when(step == pl.num_programs(0) - 1)
    def _():
        def norm_step(i, carry):
            at = pl.ds(pl.multiple_of(i * 128, 128), 128)
            through, gains, biases = norm_grad_rows(hidden[at, :], total[at, :], vec[5:6, :])
            value = dy[at, :].astype(F32) + through
            grad_hidden[at, :] = value
            rounded = value.astype(BF16)
            branch[at, :] = rounded
            return (
                carry[0] + gains,
                carry[1] + biases,
                carry[2] + jnp.sum(rounded.astype(F32), axis=0, keepdims=True),
            )

        zero = jnp.zeros((1, width), F32)
        gains, biases, outs = lax.fori_loop(0, rows // 128, norm_step, (zero, zero, zero))
        sums[0:1, :] = gains
        sums[1:2, :] = biases
        sums[2:3, :] = outs


def up_grad(half, slope, dy, second_turned, fc1_w, fc2_w, tail, deps):
    rows, width = dy.shape
    ff = slope.shape[1]
    chunk = 512
    steps = ff // 2 // chunk
    start = half * steps
    last = half == 1
    square = whole((rows, width))
    split = pl.BlockSpec((2, width // 4, chunk), lambda j: (0, 0, j))
    inputs = [
        (slope, pl.BlockSpec((rows, chunk), lambda j: (0, j + start))),
        (dy, square),
        (second_turned, whole((width, rows))),
        (fc1_w, pl.BlockSpec((width, chunk), lambda j: (0, j + start))),
        (fc2_w, pl.BlockSpec((chunk, width), lambda j: (j + start, 0))),
    ]
    outputs = [
        ((2, width // 4, ff // 2), BF16, split),
        ((2, width // 4, ff // 2), BF16, split),
        ((1, ff // 2), F32, pl.BlockSpec((1, chunk), lambda j: (0, j))),
    ]
    if last:
        earlier, hidden, vec = tail
        inputs += [(earlier, square), (hidden, square), (vec, whole(vec.shape))]
        outputs += [
            ((rows, width), F32, square),
            ((rows, width), BF16, square),
            ((3, width), F32, whole((3, width))),
        ]
        scratch = [pltpu.VMEM((rows, width), F32)]
    else:
        outputs += [((rows, width), F32, square)]
        scratch = []
    return run(
        partial(up_grad_kernel, last), "up_grad", inputs, outputs, scratch, deps, (steps,)
    )


def attend_grad_kernel(length, with_out, branch, weight, packed, logsum, first_turned, *refs):
    if with_out:
        info, mixed_turned, keep, send, grad_packed, sums, grad_mixed, turned = refs
    else:
        keep, send, grad_packed, sums, grad_mixed = refs
    rows, width = branch.shape
    side = width // 2
    grad_mixed[...] = dot_nt(branch[...], weight[...]).astype(BF16)

    pairs = side // 128
    blocks = length // 128
    causal = triangle(128)

    def pair_step(it, _):
        seq = it // pairs
        pair = it % pairs
        base = seq * length
        column = pair * 128
        at = pl.ds(pl.multiple_of(base, 128), length)
        at_query = pl.ds(pl.multiple_of(column, 128), 128)
        at_key = pl.ds(pl.multiple_of(side + column, 128), 128)
        at_value = pl.ds(pl.multiple_of(2 * side + column, 128), 128)
        query, key, value = packed[at, at_query], packed[at, at_key], packed[at, at_value]
        incoming = grad_mixed[at, at_query]
        lane = lax.broadcasted_iota(jnp.int32, query.shape, 1)
        results = []
        for head in range(2):
            here = (lane < HEAD) == (head == 0)
            query_h = jnp.where(here, query, jnp.zeros_like(query))
            incoming_h = jnp.where(here, incoming, jnp.zeros_like(incoming))
            probs, grads = [], []
            for kb in range(blocks):
                rows_k = slice(kb * 128, (kb + 1) * 128)
                scores = dot_nt(key[rows_k], query_h[kb * 128 :])
                stats = logsum[seq, pair * 2 + head, 0:1, kb * 128 :]
                expo = jnp.exp(scores - stats)
                diagonal = jnp.where(causal, expo[:, :128], 0.0)
                if kb < blocks - 1:
                    expo = jnp.concatenate([diagonal, expo[:, 128:]], axis=1)
                else:
                    expo = diagonal
                probs.append(expo)
                grads.append(dot_nt(value[rows_k], incoming_h[kb * 128 :]))
            inner = []
            for qb in range(blocks):
                total = None
                for kb in range(qb + 1):
                    cut = slice((qb - kb) * 128, (qb - kb + 1) * 128)
                    term = probs[kb][:, cut] * grads[kb][:, cut]
                    total = term if total is None else total + term
                inner.append(jnp.sum(total, axis=0, keepdims=True))
            inner = jnp.concatenate(inner, axis=1)
            score_grads = [
                (probs[kb] * (grads[kb] - inner[:, kb * 128 :])).astype(BF16)
                for kb in range(blocks)
            ]
            grad_values = [
                dot_nn(probs[kb].astype(BF16), incoming[kb * 128 :]) for kb in range(blocks)
            ]
            grad_keys = [dot_nn(score_grads[kb], query[kb * 128 :]) for kb in range(blocks)]
            grad_query = []
            for qb in range(blocks):
                tiles = [
                    score_grads[kb][:, (qb - kb) * 128 : (qb - kb + 1) * 128]
                    for kb in range(qb + 1)
                ]
                grad_query.append(dot_tn(key[: (qb + 1) * 128], jnp.concatenate(tiles, axis=0)))
            results.append((grad_values, grad_keys, grad_query))
        left = lax.broadcasted_iota(jnp.int32, (128, 128), 1) < HEAD
        for b in range(blocks):
            to = pl.ds(pl.multiple_of(base + b * 128, 128), 128)
            grad_packed[to, at_value] = jnp.where(left, results[0][0][b], results[1][0][b]).astype(
                BF16
            )
            grad_packed[to, at_key] = jnp.where(left, results[0][1][b], results[1][1][b]).astype(
                BF16
            )
            both = jnp.concatenate([results[0][2][b][:HEAD], results[1][2][b][HEAD:]], axis=0)
            grad_packed[to, at_query] = (both * HEAD**-0.5).astype(BF16).T
        return 0

    lax.fori_loop(0, (rows // length) * pairs, pair_step, 0)

    quarter = width // 4

    def place(grad, start, stop):
        grad = grad.astype(BF16)
        for slot in range(2):
            keep[slot, :, start:stop] = grad[slot * quarter : (slot + 1) * quarter]
            send[slot, :, start:stop] = grad[(slot + 2) * quarter : (slot + 3) * quarter]

    place(dot_nn(first_turned[...], grad_packed[...]), 0, 3 * side)
    sums[...] = jnp.sum(grad_packed[...].astype(F32), axis=0, keepdims=True)
    if with_out:
        copy_by_owner(info[0], mixed_turned, turned)
        place(dot_nn(turned[...], branch[...]), 3 * side, 3 * side + width)


def attend_grad(half, branch, weight, packed, logsum, first_turned, extra, length, deps):
    rows, width = branch.shape
    side = width // 2
    heads = side // HEAD
    seqs = rows // length
    with_out = half == 0
    columns = 3 * side + (width if with_out else 0)
    inputs = [
        (branch, whole((rows, width))),
        (weight, pl.BlockSpec((side, width), lambda i: (half, 0))),
        (packed, pl.BlockSpec((rows, 3 * side), lambda i: (0, half))),
        (logsum, pl.BlockSpec((seqs, heads, 1, length), lambda i: (0, half, 0, 0))),
        (first_turned, whole((width, rows))),
    ]
    scratch = [pltpu.VMEM((rows, side), BF16)]
    if with_out:
        info, mixed_turned = extra
        inputs += [(info, SMEM), (mixed_turned, whole((width, rows)))]
        scratch += [pltpu.VMEM((width, rows), BF16)]
    split = (2, width // 4, columns)
    return run(
        partial(attend_grad_kernel, length, with_out),
        "attend_grad",
        inputs,
        [
            (split, BF16, whole(split)),
            (split, BF16, whole(split)),
            ((rows, 3 * side), BF16, whole((rows, 3 * side))),
            ((1, 3 * side), F32, whole((1, 3 * side))),
        ],
        scratch,
        deps,
        (1,),
    )


def input_grad_kernel(grad_a, grad_b, tok, grad_hidden, vec, weight, in_grad, sums):
    step = pl.program_id(0)

    @pl.when(step == 0)
    def _():
        sums[...] = jnp.zeros_like(sums)

    side = grad_a.shape[1] // 3
    parts = []
    for part in range(3):
        for grad in (grad_a, grad_b):
            parts.append(grad[:, part * side : (part + 1) * side])
    grad_first = dot_nt(jnp.concatenate(parts, axis=1), weight[...])
    through, gains, biases = norm_grad_rows(tok[...].astype(F32), grad_first, vec[0:1, :])
    in_grad[...] = (grad_hidden[...] + through).astype(BF16)
    sums[0:1, :] += gains
    sums[1:2, :] += biases


def input_grad(grad_a, grad_b, tok, grad_hidden, vec, weight, deps):
    rows, width = tok.shape
    block = 256
    by_row = pl.BlockSpec((block, width), lambda i: (i, 0))
    part = pl.BlockSpec((block, 3 * width // 2), lambda i: (i, 0))
    return run(
        input_grad_kernel,
        "input_grad",
        [
            (grad_a, part),
            (grad_b, part),
            (tok, by_row),
            (grad_hidden, by_row),
            (vec, whole(vec.shape)),
            (weight, whole(weight.shape)),
        ],
        [((rows, width), BF16, by_row), ((2, width), F32, whole((2, width)))],
        deps=deps,
        grid=(rows // block,),
    )


def output_kernel(act, hidden, vec, weight, out):
    out[...] = (hidden[...] + dot_nn(act[...], weight[...]) + vec[7:8, :]).astype(BF16)


def output_rows(act, hidden, vec, weight, deps):
    rows, width = hidden.shape
    ff = act.shape[1]
    block = 256
    by_row = pl.BlockSpec((block, width), lambda i: (i, 0))
    return run(
        output_kernel,
        "output_rows",
        [
            (act, pl.BlockSpec((block, ff), lambda i: (i, 0))),
            (hidden, by_row),
            (vec, whole(vec.shape)),
            (weight, whole(weight.shape)),
        ],
        [((rows, width), BF16, by_row)],
        deps=deps,
        grid=(rows // block,),
    )


def swap(value, axis, size, bit):
    return lax.ppermute(value, axis, [(i, i ^ bit) for i in range(size)])


def gate(value):
    return run(lambda: None, "gate", [], [], deps=[value])[0][0]


def half_rows(block, half):
    part = block.shape[0] // 2
    return lax.dynamic_slice_in_dim(block, half * part, part, 0)


def after(value, token):
    return value + token.astype(value.dtype)


class Chain:
    def __init__(self, keep, send, me, rep, reps, order):
        self.rep, self.me, self.reps = rep, me, reps
        levels = list(range(reps.bit_length() - 1))
        self.steps = []
        for name in order:
            self.steps += levels if name == "r" else [name]
        self.back = [level for level in reversed(self.steps) if level != "x"]
        self.blocks = 2
        self.keep = [keep]
        self.operand = send
        self.got = swap(send, "shard", 4, 1)
        self.cut_rows = []

    def bit(self, level, token):
        return ((self.rep >> level) & 1) + token

    def fold(self, token=0):
        step = self.steps.pop(0)
        terms = self.keep + [self.got]

        def cut(start, size, axis):
            total = None
            for term in terms:
                piece = lax.dynamic_slice_in_dim(term, start, size, axis).astype(F32)
                total = piece if total is None else total + piece
            return total.astype(BF16)

        if step == "x":
            self.operand = cut(1 + token, 1, 0)
            self.keep = [lax.slice_in_dim(term, 0, 1, axis=0) for term in terms]
            self.got = swap(self.operand, "shard", 4, 2)
        else:
            size = terms[0].shape[1] // 2
            bit = self.bit(step, token)
            self.operand = cut((1 - bit) * size, size, 1)
            self.keep = [cut(bit * size, size, 1)]
            self.got = swap(self.operand, "rep", self.reps, 1 << step)
        return self.operand

    def turn(self):
        terms = self.keep + [self.got]
        self.total = sum(term.astype(F32) for term in terms).astype(BF16)[0]

    def spread(self):
        level = self.back.pop(0)
        other = swap(self.total, "rep", self.reps, 1 << level)
        self.total = jnp.where(
            self.bit(level, 0) == 0,
            jnp.concatenate([self.total, other], axis=0),
            jnp.concatenate([other, self.total], axis=0),
        )

    def finish(self):
        while self.steps:
            self.fold()
        self.turn()
        while self.back:
            self.spread()
        return self.total.astype(F32)


def sum_small(value, reps):
    value = value + swap(value, "shard", 4, 1)
    value = value + swap(value, "shard", 4, 2)
    bit = 1
    while bit < reps:
        value = value + swap(value, "rep", reps, bit)
        bit *= 2
    return value


def on_device(
    reps,
    tokens,
    ln1_gain,
    ln1_bias,
    qkv_weight,
    query_bias,
    value_bias,
    out_weight,
    out_bias,
    ln2_gain,
    ln2_bias,
    fc1_weight,
    fc1_bias,
    fc2_weight,
    fc2_bias,
    cotangent,
):
    seqs_here, length, width = tokens.shape
    rows = seqs_here * length
    share = width // 4
    me = lax.axis_index("shard").astype(jnp.int32)
    rep = lax.axis_index("rep").astype(jnp.int32)
    half = rep & 1
    info = jnp.stack([me, half])
    tok = tokens.reshape(rows, width)
    dy = cotangent.reshape(rows, width)

    core = lambda value: swap(value, "shard", 4, 1)
    chip_x = lambda value: swap(value, "shard", 4, 2)
    chip_y = lambda value: swap(value, "rep", reps, 1)

    qkv_mine = half_rows(qkv_weight, half)
    qkv_far = chip_x(qkv_mine)
    small = jnp.concatenate(
        [
            v.reshape(-1, share).astype(F32)
            for v in (
                ln1_gain,
                ln1_bias,
                query_bias,
                value_bias,
                out_bias,
                ln2_gain,
                ln2_bias,
                fc2_bias,
                fc1_bias,
            )
        ],
        axis=0,
    )
    pair = jnp.stack([small, core(small)], axis=0)
    near = jnp.concatenate([pair, chip_x(pair)], axis=0)
    near = jnp.where((me & 1) == 0, near, near[jnp.array([1, 0, 3, 2])])
    near = jnp.where((me & 2) == 0, near, near[jnp.array([2, 3, 0, 1])])
    vec = near[:, :8].transpose(1, 0, 2).reshape(8, width)
    bias = near[:, 8:].reshape(1, -1)

    token = gate(qkv_far)
    out_far = chip_x(half_rows(out_weight, half + token))
    fc1_mine = half_rows(fc1_weight, half + token)
    fc1_far = chip_x(fc1_mine)
    qkv_far_b = chip_y(qkv_far)
    qkv = (qkv_weight, core(qkv_weight), qkv_far, qkv_far_b, core(qkv_far), core(qkv_far_b))
    packed, first_turned, qkv_full, token = project(info, tok, vec, qkv, [fc1_mine])

    token = token[0]
    out_far = after(out_far, token)
    fc1_far = after(fc1_far, token)
    out_far_b = chip_y(out_far)
    fc1_far_b = chip_y(fc1_far)
    fc2_mine = half_rows(fc2_weight, half + token)
    fc2_far = chip_x(fc2_mine)
    mixed, mixed_turned, logsum, token = attend(packed, length, [out_far, fc1_far, fc2_mine])

    token = token[0]
    fc2_far = after(fc2_far, token)
    fc2_far_b = chip_y(fc2_far)
    out = (out_weight, core(out_weight), out_far, out_far_b, core(out_far), core(out_far_b))
    fc1 = (fc1_weight, core(fc1_weight), fc1_far, fc1_far_b, core(fc1_far), core(fc1_far_b))
    fc2 = (fc2_weight, core(fc2_weight), fc2_far, fc2_far_b, core(fc2_far), core(fc2_far_b))
    hidden, second_turned, act, slope, out_full, fc1_full, token = feed(
        info, mixed, tok, vec, bias, out, fc1, [fc2_far]
    )
    send2, keep2, sums_dy, fc2_full, token = down_grad(info, act, dy, fc2, [])

    chain2 = Chain(keep2, send2, me, rep, reps, "xr")
    keep1a, send1a, sums_a, partial_second, token = up_grad(
        0, slope, dy, second_turned, fc1_full, fc2_full, None, [send2]
    )
    sent = chain2.fold(token[0])
    chain1a = Chain(keep1a, send1a, me, rep, reps, "rx")
    keep1b, send1b, sums_b, grad_hidden, branch, sums_ln2, token = up_grad(
        1, slope, dy, second_turned, fc1_full, fc2_full, (partial_second, hidden, vec), [sent]
    )
    sent1a = chain1a.fold(token[0])
    chain1b = Chain(keep1b, send1b, me, rep, reps, "xr")
    keep0a, send0a, grad_a, sums_qa, token = attend_grad(
        0, branch, out_full, packed, logsum, first_turned, (info, mixed_turned), length, [sent1a]
    )
    sent1a = chain1a.fold(token[0])
    sent1b = chain1b.fold(token[0])
    chain0a = Chain(keep0a, send0a, me, rep, reps, "rx")
    keep0b, send0b, grad_b, sums_qb, token = attend_grad(
        1, branch, out_full, packed, logsum, first_turned, None, length, [sent1a, sent1b]
    )
    sent2 = chain2.fold(token[0])
    sent0a = chain0a.fold(token[0])
    chain0b = Chain(keep0b, send0b, me, rep, reps, "xr")
    in_grad, sums_ln1, token = input_grad(
        grad_a, grad_b, tok, grad_hidden, vec, qkv_full, [sent2, sent0a]
    )
    sent1a = chain1a.fold(token[0])
    sent0b = chain0b.fold(token[0])
    output, token = output_rows(act, hidden, vec, fc2_full, [sent1a, sent0b])

    side = width // 2
    sums_packed = jnp.concatenate(
        [sums_qa[:, :side], sums_qb[:, :side], sums_qa[:, 2 * side :], sums_qb[:, 2 * side :]],
        axis=1,
    )
    sums = jnp.concatenate(
        [
            sums_ln1,
            sums_packed.reshape(2, width),
            sums_ln2,
            sums_dy,
            jnp.concatenate([sums_a, sums_b], axis=1).reshape(4, width),
        ],
        axis=0,
    )
    sums = sum_small(sums, reps)
    mine = lax.dynamic_slice_in_dim(sums, me * share, share, 1)
    fc1b = lax.dynamic_slice_in_dim(sums, 8 + me, 1, 0).reshape(width)
    total2 = chain2.finish()
    total1 = jnp.concatenate([chain1a.finish(), chain1b.finish()], axis=1)
    total_a = chain0a.finish()
    total_b = chain0b.finish()
    qkv_grad = jnp.concatenate(
        [
            total[:, part * side : (part + 1) * side]
            for part in range(3)
            for total in (total_a, total_b)
        ],
        axis=1,
    )
    return (
        output.reshape(tokens.shape),
        in_grad.reshape(tokens.shape),
        mine[0],
        mine[1],
        qkv_grad,
        mine[2],
        mine[3],
        total_a[:, 3 * side :],
        mine[6],
        mine[4],
        mine[5],
        total1,
        fc1b,
        total2,
        mine[7],
    )


def solution(mesh):
    spread = P(("rep", "shard"), None, None)
    matrix = P("shard", None)
    vector = P("shard")
    return jax.shard_map(
        partial(on_device, mesh.shape["rep"]),
        mesh=mesh,
        in_specs=(
            spread, vector, vector, matrix, vector, vector, matrix, vector,
            vector, vector, matrix, vector, matrix, vector, spread,
        ),
        out_specs=(
            spread, spread, vector, vector, matrix, vector, vector, matrix,
            vector, vector, vector, matrix, vector, matrix, vector,
        ),
        check_vma=False,
    )
```

```python
from functools import partial
import math

import jax
import jax.numpy as jnp
from jax import lax
from jax.experimental import pallas as pl
from jax.experimental.pallas import tpu as pltpu
from jax.sharding import PartitionSpec as P

HEAD = 64
EPSILON = 1e-05
F32 = jnp.float32
BF16 = jnp.bfloat16
LIMIT = 56 * 1024 * 1024
TANH_SCALE = math.sqrt(2.0 / math.pi)


def dot_nn(left, right):
    return jnp.dot(left, right, preferred_element_type=F32)


def dot_nt(left, right):
    return lax.dot_general(left, right, (((1,), (1,)), ((), ())), preferred_element_type=F32)


def dot_tn(left, right):
    return lax.dot_general(left, right, (((0,), (0,)), ((), ())), preferred_element_type=F32)


def whole(shape):
    return pl.BlockSpec(shape, lambda *_: (0,) * len(shape))


HBM = pl.BlockSpec(memory_space=pl.ANY)
VMEM = pl.BlockSpec(memory_space=pltpu.VMEM)
SMEM = pl.BlockSpec(memory_space=pltpu.SMEM)


def run(body, name, cost, inputs, outputs, scratch=(), deps=(), grid=()):
    count, hidden_inputs = len(inputs), len(deps)
    given = len(outputs)

    def kernel(*refs):
        first = True
        for axis in range(len(grid)):
            first = first & (pl.program_id(axis) == 0)
        token = refs[count + hidden_inputs + given]

        @pl.when(first)
        def _():
            token[0] = 0

        ins = refs[:count]
        outs = refs[count + hidden_inputs : count + hidden_inputs + given]
        body(*ins, *outs, *refs[count + hidden_inputs + given + 1 :])

    return pl.pallas_call(
        kernel,
        grid=grid,
        in_specs=[spec for _, spec in inputs] + [HBM] * hidden_inputs,
        out_specs=[spec for _, _, spec in outputs] + [SMEM],
        out_shape=[jax.ShapeDtypeStruct(shape, dtype) for shape, dtype, _ in outputs]
        + [jax.ShapeDtypeStruct((1,), jnp.int32)],
        scratch_shapes=list(scratch),
        compiler_params=pltpu.CompilerParams(
            vmem_limit_bytes=LIMIT,
            dimension_semantics=("arbitrary",) * len(grid) if grid else None,
        ),
        cost_estimate=pl.CostEstimate(flops=cost, bytes_accessed=cost, transcendentals=0),
        name=name,
    )(*[value for value, _ in inputs], *deps)


def weight_copies(info, pieces, target, sems, start=0):
    me, half = info[0], info[1]
    block = pieces[0].shape[0]
    part = block // 2
    rows = [me * block, (me ^ 1) * block]
    for owner in (me ^ 2, me ^ 3):
        rows += [owner * block + half * part, owner * block + (1 - half) * part]
    columns = pl.ds(start, target.shape[1])
    copies = []
    for index, (piece, row) in enumerate(zip(pieces, rows)):
        size = piece.shape[0]
        row = pl.multiple_of(row, 16)
        source = piece if index < 2 else piece.at[:, columns]
        copies.append(
            pltpu.make_async_copy(source, target.at[pl.ds(row, size), :], sems.at[index])
        )
    return copies


def norm_parts(values):
    average = jnp.mean(values, axis=-1, keepdims=True)
    centred = values - average
    inverse = lax.rsqrt(jnp.mean(centred * centred, axis=-1, keepdims=True) + EPSILON)
    return centred * inverse, inverse


def triangle(block):
    return lax.broadcasted_iota(jnp.int32, (block, block), 0) <= lax.broadcasted_iota(
        jnp.int32, (block, block), 1
    )


def transpose_by_owner(info, source, target):
    block = source.shape[1] // 4
    for owner in range(4):
        turned = source[:, owner * block : (owner + 1) * block].T
        near = owner ^ info[0]
        slot = (near & 1) * 2 + near // 2
        target[pl.ds(pl.multiple_of(slot * block, 16), block), :] = turned


def norm_grad_rows(values, incoming, gain):
    white, inverse = norm_parts(values)
    scaled = incoming * gain
    inner = (
        scaled
        - jnp.mean(scaled, axis=-1, keepdims=True)
        - white * jnp.mean(scaled * white, axis=-1, keepdims=True)
    )
    return (
        inner * inverse,
        jnp.sum(incoming * white, axis=0, keepdims=True),
        jnp.sum(incoming, axis=0, keepdims=True),
    )


def copy_by_owner(me, source, target):
    block = source.shape[0] // 4
    for slot in range(4):
        owner = me ^ ((slot & 1) * 2 + slot // 2)
        target[slot * block : (slot + 1) * block, :] = source[
            pl.ds(pl.multiple_of(owner * block, 16), block), :
        ]


def project_kernel(info, tok, vec, *refs):
    pieces, (packed, turned, weight), (white_first, sems) = refs[:6], refs[6:9], refs[9:]
    rows, width = tok.shape
    copies = weight_copies(info, pieces, weight, sems)
    for copy in copies:
        copy.start()

    def norm_step(i, _):
        at = pl.ds(pl.multiple_of(i * 128, 128), 128)
        white, _inverse = norm_parts(tok[at, :].astype(F32))
        white_first[at, :] = (white * vec[0:1, :] + vec[1:2, :]).astype(BF16)
        return 0

    lax.fori_loop(0, rows // 128, norm_step, 0)
    transpose_by_owner(info, white_first, turned)
    for copy in copies:
        copy.wait()
    side = width // 2
    for part in range(3):
        value = dot_nn(white_first[...], weight[:, part * width : (part + 1) * width])
        if part == 0:
            value = (value + vec[2:3, :]).astype(BF16) * jnp.asarray(HEAD**-0.5, BF16)
        elif part == 2:
            value = (value + vec[3:4, :]).astype(BF16)
        else:
            value = value.astype(BF16)
        packed[:, part * side : (part + 1) * side] = value[:, :side]
        packed[:, (3 + part) * side : (4 + part) * side] = value[:, side:]


def project(info, tok, vec, pieces, deps):
    rows, width = tok.shape
    return run(
        project_kernel,
        "project",
        1,
        [(info, SMEM), (tok, VMEM), (vec, VMEM)] + [(piece, HBM) for piece in pieces],
        [
            ((rows, 3 * width), BF16, VMEM),
            ((width, rows), BF16, VMEM),
            ((width, 3 * width), BF16, VMEM),
        ],
        [pltpu.VMEM((rows, width), BF16), pltpu.SemaphoreType.DMA((6,))],
        deps,
    )


def attend_kernel(length, packed, mixed, mixed_turned, logsum):
    side = packed.shape[1] // 3
    blocks = length // 128
    keep = triangle(128)

    def pair_step(pair, _):
        column = pair * 128
        query = packed[:, pl.ds(pl.multiple_of(column, 128), 128)]
        key = packed[:, pl.ds(pl.multiple_of(side + column, 128), 128)]
        value = packed[:, pl.ds(pl.multiple_of(2 * side + column, 128), 128)]
        lane = lax.broadcasted_iota(jnp.int32, query.shape, 1)
        halves = []
        for head in range(2):
            masked = jnp.where((lane < HEAD) == (head == 0), query, jnp.zeros_like(query))
            scores = [
                dot_nt(key[kb * 128 : (kb + 1) * 128], masked[kb * 128 :]) for kb in range(blocks)
            ]
            outs = []
            for qb in range(blocks):
                tiles = [
                    scores[kb][:, (qb - kb) * 128 : (qb - kb + 1) * 128] for kb in range(qb + 1)
                ]
                tiles[qb] = jnp.where(keep, tiles[qb], -1e30)
                highest = tiles[0]
                for tile in tiles[1:]:
                    highest = jnp.maximum(highest, tile)
                highest = jnp.max(highest, axis=0, keepdims=True)
                expo = [jnp.exp(tile - highest) for tile in tiles]
                total = expo[0]
                for tile in expo[1:]:
                    total = total + tile
                total = jnp.sum(total, axis=0, keepdims=True)
                scale = 1.0 / total
                probs = jnp.concatenate([(tile * scale).astype(BF16) for tile in expo], axis=0)
                outs.append(dot_tn(value[: (qb + 1) * 128], probs))
                logsum[0, pair * 2 + head, 0:1, qb * 128 : (qb + 1) * 128] = highest + jnp.log(
                    total
                )
            halves.append(outs)
        at = pl.ds(pl.multiple_of(column, 128), 128)
        for qb in range(blocks):
            both = jnp.concatenate([halves[0][qb][:HEAD], halves[1][qb][HEAD:]], axis=0)
            both = both.astype(BF16)
            mixed_turned[at, qb * 128 : (qb + 1) * 128] = both
            mixed[qb * 128 : (qb + 1) * 128, at] = both.T
        return 0

    lax.fori_loop(0, side // 128, pair_step, 0)


def attend(packed, length, deps):
    rows, columns = packed.shape
    width, seqs = columns // 3, rows // length
    side = width // 2
    heads = side // HEAD
    return run(
        partial(attend_kernel, length),
        "attend",
        1,
        [(packed, pl.BlockSpec((length, 3 * side), lambda s, g: (s, g)))],
        [
            ((rows, width), BF16, pl.BlockSpec((length, side), lambda s, g: (s, g))),
            ((width, rows), BF16, pl.BlockSpec((side, length), lambda s, g: (g, s))),
            (
                (seqs, 2 * heads, 1, length),
                F32,
                pl.BlockSpec((1, heads, 1, length), lambda s, g: (s, g, 0, 0)),
            ),
        ],
        deps=deps,
        grid=(seqs, 2),
    )


def feed_kernel(info, mixed, tok, vec, bias, *refs):
    far = refs[4:8]
    out_pieces, fc1_pieces = refs[:2] + far, refs[2:4] + far
    hidden, second_turned, act, slope, out_w, fc1_out, second, fc1_w, sems, out_sem = refs[8:]
    step = pl.program_id(0)
    rows, width = tok.shape
    chunk = act.shape[1]
    keep_fc1 = pltpu.make_async_copy(fc1_w, fc1_out, out_sem)

    @pl.when(step == 0)
    def _():
        out_copies = weight_copies(info, out_pieces, out_w, sems.at[0])
        fc1_copies = weight_copies(info, fc1_pieces, fc1_w, sems.at[1], width)
        for copy in out_copies + fc1_copies:
            copy.start()
        for copy in out_copies:
            copy.wait()

        def norm_step(i, _):
            at = pl.ds(pl.multiple_of(i * 256, 256), 256)
            value = tok[at, :].astype(F32) + dot_nn(mixed[at, :], out_w[...]) + vec[4:5, :]
            hidden[at, :] = value
            white, _inverse = norm_parts(value)
            second[at, :] = (white * vec[5:6, :] + vec[6:7, :]).astype(BF16)
            return 0

        lax.fori_loop(0, rows // 256, norm_step, 0)
        transpose_by_owner(info, second, second_turned)
        for copy in fc1_copies:
            copy.wait()
        keep_fc1.start()

    columns = pl.ds(pl.multiple_of(step * chunk, chunk), chunk)
    u = dot_nn(second[...], fc1_w[:, columns]) + bias[...]
    square = u * u
    t = jnp.tanh(u * (TANH_SCALE + (TANH_SCALE * 0.044715) * square))
    left = 0.5 + 0.5 * t
    act[...] = (u * left).astype(BF16)
    inner = 0.5 * TANH_SCALE + (1.5 * TANH_SCALE * 0.044715) * square
    slope[...] = (left + (u - u * t * t) * inner).astype(BF16)

    @pl.when(step == pl.num_programs(0) - 1)
    def _():
        keep_fc1.wait()


def feed(info, mixed, tok, vec, bias, pieces, deps):
    rows, width = tok.shape
    ff = bias.shape[1]
    chunk = 256
    by_column = pl.BlockSpec((rows, chunk), lambda j: (0, j))
    return run(
        feed_kernel,
        "feed",
        1,
        [
            (info, SMEM),
            (mixed, whole((rows, width))),
            (tok, whole((rows, width))),
            (vec, whole(vec.shape)),
            (bias, pl.BlockSpec((1, chunk), lambda j: (0, j))),
        ]
        + [(piece, HBM) for piece in pieces],
        [
            ((rows, width), F32, whole((rows, width))),
            ((width, rows), BF16, whole((width, rows))),
            ((rows, ff), BF16, by_column),
            ((rows, ff), BF16, by_column),
            ((width, width), BF16, whole((width, width))),
            ((width, ff), BF16, HBM),
        ],
        [
            pltpu.VMEM((rows, width), BF16),
            pltpu.VMEM((width, ff), BF16),
            pltpu.SemaphoreType.DMA((2, 6)),
            pltpu.SemaphoreType.DMA,
        ],
        deps,
        (ff // chunk,),
    )


def down_grad_kernel(info, act, dy, *refs):
    pieces, (send, keep, sums, weight, held, sems, out_sem) = refs[:6], refs[6:]
    step = pl.program_id(0)
    copies = weight_copies(info, pieces, held, sems)
    keep_weight = pltpu.make_async_copy(held, weight, out_sem)

    @pl.when(step == 0)
    def _():
        for copy in copies:
            copy.start()
        sums[...] = jnp.sum(dy[...].astype(F32), axis=0, keepdims=True)

    block = send.shape[1]
    owner = info[0] ^ ((step & 1) * 2 + (1 - step // 2))
    mine = act[:, pl.ds(pl.multiple_of(owner * block, 128), block)]
    grad = dot_nn(mine.T, dy[...]).astype(BF16)

    @pl.when(step < 2)
    def _():
        send[0] = grad

    @pl.when(step >= 2)
    def _():
        keep[0] = grad

    @pl.when(step == 1)
    def _():
        for copy in copies:
            copy.wait()
        keep_weight.start()

    @pl.when(step == 3)
    def _():
        keep_weight.wait()


def down_grad(info, act, dy, pieces, deps):
    rows, width = dy.shape
    ff = act.shape[1]
    block = ff // 4
    return run(
        down_grad_kernel,
        "down_grad",
        1,
        [(info, SMEM), (act, whole((rows, ff))), (dy, whole((rows, width)))]
        + [(piece, HBM) for piece in pieces],
        [
            (
                (2, block, width),
                BF16,
                pl.BlockSpec((1, block, width), lambda i: (jnp.minimum(i, 1), 0, 0)),
            ),
            (
                (2, block, width),
                BF16,
                pl.BlockSpec((1, block, width), lambda i: (jnp.maximum(i - 2, 0), 0, 0)),
            ),
            ((1, width), F32, whole((1, width))),
            ((ff, width), BF16, HBM),
        ],
        [
            pltpu.VMEM((ff, width), BF16),
            pltpu.SemaphoreType.DMA((6,)),
            pltpu.SemaphoreType.DMA,
        ],
        deps,
        (4,),
    )


def up_grad_kernel(last, slope, dy, second_turned, fc1_w, fc2_w, *refs):
    if last:
        earlier, hidden, vec = refs[:3]
        keep, send, bias_sums, grad_hidden, branch, sums, total = refs[3:]
    else:
        keep, send, bias_sums, total = refs
    step = pl.program_id(0)
    rows, width = dy.shape
    grad_act = dot_nt(dy[...], fc2_w[...])
    grad_pre = (grad_act * slope[...].astype(F32)).astype(BF16)
    bias_sums[...] = jnp.sum(grad_pre.astype(F32), axis=0, keepdims=True)
    grad = dot_nn(second_turned[...], grad_pre).astype(BF16)
    for slot in range(2):
        keep[slot] = grad[slot * (width // 4) : (slot + 1) * (width // 4)]
        send[slot] = grad[(slot + 2) * (width // 4) : (slot + 3) * (width // 4)]
    part = dot_nt(grad_pre, fc1_w[...])

    @pl.when(step == 0)
    def _():
        total[...] = (earlier[...] + part) if last else part

    @pl.when(step > 0)
    def _():
        total[...] += part

    if not last:
        return

    @pl.when(step == pl.num_programs(0) - 1)
    def _():
        def norm_step(i, carry):
            at = pl.ds(pl.multiple_of(i * 128, 128), 128)
            through, gains, biases = norm_grad_rows(hidden[at, :], total[at, :], vec[5:6, :])
            value = dy[at, :].astype(F32) + through
            grad_hidden[at, :] = value
            rounded = value.astype(BF16)
            branch[at, :] = rounded
            return (
                carry[0] + gains,
                carry[1] + biases,
                carry[2] + jnp.sum(rounded.astype(F32), axis=0, keepdims=True),
            )

        zero = jnp.zeros((1, width), F32)
        gains, biases, outs = lax.fori_loop(0, rows // 128, norm_step, (zero, zero, zero))
        sums[0:1, :] = gains
        sums[1:2, :] = biases
        sums[2:3, :] = outs


def up_grad(half, slope, dy, second_turned, fc1_w, fc2_w, tail, deps):
    rows, width = dy.shape
    ff = slope.shape[1]
    chunk = 512
    steps = ff // 2 // chunk
    start = half * steps
    last = half == 1
    square = whole((rows, width))
    split = pl.BlockSpec((2, width // 4, chunk), lambda j: (0, 0, j))
    inputs = [
        (slope, pl.BlockSpec((rows, chunk), lambda j: (0, j + start))),
        (dy, square),
        (second_turned, whole((width, rows))),
        (fc1_w, pl.BlockSpec((width, chunk), lambda j: (0, j + start))),
        (fc2_w, pl.BlockSpec((chunk, width), lambda j: (j + start, 0))),
    ]
    outputs = [
        ((2, width // 4, ff // 2), BF16, split),
        ((2, width // 4, ff // 2), BF16, split),
        ((1, ff // 2), F32, pl.BlockSpec((1, chunk), lambda j: (0, j))),
    ]
    if last:
        earlier, hidden, vec = tail
        inputs += [(earlier, square), (hidden, square), (vec, whole(vec.shape))]
        outputs += [
            ((rows, width), F32, square),
            ((rows, width), BF16, square),
            ((3, width), F32, whole((3, width))),
        ]
        scratch = [pltpu.VMEM((rows, width), F32)]
    else:
        outputs += [((rows, width), F32, square)]
        scratch = []
    return run(
        partial(up_grad_kernel, last), "up_grad", 1, inputs, outputs, scratch, deps, (steps,)
    )


def attend_grad_kernel(length, with_out, branch, weight, packed, logsum, first_turned, *refs):
    if with_out:
        info, mixed_turned, keep, send, grad_packed, sums, grad_mixed, turned = refs
    else:
        keep, send, grad_packed, sums, grad_mixed = refs
    rows, width = branch.shape
    side = width // 2
    grad_mixed[...] = dot_nt(branch[...], weight[...]).astype(BF16)

    pairs = side // 128
    blocks = length // 128
    causal = triangle(128)

    def pair_step(it, _):
        seq = it // pairs
        pair = it % pairs
        base = seq * length
        column = pair * 128
        at = pl.ds(pl.multiple_of(base, 128), length)
        at_query = pl.ds(pl.multiple_of(column, 128), 128)
        at_key = pl.ds(pl.multiple_of(side + column, 128), 128)
        at_value = pl.ds(pl.multiple_of(2 * side + column, 128), 128)
        query, key, value = packed[at, at_query], packed[at, at_key], packed[at, at_value]
        incoming = grad_mixed[at, at_query]
        lane = lax.broadcasted_iota(jnp.int32, query.shape, 1)
        results = []
        for head in range(2):
            here = (lane < HEAD) == (head == 0)
            query_h = jnp.where(here, query, jnp.zeros_like(query))
            incoming_h = jnp.where(here, incoming, jnp.zeros_like(incoming))
            probs, grads = [], []
            for kb in range(blocks):
                rows_k = slice(kb * 128, (kb + 1) * 128)
                scores = dot_nt(key[rows_k], query_h[kb * 128 :])
                stats = logsum[seq, pair * 2 + head, 0:1, kb * 128 :]
                expo = jnp.exp(scores - stats)
                diagonal = jnp.where(causal, expo[:, :128], 0.0)
                if kb < blocks - 1:
                    expo = jnp.concatenate([diagonal, expo[:, 128:]], axis=1)
                else:
                    expo = diagonal
                probs.append(expo)
                grads.append(dot_nt(value[rows_k], incoming_h[kb * 128 :]))
            inner = []
            for qb in range(blocks):
                total = None
                for kb in range(qb + 1):
                    cut = slice((qb - kb) * 128, (qb - kb + 1) * 128)
                    term = probs[kb][:, cut] * grads[kb][:, cut]
                    total = term if total is None else total + term
                inner.append(jnp.sum(total, axis=0, keepdims=True))
            inner = jnp.concatenate(inner, axis=1)
            score_grads = [
                (probs[kb] * (grads[kb] - inner[:, kb * 128 :])).astype(BF16)
                for kb in range(blocks)
            ]
            grad_values = [
                dot_nn(probs[kb].astype(BF16), incoming[kb * 128 :]) for kb in range(blocks)
            ]
            grad_keys = [dot_nn(score_grads[kb], query[kb * 128 :]) for kb in range(blocks)]
            grad_query = []
            for qb in range(blocks):
                tiles = [
                    score_grads[kb][:, (qb - kb) * 128 : (qb - kb + 1) * 128]
                    for kb in range(qb + 1)
                ]
                grad_query.append(dot_tn(key[: (qb + 1) * 128], jnp.concatenate(tiles, axis=0)))
            results.append((grad_values, grad_keys, grad_query))
        left = lax.broadcasted_iota(jnp.int32, (128, 128), 1) < HEAD
        for b in range(blocks):
            to = pl.ds(pl.multiple_of(base + b * 128, 128), 128)
            grad_packed[to, at_value] = jnp.where(left, results[0][0][b], results[1][0][b]).astype(
                BF16
            )
            grad_packed[to, at_key] = jnp.where(left, results[0][1][b], results[1][1][b]).astype(
                BF16
            )
            both = jnp.concatenate([results[0][2][b][:HEAD], results[1][2][b][HEAD:]], axis=0)
            grad_packed[to, at_query] = (both * HEAD**-0.5).astype(BF16).T
        return 0

    lax.fori_loop(0, (rows // length) * pairs, pair_step, 0)

    quarter = width // 4

    def place(grad, start, stop):
        grad = grad.astype(BF16)
        for slot in range(2):
            keep[slot, :, start:stop] = grad[slot * quarter : (slot + 1) * quarter]
            send[slot, :, start:stop] = grad[(slot + 2) * quarter : (slot + 3) * quarter]

    place(dot_nn(first_turned[...], grad_packed[...]), 0, 3 * side)
    sums[...] = jnp.sum(grad_packed[...].astype(F32), axis=0, keepdims=True)
    if with_out:
        copy_by_owner(info[0], mixed_turned, turned)
        place(dot_nn(turned[...], branch[...]), 3 * side, 3 * side + width)


def attend_grad(half, branch, weight, packed, logsum, first_turned, extra, length, deps):
    rows, width = branch.shape
    side = width // 2
    heads = side // HEAD
    seqs = rows // length
    with_out = half == 0
    columns = 3 * side + (width if with_out else 0)
    inputs = [
        (branch, whole((rows, width))),
        (weight, pl.BlockSpec((side, width), lambda i: (half, 0))),
        (packed, pl.BlockSpec((rows, 3 * side), lambda i: (0, half))),
        (logsum, pl.BlockSpec((seqs, heads, 1, length), lambda i: (0, half, 0, 0))),
        (first_turned, whole((width, rows))),
    ]
    scratch = [pltpu.VMEM((rows, side), BF16)]
    if with_out:
        info, mixed_turned = extra
        inputs += [(info, SMEM), (mixed_turned, whole((width, rows)))]
        scratch += [pltpu.VMEM((width, rows), BF16)]
    split = (2, width // 4, columns)
    return run(
        partial(attend_grad_kernel, length, with_out),
        "attend_grad",
        1,
        inputs,
        [
            (split, BF16, whole(split)),
            (split, BF16, whole(split)),
            ((rows, 3 * side), BF16, whole((rows, 3 * side))),
            ((1, 3 * side), F32, whole((1, 3 * side))),
        ],
        scratch,
        deps,
        (1,),
    )


def input_grad_kernel(grad_a, grad_b, tok, grad_hidden, vec, weight, in_grad, sums):
    step = pl.program_id(0)

    @pl.when(step == 0)
    def _():
        sums[...] = jnp.zeros_like(sums)

    side = grad_a.shape[1] // 3
    parts = []
    for part in range(3):
        for grad in (grad_a, grad_b):
            parts.append(grad[:, part * side : (part + 1) * side])
    grad_first = dot_nt(jnp.concatenate(parts, axis=1), weight[...])
    through, gains, biases = norm_grad_rows(tok[...].astype(F32), grad_first, vec[0:1, :])
    in_grad[...] = (grad_hidden[...] + through).astype(BF16)
    sums[0:1, :] += gains
    sums[1:2, :] += biases


def input_grad(grad_a, grad_b, tok, grad_hidden, vec, weight, deps):
    rows, width = tok.shape
    block = 256
    by_row = pl.BlockSpec((block, width), lambda i: (i, 0))
    part = pl.BlockSpec((block, 3 * width // 2), lambda i: (i, 0))
    return run(
        input_grad_kernel,
        "input_grad",
        1,
        [
            (grad_a, part),
            (grad_b, part),
            (tok, by_row),
            (grad_hidden, by_row),
            (vec, whole(vec.shape)),
            (weight, whole(weight.shape)),
        ],
        [((rows, width), BF16, by_row), ((2, width), F32, whole((2, width)))],
        deps=deps,
        grid=(rows // block,),
    )


def output_kernel(act, hidden, vec, weight, out):
    out[...] = (hidden[...] + dot_nn(act[...], weight[...]) + vec[7:8, :]).astype(BF16)


def output_rows(act, hidden, vec, weight, deps):
    rows, width = hidden.shape
    ff = act.shape[1]
    block = 256
    by_row = pl.BlockSpec((block, width), lambda i: (i, 0))
    return run(
        output_kernel,
        "output_rows",
        1,
        [
            (act, pl.BlockSpec((block, ff), lambda i: (i, 0))),
            (hidden, by_row),
            (vec, whole(vec.shape)),
            (weight, whole(weight.shape)),
        ],
        [((rows, width), BF16, by_row)],
        deps=deps,
        grid=(rows // block,),
    )


def swap(value, axis, size, bit):
    return lax.ppermute(value, axis, [(i, i ^ bit) for i in range(size)])


def gate(value):
    return run(lambda: None, "gate", 1, [], [], deps=[value])[0][0]


def hold(values, after):
    count = len(values)
    shapes = [jax.ShapeDtypeStruct(value.shape, value.dtype) for value in values]
    return pl.pallas_call(
        lambda *_: None,
        in_specs=[HBM] * (count + len(after)),
        out_specs=[HBM] * count,
        out_shape=shapes,
        input_output_aliases={index: index for index in range(count)},
        cost_estimate=pl.CostEstimate(flops=1, bytes_accessed=1, transcendentals=0),
        name="hold",
    )(*values, *after)


def half_rows(block, half):
    part = block.shape[0] // 2
    return lax.dynamic_slice_in_dim(block, half * part, part, 0)


class Chain:
    def __init__(self, keep, send, me, rep, reps, order):
        self.rep, self.me, self.reps = rep, me, reps
        levels = list(range(reps.bit_length() - 1))
        self.steps = []
        for name in order:
            self.steps += levels if name == "r" else [name]
        self.whole = levels[-1]
        self.back = levels[-2::-1]
        self.keep = [keep]
        self.operand = send
        self.got = swap(send, "shard", 4, 1)
        self.total = None
        self.done = False

    def bit(self, level):
        return (self.rep >> level) & 1

    def active(self):
        return not self.done

    def fold(self, after):
        (self.got,) = hold([self.got], [after])
        if not self.steps:
            return self.spread()
        step = self.steps.pop(0)
        terms = self.keep + [self.got]

        def cut(start, size, axis):
            total = None
            for term in terms:
                piece = lax.dynamic_slice_in_dim(term, start, size, axis).astype(F32)
                total = piece if total is None else total + piece
            return total.astype(BF16)

        if step == "x":
            self.operand = cut(1, 1, 0)
            self.keep = [lax.slice_in_dim(term, 0, 1, axis=0) for term in terms]
            self.got = swap(self.operand, "shard", 4, 2)
        elif step == self.whole:
            self.operand = cut(0, terms[0].shape[0], 0)
            self.keep = [self.operand]
            self.got = swap(self.operand, "rep", self.reps, 1 << step)
        else:
            size = terms[0].shape[1] // 2
            bit = self.bit(step)
            self.operand = cut((1 - bit) * size, size, 1)
            self.keep = [cut(bit * size, size, 1)]
            self.got = swap(self.operand, "rep", self.reps, 1 << step)
        return self.operand

    def spread(self):
        if self.total is None:
            terms = self.keep + [self.got]
            self.total = sum(term.astype(F32) for term in terms).astype(BF16)[0]
        else:
            self.total = jnp.where(
                self.bit(self.level) == 0,
                jnp.concatenate([self.total, self.got], axis=0),
                jnp.concatenate([self.got, self.total], axis=0),
            )
        if self.back:
            self.level = self.back.pop(0)
            self.got = swap(self.total, "rep", self.reps, 1 << self.level)
        else:
            self.done = True
        return self.total


def sum_small(value, reps):
    value = value + swap(value, "shard", 4, 1)
    value = value + swap(value, "shard", 4, 2)
    bit = 1
    while bit < reps:
        value = value + swap(value, "rep", reps, bit)
        bit *= 2
    return value


def on_device(
    reps,
    tokens,
    ln1_gain,
    ln1_bias,
    qkv_weight,
    query_bias,
    value_bias,
    out_weight,
    out_bias,
    ln2_gain,
    ln2_bias,
    fc1_weight,
    fc1_bias,
    fc2_weight,
    fc2_bias,
    cotangent,
):
    seqs_here, length, width = tokens.shape
    rows = seqs_here * length
    share = width // 4
    me = lax.axis_index("shard").astype(jnp.int32)
    rep = lax.axis_index("rep").astype(jnp.int32)
    half = rep & 1
    info = jnp.stack([me, half])
    tok = tokens.reshape(rows, width)
    dy = cotangent.reshape(rows, width)

    core = lambda value: swap(value, "shard", 4, 1)
    chip_x = lambda value: swap(value, "shard", 4, 2)
    chip_y = lambda value: swap(value, "rep", reps, 1)

    qkv_mine = half_rows(qkv_weight, half)
    qkv_far = chip_x(qkv_mine)
    early = gate(qkv_mine).astype(F32)
    small = jnp.concatenate(
        [
            v.reshape(-1, share).astype(F32) + early
            for v in (
                ln1_gain,
                ln1_bias,
                query_bias,
                value_bias,
                out_bias,
                ln2_gain,
                ln2_bias,
                fc2_bias,
                fc1_bias,
            )
        ],
        axis=0,
    )
    pair = jnp.stack([small, core(small)], axis=0)
    near = jnp.concatenate([pair, chip_x(pair)], axis=0)
    near = jnp.where((me & 1) == 0, near, near[jnp.array([1, 0, 3, 2])])
    near = jnp.where((me & 2) == 0, near, near[jnp.array([2, 3, 0, 1])])
    vec = near[:, :8].transpose(1, 0, 2).reshape(8, width)
    bias = near[:, 8:].reshape(1, -1)

    token = gate(qkv_far)
    joint_mine = jnp.concatenate(
        [half_rows(out_weight, half + token), half_rows(fc1_weight, half + token)], axis=1
    )
    joint_far = chip_x(joint_mine)
    qkv_far_b = chip_y(qkv_far)
    qkv = (qkv_weight, core(qkv_weight), qkv_far, qkv_far_b, core(qkv_far), core(qkv_far_b))
    packed, first_turned, qkv_full, token = project(info, tok, vec, qkv, [joint_mine])

    fc2_mine = half_rows(fc2_weight, half)
    joint_far, fc2_mine = hold([joint_far, fc2_mine], [packed])
    joint_far_b = chip_y(joint_far)
    fc2_far = chip_x(fc2_mine)
    mixed, mixed_turned, logsum, token = attend(packed, length, [joint_far, fc2_mine])

    joint_far_b, fc2_far = hold([joint_far_b, fc2_far], [mixed])
    fc2_far_b = chip_y(fc2_far)
    joint = (
        out_weight,
        core(out_weight),
        fc1_weight,
        core(fc1_weight),
        joint_far,
        joint_far_b,
        core(joint_far),
        core(joint_far_b),
    )
    hidden, second_turned, act, slope, out_full, fc1_full, token = feed(
        info, mixed, tok, vec, bias, joint, [fc2_far]
    )
    (fc2_far_b,) = hold([fc2_far_b], [hidden])
    fc2 = (fc2_weight, core(fc2_weight), fc2_far, fc2_far_b, core(fc2_far), core(fc2_far_b))
    send2, keep2, sums_dy, fc2_full, token = down_grad(info, act, dy, fc2, [])

    def chain(keep, send, order):
        return Chain(keep, send, me, rep, reps, order)

    def fold(after, *chains):
        sent = []
        for one in chains:
            after = one.fold(after)
            sent.append(after)
        return sent

    chain2 = chain(keep2, send2, "xr")
    keep1a, send1a, sums_a, partial_second, token = up_grad(
        0, slope, dy, second_turned, fc1_full, fc2_full, None, [send2]
    )
    sent = fold(partial_second, chain2)
    chain1a = chain(keep1a, send1a, "rx")
    keep1b, send1b, sums_b, grad_hidden, branch, sums_ln2, token = up_grad(
        1, slope, dy, second_turned, fc1_full, fc2_full, (partial_second, hidden, vec), sent
    )
    sent = fold(branch, chain1a)
    chain1b = chain(keep1b, send1b, "xr")
    keep0a, send0a, grad_a, sums_qa, token = attend_grad(
        0, branch, out_full, packed, logsum, first_turned, (info, mixed_turned), length, sent
    )
    sent = fold(grad_a, chain1a, chain1b, chain2)
    chain0a = chain(keep0a, send0a, "xr")
    keep0b, send0b, grad_b, sums_qb, token = attend_grad(
        1, branch, out_full, packed, logsum, first_turned, None, length, sent
    )
    sent = fold(grad_b, chain0a, chain1a, chain1b, chain2)
    chain0b = chain(keep0b, send0b, "rx")
    in_grad, sums_ln1, token = input_grad(
        grad_a, grad_b, tok, grad_hidden, vec, qkv_full, sent
    )
    sent = fold(in_grad, chain0b, chain1b, chain1a, chain2)
    output, token = output_rows(act, hidden, vec, fc2_full, sent)
    chains = [chain0a, chain0b, chain1b, chain1a, chain2]
    after = output
    while any(one.active() for one in chains):
        after = fold(after, *[one for one in chains if one.active()])[-1]

    side = width // 2
    sums_packed = jnp.concatenate(
        [sums_qa[:, :side], sums_qb[:, :side], sums_qa[:, 2 * side :], sums_qb[:, 2 * side :]],
        axis=1,
    )
    sums = jnp.concatenate(
        [
            sums_ln1,
            sums_packed.reshape(2, width),
            sums_ln2,
            sums_dy,
            jnp.concatenate([sums_a, sums_b], axis=1).reshape(4, width),
        ],
        axis=0,
    )
    sums = sum_small(sums, reps)
    mine = lax.dynamic_slice_in_dim(sums, me * share, share, 1)
    fc1b = lax.dynamic_slice_in_dim(sums, 8 + me, 1, 0).reshape(width)
    total2 = chain2.total.astype(F32)
    total1 = jnp.concatenate([chain1a.total, chain1b.total], axis=1).astype(F32)
    total_a = chain0a.total.astype(F32)
    total_b = chain0b.total.astype(F32)
    qkv_grad = jnp.concatenate(
        [
            total[:, part * side : (part + 1) * side]
            for part in range(3)
            for total in (total_a, total_b)
        ],
        axis=1,
    )
    return (
        output.reshape(tokens.shape),
        in_grad.reshape(tokens.shape),
        mine[0],
        mine[1],
        qkv_grad,
        mine[2],
        mine[3],
        total_a[:, 3 * side :],
        mine[6],
        mine[4],
        mine[5],
        total1,
        fc1b,
        total2,
        mine[7],
    )


def solution(mesh):
    spread = P(("rep", "shard"), None, None)
    matrix = P("shard", None)
    vector = P("shard")
    return jax.shard_map(
        partial(on_device, mesh.shape["rep"]),
        mesh=mesh,
        in_specs=(
            spread, vector, vector, matrix, vector, vector, matrix, vector,
            vector, vector, matrix, vector, matrix, vector, spread,
        ),
        out_specs=(
            spread, spread, vector, vector, matrix, vector, vector, matrix,
            vector, vector, vector, matrix, vector, matrix, vector,
        ),
        check_vma=False,
    )
```

```python
from functools import partial
import math

import jax
import jax.numpy as jnp
from jax import lax
from jax.experimental import pallas as pl
from jax.experimental.pallas import tpu as pltpu
from jax.sharding import PartitionSpec as P

HEAD = 64
EPSILON = 1e-05
F32 = jnp.float32
BF16 = jnp.bfloat16
LIMIT = 56 * 1024 * 1024
TANH_SCALE = math.sqrt(2.0 / math.pi)


def dot_nn(left, right):
    return jnp.dot(left, right, preferred_element_type=F32)


def dot_nt(left, right):
    return lax.dot_general(left, right, (((1,), (1,)), ((), ())), preferred_element_type=F32)


def dot_tn(left, right):
    return lax.dot_general(left, right, (((0,), (0,)), ((), ())), preferred_element_type=F32)


def whole(shape):
    return pl.BlockSpec(shape, lambda *_: (0,) * len(shape))


HBM = pl.BlockSpec(memory_space=pl.ANY)
COST = 1e-9
UNROLL_A = 1
UNROLL_B = 1
VMEM = pl.BlockSpec(memory_space=pltpu.VMEM)
SMEM = pl.BlockSpec(memory_space=pltpu.SMEM)


def run(body, name, cost, inputs, outputs, scratch=(), deps=(), grid=()):
    count, hidden_inputs = len(inputs), len(deps)
    given = len(outputs)

    def kernel(*refs):
        first = True
        for axis in range(len(grid)):
            first = first & (pl.program_id(axis) == 0)
        token = refs[count + hidden_inputs + given]

        @pl.when(first)
        def _():
            token[0] = 0

        ins = refs[:count]
        outs = refs[count + hidden_inputs : count + hidden_inputs + given]
        body(*ins, *outs, *refs[count + hidden_inputs + given + 1 :])

    return pl.pallas_call(
        kernel,
        grid=grid,
        in_specs=[spec for _, spec in inputs] + [HBM] * hidden_inputs,
        out_specs=[spec for _, _, spec in outputs] + [SMEM],
        out_shape=[jax.ShapeDtypeStruct(shape, dtype) for shape, dtype, _ in outputs]
        + [jax.ShapeDtypeStruct((1,), jnp.int32)],
        scratch_shapes=list(scratch),
        compiler_params=pltpu.CompilerParams(
            vmem_limit_bytes=LIMIT,
            dimension_semantics=("arbitrary",) * len(grid) if grid else None,
        ),
        cost_estimate=pl.CostEstimate(
            flops=int(cost * COST), bytes_accessed=1, transcendentals=0
        ),
        name=name,
    )(*[value for value, _ in inputs], *deps)


def weight_copies(info, pieces, target, sems, start=0):
    me, half = info[0], info[1]
    block = pieces[0].shape[0]
    part = block // 2
    rows = [me * block, (me ^ 1) * block]
    for owner in (me ^ 2, me ^ 3):
        rows += [owner * block + half * part, owner * block + (1 - half) * part]
    columns = pl.ds(start, target.shape[1])
    copies = []
    for index, (piece, row) in enumerate(zip(pieces, rows)):
        size = piece.shape[0]
        row = pl.multiple_of(row, 16)
        source = piece if index < 2 else piece.at[:, columns]
        copies.append(
            pltpu.make_async_copy(source, target.at[pl.ds(row, size), :], sems.at[index])
        )
    return copies


def norm_parts(values):
    average = jnp.mean(values, axis=-1, keepdims=True)
    centred = values - average
    inverse = lax.rsqrt(jnp.mean(centred * centred, axis=-1, keepdims=True) + EPSILON)
    return centred * inverse, inverse


def triangle(block):
    return lax.broadcasted_iota(jnp.int32, (block, block), 0) <= lax.broadcasted_iota(
        jnp.int32, (block, block), 1
    )


def transpose_by_owner(info, source, target):
    block = source.shape[1] // 4
    for owner in range(4):
        turned = source[:, owner * block : (owner + 1) * block].T
        near = owner ^ info[0]
        slot = (near & 1) * 2 + near // 2
        target[pl.ds(pl.multiple_of(slot * block, 16), block), :] = turned


def norm_grad_rows(values, incoming, gain):
    white, inverse = norm_parts(values)
    scaled = incoming * gain
    inner = (
        scaled
        - jnp.mean(scaled, axis=-1, keepdims=True)
        - white * jnp.mean(scaled * white, axis=-1, keepdims=True)
    )
    return (
        inner * inverse,
        jnp.sum(incoming * white, axis=0, keepdims=True),
        jnp.sum(incoming, axis=0, keepdims=True),
    )


def copy_by_owner(me, source, target):
    block = source.shape[0] // 4
    for slot in range(4):
        owner = me ^ ((slot & 1) * 2 + slot // 2)
        target[slot * block : (slot + 1) * block, :] = source[
            pl.ds(pl.multiple_of(owner * block, 16), block), :
        ]


def project_kernel(info, tok, vec, *refs):
    pieces, (packed, turned, weight), (white_first, sems) = refs[:6], refs[6:9], refs[9:]
    rows, width = tok.shape
    copies = weight_copies(info, pieces, weight, sems)
    for copy in copies:
        copy.start()

    def norm_step(i, _):
        at = pl.ds(pl.multiple_of(i * 128, 128), 128)
        white, _inverse = norm_parts(tok[at, :].astype(F32))
        white_first[at, :] = (white * vec[0:1, :] + vec[1:2, :]).astype(BF16)
        return 0

    lax.fori_loop(0, rows // 128, norm_step, 0)
    transpose_by_owner(info, white_first, turned)
    for copy in copies:
        copy.wait()
    side = width // 2
    for part in range(3):
        value = dot_nn(white_first[...], weight[:, part * width : (part + 1) * width])
        if part == 0:
            value = (value + vec[2:3, :]).astype(BF16) * jnp.asarray(HEAD**-0.5, BF16)
        elif part == 2:
            value = (value + vec[3:4, :]).astype(BF16)
        else:
            value = value.astype(BF16)
        packed[:, part * side : (part + 1) * side] = value[:, :side]
        packed[:, (3 + part) * side : (4 + part) * side] = value[:, side:]


def project(info, tok, vec, pieces, deps):
    rows, width = tok.shape
    return run(
        project_kernel,
        "project",
        1e-9,
        [(info, SMEM), (tok, VMEM), (vec, VMEM)] + [(piece, HBM) for piece in pieces],
        [
            ((rows, 3 * width), BF16, VMEM),
            ((width, rows), BF16, VMEM),
            ((width, 3 * width), BF16, VMEM),
        ],
        [pltpu.VMEM((rows, width), BF16), pltpu.SemaphoreType.DMA((6,))],
        deps,
    )


def attend_kernel(length, packed, mixed, mixed_turned, logsum):
    side = packed.shape[1] // 3
    blocks = length // 128
    keep = triangle(128)

    def pair_step(pair, _):
        column = pair * 128
        query = packed[:, pl.ds(pl.multiple_of(column, 128), 128)]
        key = packed[:, pl.ds(pl.multiple_of(side + column, 128), 128)]
        value = packed[:, pl.ds(pl.multiple_of(2 * side + column, 128), 128)]
        lane = lax.broadcasted_iota(jnp.int32, query.shape, 1)
        halves = []
        for head in range(2):
            masked = jnp.where((lane < HEAD) == (head == 0), query, jnp.zeros_like(query))
            scores = [
                dot_nt(key[kb * 128 : (kb + 1) * 128], masked[kb * 128 :]) for kb in range(blocks)
            ]
            outs = []
            for qb in range(blocks):
                tiles = [
                    scores[kb][:, (qb - kb) * 128 : (qb - kb + 1) * 128] for kb in range(qb + 1)
                ]
                tiles[qb] = jnp.where(keep, tiles[qb], -1e30)
                highest = tiles[0]
                for tile in tiles[1:]:
                    highest = jnp.maximum(highest, tile)
                highest = jnp.max(highest, axis=0, keepdims=True)
                expo = [jnp.exp(tile - highest) for tile in tiles]
                total = expo[0]
                for tile in expo[1:]:
                    total = total + tile
                total = jnp.sum(total, axis=0, keepdims=True)
                scale = 1.0 / total
                probs = jnp.concatenate([(tile * scale).astype(BF16) for tile in expo], axis=0)
                outs.append(dot_tn(value[: (qb + 1) * 128], probs))
                logsum[0, pair * 2 + head, 0:1, qb * 128 : (qb + 1) * 128] = highest + jnp.log(
                    total
                )
            halves.append(outs)
        at = pl.ds(pl.multiple_of(column, 128), 128)
        for qb in range(blocks):
            both = jnp.concatenate([halves[0][qb][:HEAD], halves[1][qb][HEAD:]], axis=0)
            both = both.astype(BF16)
            mixed_turned[at, qb * 128 : (qb + 1) * 128] = both
            mixed[qb * 128 : (qb + 1) * 128, at] = both.T
        return 0

    lax.fori_loop(0, side // 128, pair_step, 0, unroll=UNROLL_A)


def attend(packed, length, deps):
    rows, columns = packed.shape
    width, seqs = columns // 3, rows // length
    side = width // 2
    heads = side // HEAD
    return run(
        partial(attend_kernel, length),
        "attend",
        13,
        [(packed, pl.BlockSpec((length, 3 * side), lambda s, g: (s, g)))],
        [
            ((rows, width), BF16, pl.BlockSpec((length, side), lambda s, g: (s, g))),
            ((width, rows), BF16, pl.BlockSpec((side, length), lambda s, g: (g, s))),
            (
                (seqs, 2 * heads, 1, length),
                F32,
                pl.BlockSpec((1, heads, 1, length), lambda s, g: (s, g, 0, 0)),
            ),
        ],
        deps=deps,
        grid=(seqs, 2),
    )


def feed_kernel(info, mixed, tok, vec, bias, *refs):
    far = refs[4:8]
    out_pieces, fc1_pieces = refs[:2] + far, refs[2:4] + far
    hidden, second_turned, act, slope, out_w, fc1_out, second, fc1_w, sems, out_sem = refs[8:]
    step = pl.program_id(0)
    rows, width = tok.shape
    chunk = act.shape[1]
    keep_fc1 = pltpu.make_async_copy(fc1_w, fc1_out, out_sem)

    @pl.when(step == 0)
    def _():
        out_copies = weight_copies(info, out_pieces, out_w, sems.at[0])
        fc1_copies = weight_copies(info, fc1_pieces, fc1_w, sems.at[1], width)
        for copy in out_copies + fc1_copies:
            copy.start()
        for copy in out_copies:
            copy.wait()

        def norm_step(i, _):
            at = pl.ds(pl.multiple_of(i * 256, 256), 256)
            value = tok[at, :].astype(F32) + dot_nn(mixed[at, :], out_w[...]) + vec[4:5, :]
            hidden[at, :] = value
            white, _inverse = norm_parts(value)
            second[at, :] = (white * vec[5:6, :] + vec[6:7, :]).astype(BF16)
            return 0

        lax.fori_loop(0, rows // 256, norm_step, 0)
        transpose_by_owner(info, second, second_turned)
        for copy in fc1_copies:
            copy.wait()
        keep_fc1.start()

    columns = pl.ds(pl.multiple_of(step * chunk, chunk), chunk)
    u = dot_nn(second[...], fc1_w[:, columns]) + bias[...]
    square = u * u
    t = jnp.tanh(u * (TANH_SCALE + (TANH_SCALE * 0.044715) * square))
    left = 0.5 + 0.5 * t
    act[...] = (u * left).astype(BF16)
    inner = 0.5 * TANH_SCALE + (1.5 * TANH_SCALE * 0.044715) * square
    slope[...] = (left + (u - u * t * t) * inner).astype(BF16)

    @pl.when(step == pl.num_programs(0) - 1)
    def _():
        keep_fc1.wait()


def feed(info, mixed, tok, vec, bias, pieces, deps):
    rows, width = tok.shape
    ff = bias.shape[1]
    chunk = 256
    by_column = pl.BlockSpec((rows, chunk), lambda j: (0, j))
    return run(
        feed_kernel,
        "feed",
        18,
        [
            (info, SMEM),
            (mixed, whole((rows, width))),
            (tok, whole((rows, width))),
            (vec, whole(vec.shape)),
            (bias, pl.BlockSpec((1, chunk), lambda j: (0, j))),
        ]
        + [(piece, HBM) for piece in pieces],
        [
            ((rows, width), F32, whole((rows, width))),
            ((width, rows), BF16, whole((width, rows))),
            ((rows, ff), BF16, by_column),
            ((rows, ff), BF16, by_column),
            ((width, width), BF16, whole((width, width))),
            ((width, ff), BF16, HBM),
        ],
        [
            pltpu.VMEM((rows, width), BF16),
            pltpu.VMEM((width, ff), BF16),
            pltpu.SemaphoreType.DMA((2, 6)),
            pltpu.SemaphoreType.DMA,
        ],
        deps,
        (ff // chunk,),
    )


def down_grad_kernel(keeping, info, act, dy, *refs):
    if keeping:
        pieces, (near, far, weight, held, mine, sems, piece_sems, out_sem) = refs[:6], refs[6:]
    else:
        near, far, sums, mine, sems = refs
    step = pl.program_id(0)
    block = near.shape[0]

    def fetch(index):
        owner = info[0] ^ (2 * index + (0 if keeping else 1))
        columns = pl.ds(pl.multiple_of(owner * block, 128), block)
        return pltpu.make_async_copy(act.at[:, columns], mine.at[index], sems.at[index])

    if keeping:
        copies = weight_copies(info, pieces, held, piece_sems)
        keep_weight = pltpu.make_async_copy(held, weight, out_sem)

    @pl.when(step == 0)
    def _():
        fetch(0).start()
        fetch(1).start()
        if keeping:
            for copy in copies:
                copy.start()
        else:
            sums[...] = jnp.sum(dy[...].astype(F32), axis=0, keepdims=True)
        fetch(0).wait()
        near[...] = dot_nn(mine[0].T, dy[...]).astype(BF16)
        if keeping:
            for copy in copies:
                copy.wait()
            keep_weight.start()

    @pl.when(step == 1)
    def _():
        fetch(1).wait()
        far[...] = dot_nn(mine[1].T, dy[...]).astype(BF16)
        if keeping:
            keep_weight.wait()


def down_grad(info, act, dy, pieces, deps):
    rows, width = dy.shape
    ff = act.shape[1]
    block = ff // 4
    keeping = len(pieces) > 0
    inputs = [(info, SMEM), (act, HBM), (dy, whole((rows, width)))]
    outputs = [((block, width), BF16, whole((block, width)))] * 2
    scratch = [pltpu.VMEM((2, rows, block), BF16), pltpu.SemaphoreType.DMA((2,))]
    if keeping:
        inputs += [(piece, HBM) for piece in pieces]
        outputs += [((ff, width), BF16, HBM)]
        scratch = [pltpu.VMEM((ff, width), BF16)] + scratch
        scratch += [pltpu.SemaphoreType.DMA((6,)), pltpu.SemaphoreType.DMA]
    else:
        outputs += [((1, width), F32, whole((1, width)))]
    return run(
        partial(down_grad_kernel, keeping), "down_grad", 6, inputs, outputs, scratch, deps, (2,)
    )


def up_grad_kernel(
    slope,
    dy,
    second_turned,
    fc1_w,
    fc2_w,
    hidden,
    vec,
    keep_near,
    keep_far,
    send_near,
    send_far,
    bias_sums,
    grad_hidden,
    branch,
    sums,
    total,
):
    step = pl.program_id(0)
    rows, width = dy.shape
    quarter = width // 4
    grad_act = dot_nt(dy[...], fc2_w[...])
    grad_pre = (grad_act * slope[...].astype(F32)).astype(BF16)
    bias_sums[...] = jnp.sum(grad_pre.astype(F32), axis=0, keepdims=True)
    grad = dot_nn(second_turned[...], grad_pre).astype(BF16)
    for slot, target in enumerate((keep_near, keep_far, send_near, send_far)):
        target[...] = grad[slot * quarter : (slot + 1) * quarter]
    part = dot_nt(grad_pre, fc1_w[...])

    @pl.when(step == 0)
    def _():
        total[...] = part

    @pl.when(step > 0)
    def _():
        total[...] += part

    @pl.when(step == pl.num_programs(0) - 1)
    def _():
        def norm_step(i, carry):
            at = pl.ds(pl.multiple_of(i * 128, 128), 128)
            through, gains, biases = norm_grad_rows(hidden[at, :], total[at, :], vec[5:6, :])
            value = dy[at, :].astype(F32) + through
            grad_hidden[at, :] = value
            rounded = value.astype(BF16)
            branch[at, :] = rounded
            return (
                carry[0] + gains,
                carry[1] + biases,
                carry[2] + jnp.sum(rounded.astype(F32), axis=0, keepdims=True),
            )

        zero = jnp.zeros((1, width), F32)
        gains, biases, outs = lax.fori_loop(0, rows // 128, norm_step, (zero, zero, zero))
        sums[0:1, :] = gains
        sums[1:2, :] = biases
        sums[2:3, :] = outs


def up_grad(slope, dy, second_turned, fc1_w, fc2_w, hidden, vec, deps):
    rows, width = dy.shape
    ff = slope.shape[1]
    chunk = 768
    square = whole((rows, width))
    split = ((width // 4, ff), BF16, pl.BlockSpec((width // 4, chunk), lambda j: (0, j)))
    return run(
        up_grad_kernel,
        "up_grad",
        22,
        [
            (slope, pl.BlockSpec((rows, chunk), lambda j: (0, j))),
            (dy, square),
            (second_turned, whole((width, rows))),
            (fc1_w, pl.BlockSpec((width, chunk), lambda j: (0, j))),
            (fc2_w, pl.BlockSpec((chunk, width), lambda j: (j, 0))),
            (hidden, square),
            (vec, whole(vec.shape)),
        ],
        [
            split,
            split,
            split,
            split,
            ((1, ff), F32, pl.BlockSpec((1, chunk), lambda j: (0, j))),
            ((rows, width), F32, square),
            ((rows, width), BF16, square),
            ((3, width), F32, whole((3, width))),
        ],
        [pltpu.VMEM((rows, width), F32)],
        deps,
        (ff // chunk,),
    )


def attend_grad_kernel(length, with_out, branch, weight, packed, logsum, first_turned, *refs):
    if with_out:
        info, mixed_turned = refs[:2]
        grad_packed, sums, grad_mixed, turned = refs[6:]
    else:
        grad_packed, sums, grad_mixed = refs[4:]
    targets = refs[2:6] if with_out else refs[:4]
    rows, width = branch.shape
    side = width // 2
    grad_mixed[...] = dot_nt(branch[...], weight[...]).astype(BF16)

    pairs = side // 128
    blocks = length // 128
    causal = triangle(128)

    def pair_step(it, _):
        seq = it // pairs
        pair = it % pairs
        base = seq * length
        column = pair * 128
        at = pl.ds(pl.multiple_of(base, 128), length)
        at_query = pl.ds(pl.multiple_of(column, 128), 128)
        at_key = pl.ds(pl.multiple_of(side + column, 128), 128)
        at_value = pl.ds(pl.multiple_of(2 * side + column, 128), 128)
        query, key, value = packed[at, at_query], packed[at, at_key], packed[at, at_value]
        incoming = grad_mixed[at, at_query]
        lane = lax.broadcasted_iota(jnp.int32, query.shape, 1)
        results = []
        for head in range(2):
            here = (lane < HEAD) == (head == 0)
            query_h = jnp.where(here, query, jnp.zeros_like(query))
            incoming_h = jnp.where(here, incoming, jnp.zeros_like(incoming))
            probs, grads = [], []
            for kb in range(blocks):
                rows_k = slice(kb * 128, (kb + 1) * 128)
                scores = dot_nt(key[rows_k], query_h[kb * 128 :])
                stats = logsum[seq, pair * 2 + head, 0:1, kb * 128 :]
                expo = jnp.exp(scores - stats)
                diagonal = jnp.where(causal, expo[:, :128], 0.0)
                if kb < blocks - 1:
                    expo = jnp.concatenate([diagonal, expo[:, 128:]], axis=1)
                else:
                    expo = diagonal
                probs.append(expo)
                grads.append(dot_nt(value[rows_k], incoming_h[kb * 128 :]))
            inner = []
            for qb in range(blocks):
                total = None
                for kb in range(qb + 1):
                    cut = slice((qb - kb) * 128, (qb - kb + 1) * 128)
                    term = probs[kb][:, cut] * grads[kb][:, cut]
                    total = term if total is None else total + term
                inner.append(jnp.sum(total, axis=0, keepdims=True))
            inner = jnp.concatenate(inner, axis=1)
            score_grads = [
                (probs[kb] * (grads[kb] - inner[:, kb * 128 :])).astype(BF16)
                for kb in range(blocks)
            ]
            grad_values = [
                dot_nn(probs[kb].astype(BF16), incoming[kb * 128 :]) for kb in range(blocks)
            ]
            grad_keys = [dot_nn(score_grads[kb], query[kb * 128 :]) for kb in range(blocks)]
            grad_query = []
            for qb in range(blocks):
                tiles = [
                    score_grads[kb][:, (qb - kb) * 128 : (qb - kb + 1) * 128]
                    for kb in range(qb + 1)
                ]
                grad_query.append(dot_tn(key[: (qb + 1) * 128], jnp.concatenate(tiles, axis=0)))
            results.append((grad_values, grad_keys, grad_query))
        left = lax.broadcasted_iota(jnp.int32, (128, 128), 1) < HEAD
        for b in range(blocks):
            to = pl.ds(pl.multiple_of(base + b * 128, 128), 128)
            grad_packed[to, at_value] = jnp.where(left, results[0][0][b], results[1][0][b]).astype(
                BF16
            )
            grad_packed[to, at_key] = jnp.where(left, results[0][1][b], results[1][1][b]).astype(
                BF16
            )
            both = jnp.concatenate([results[0][2][b][:HEAD], results[1][2][b][HEAD:]], axis=0)
            grad_packed[to, at_query] = (both * HEAD**-0.5).astype(BF16).T
        return 0

    lax.fori_loop(0, (rows // length) * pairs, pair_step, 0, unroll=UNROLL_B)

    quarter = width // 4

    def place(grad, start, stop):
        grad = grad.astype(BF16)
        for slot, target in enumerate(targets):
            target[:, start:stop] = grad[slot * quarter : (slot + 1) * quarter]

    place(dot_nn(first_turned[...], grad_packed[...]), 0, 3 * side)
    sums[...] = jnp.sum(grad_packed[...].astype(F32), axis=0, keepdims=True)
    if with_out:
        copy_by_owner(info[0], mixed_turned, turned)
        place(dot_nn(turned[...], branch[...]), 3 * side, 3 * side + width)


def attend_grad(half, branch, weight, packed, logsum, first_turned, extra, length, deps):
    rows, width = branch.shape
    side = width // 2
    heads = side // HEAD
    seqs = rows // length
    with_out = half == 0
    columns = 3 * side + (width if with_out else 0)
    inputs = [
        (branch, whole((rows, width))),
        (weight, pl.BlockSpec((side, width), lambda i: (half, 0))),
        (packed, pl.BlockSpec((rows, 3 * side), lambda i: (0, half))),
        (logsum, pl.BlockSpec((seqs, heads, 1, length), lambda i: (0, half, 0, 0))),
        (first_turned, whole((width, rows))),
    ]
    scratch = [pltpu.VMEM((rows, side), BF16)]
    if with_out:
        info, mixed_turned = extra
        inputs += [(info, SMEM), (mixed_turned, whole((width, rows)))]
        scratch += [pltpu.VMEM((width, rows), BF16)]
    split = (width // 4, columns)
    return run(
        partial(attend_grad_kernel, length, with_out),
        "attend_grad",
        13,
        inputs,
        [
            (split, BF16, whole(split)),
            (split, BF16, whole(split)),
            (split, BF16, whole(split)),
            (split, BF16, whole(split)),
            ((rows, 3 * side), BF16, whole((rows, 3 * side))),
            ((1, 3 * side), F32, whole((1, 3 * side))),
        ],
        scratch,
        deps,
        (1,),
    )


def finish_kernel(
    grad_a, grad_b, tok, grad_hidden, vec, weight, act, hidden, fc2_w, in_grad, sums, out
):
    step = pl.program_id(0)

    @pl.when(step == 0)
    def _():
        sums[...] = jnp.zeros_like(sums)

    side = grad_a.shape[1] // 3
    parts = []
    for part in range(3):
        for grad in (grad_a, grad_b):
            parts.append(grad[:, part * side : (part + 1) * side])
    grad_first = dot_nt(jnp.concatenate(parts, axis=1), weight[...])
    through, gains, biases = norm_grad_rows(tok[...].astype(F32), grad_first, vec[0:1, :])
    in_grad[...] = (grad_hidden[...] + through).astype(BF16)
    sums[0:1, :] += gains
    sums[1:2, :] += biases
    out[...] = (hidden[...] + dot_nn(act[...], fc2_w[...]) + vec[7:8, :]).astype(BF16)


def finish(grad_a, grad_b, tok, grad_hidden, vec, weight, act, hidden, fc2_w, deps):
    rows, width = tok.shape
    ff = act.shape[1]
    block = 256
    by_row = pl.BlockSpec((block, width), lambda i: (i, 0))
    part = pl.BlockSpec((block, 3 * width // 2), lambda i: (i, 0))
    return run(
        finish_kernel,
        "finish",
        1e20,
        [
            (grad_a, part),
            (grad_b, part),
            (tok, by_row),
            (grad_hidden, by_row),
            (vec, whole(vec.shape)),
            (weight, whole(weight.shape)),
            (act, pl.BlockSpec((block, ff), lambda i: (i, 0))),
            (hidden, by_row),
            (fc2_w, whole(fc2_w.shape)),
        ],
        [
            ((rows, width), BF16, by_row),
            ((2, width), F32, whole((2, width))),
            ((rows, width), BF16, by_row),
        ],
        deps=deps,
        grid=(rows // block,),
    )


def swap(value, axis, size, bit):
    return lax.ppermute(value, axis, [(i, i ^ bit) for i in range(size)])


def gate(*values):
    return run(lambda: None, "gate", 1, [], [], deps=values)[0][0]


def hold(values, after):
    count = len(values)
    shapes = [jax.ShapeDtypeStruct(value.shape, value.dtype) for value in values]
    return pl.pallas_call(
        lambda *_: None,
        in_specs=[HBM] * (count + len(after)),
        out_specs=[HBM] * count,
        out_shape=shapes,
        input_output_aliases={index: index for index in range(count)},
        cost_estimate=pl.CostEstimate(flops=1, bytes_accessed=1, transcendentals=0),
        name="hold",
    )(*values, *after)


def half_rows(block, half):
    part = block.shape[0] // 2
    return lax.dynamic_slice_in_dim(block, half * part, part, 0)


class Chain:
    def __init__(self, keep, send, rep, reps):
        self.rep, self.reps = rep, reps
        self.levels = list(range(reps.bit_length() - 1))
        self.back = self.levels[-2::-1]
        self.terms, self.far = [keep[0]], keep[1]
        self.got_far = swap(send[1], "shard", 4, 1)
        self.got = swap(send[0], "shard", 4, 1)
        self.total = None
        self.done = False

    def active(self):
        return not self.done

    def fold(self, token, extra=None):
        self.terms = self.terms + [self.got]
        if self.far is not None:
            total = jnp.where(token == 0, self.far.astype(F32) + self.got_far.astype(F32), 0.0)
            self.operand, self.far = total.astype(BF16), None
            if extra is not None:
                near = (self.terms[0].astype(F32) + self.got.astype(F32)).astype(BF16)
                self.terms = [jnp.concatenate([near, extra[0]], axis=0)]
                self.operand = jnp.concatenate([self.operand, extra[1]], axis=0)
            self.got = swap(self.operand, "shard", 4, 2)
        elif len(self.levels) > 1:
            level = self.levels.pop(0)
            bit = ((self.rep >> level) & 1) + token
            size = self.terms[0].shape[0] // 2
            self.operand = self.cut((1 - bit) * size, size)
            self.terms = [self.cut(bit * size, size)]
            self.got = swap(self.operand, "rep", self.reps, 1 << level)
        elif self.levels:
            level = self.levels.pop(0)
            self.operand = self.add(token)
            self.terms = [self.operand]
            self.got = swap(self.operand, "rep", self.reps, 1 << level)
        else:
            if self.total is None:
                self.total = self.add(token)
            else:
                first = ((self.rep >> self.level) & 1) + token == 0
                self.total = jnp.where(
                    first,
                    jnp.concatenate([self.total, self.got], axis=0),
                    jnp.concatenate([self.got, self.total], axis=0),
                )
            self.operand = self.total
            if self.back:
                self.level = self.back.pop(0)
                self.got = swap(self.total, "rep", self.reps, 1 << self.level)
            else:
                self.done = True
        return self.operand

    def add(self, token):
        total = sum(term.astype(F32) for term in self.terms)
        return jnp.where(token == 0, total, 0.0).astype(BF16)

    def cut(self, start, size):
        total = 0.0
        for term in self.terms:
            total = total + lax.dynamic_slice_in_dim(term, start, size, 0).astype(F32)
        return total.astype(BF16)


def on_device(
    reps,
    tokens,
    ln1_gain,
    ln1_bias,
    qkv_weight,
    query_bias,
    value_bias,
    out_weight,
    out_bias,
    ln2_gain,
    ln2_bias,
    fc1_weight,
    fc1_bias,
    fc2_weight,
    fc2_bias,
    cotangent,
):
    seqs_here, length, width = tokens.shape
    rows = seqs_here * length
    share = width // 4
    me = lax.axis_index("shard").astype(jnp.int32)
    rep = lax.axis_index("rep").astype(jnp.int32)
    half = rep & 1
    info = jnp.stack([me, half])
    tok = tokens.reshape(rows, width)
    dy = cotangent.reshape(rows, width)

    core = lambda value: swap(value, "shard", 4, 1)
    chip_x = lambda value: swap(value, "shard", 4, 2)
    chip_y = lambda value: swap(value, "rep", reps, 1)

    qkv_mine = half_rows(qkv_weight, half)
    qkv_far = chip_x(qkv_mine)
    early = gate(qkv_mine).astype(F32)
    small = jnp.concatenate(
        [
            v.reshape(-1, share).astype(F32) + early
            for v in (
                ln1_gain,
                ln1_bias,
                query_bias,
                value_bias,
                out_bias,
                ln2_gain,
                ln2_bias,
                fc2_bias,
                fc1_bias,
            )
        ],
        axis=0,
    )
    pair = jnp.stack([small, core(small)], axis=0)
    near = jnp.concatenate([pair, chip_x(pair)], axis=0)
    near = jnp.where((me & 1) == 0, near, near[jnp.array([1, 0, 3, 2])])
    near = jnp.where((me & 2) == 0, near, near[jnp.array([2, 3, 0, 1])])
    vec = near[:, :8].transpose(1, 0, 2).reshape(8, width)
    bias = near[:, 8:].reshape(1, -1)

    token = gate(qkv_far)
    joint_mine = jnp.concatenate(
        [half_rows(out_weight, half + token), half_rows(fc1_weight, half + token)], axis=1
    )
    joint_far = chip_x(joint_mine)
    qkv_far_b = chip_y(qkv_far)
    qkv = (qkv_weight, core(qkv_weight), qkv_far, qkv_far_b, core(qkv_far), core(qkv_far_b))
    packed, first_turned, qkv_full, token = project(info, tok, vec, qkv, [joint_mine])

    fc2_mine = half_rows(fc2_weight, half)
    joint_far, fc2_mine = hold([joint_far, fc2_mine], [packed])
    joint_far_b = chip_y(joint_far)
    fc2_far = chip_x(fc2_mine)
    mixed, mixed_turned, logsum, token = attend(packed, length, [joint_far, fc2_mine])

    joint_far_b, fc2_far = hold([joint_far_b, fc2_far], [mixed])
    fc2_far_b = chip_y(fc2_far)
    joint = (
        out_weight,
        core(out_weight),
        fc1_weight,
        core(fc1_weight),
        joint_far,
        joint_far_b,
        core(joint_far),
        core(joint_far_b),
    )
    hidden, second_turned, act, slope, out_full, fc1_full, token = feed(
        info, mixed, tok, vec, bias, joint, [fc2_far]
    )
    *send, sums_dy, token = down_grad(info, act, dy, (), [])

    def fold(token, *chains):
        return [one.fold(token) for one in chains if one.active()]

    (fc2_far_b,) = hold([fc2_far_b], [hidden])
    fc2 = (fc2_weight, core(fc2_weight), fc2_far, fc2_far_b, core(fc2_far), core(fc2_far_b))
    *keep, fc2_full, token = down_grad(info, act, dy, fc2, [])
    chain2 = Chain(keep, send, rep, reps)
    sent = fold(token[0], chain2)
    *parts, sums_fc1, grad_hidden, branch, sums_ln2, token = up_grad(
        slope, dy, second_turned, fc1_full, fc2_full, hidden, vec, sent
    )
    chain1 = Chain(parts[:2], parts[2:], rep, reps)
    sent = fold(token[0], chain2)
    sent += fold(gate(*sent), chain1)
    *parts, grad_a, sums_qa, token = attend_grad(
        0, branch, out_full, packed, logsum, first_turned, (info, mixed_turned), length, sent
    )
    chain0a = Chain(parts[:2], parts[2:], rep, reps)
    sent = fold(token[0], chain2)
    *parts, grad_b, sums_qb, token = attend_grad(
        1, branch, out_full, packed, logsum, first_turned, None, length, sent
    )
    chain0b = Chain(parts[:2], parts[2:], rep, reps)
    sent = fold(token[0], chain1)
    sent += fold(gate(*sent), chain2, chain0a)
    in_grad, sums_ln1, output, token = finish(
        grad_a, grad_b, tok, grad_hidden, vec, qkv_full, act, hidden, fc2_full, sent
    )
    side = width // 2
    sums_packed = jnp.concatenate(
        [sums_qa[:, :side], sums_qb[:, :side], sums_qa[:, 2 * side :], sums_qb[:, 2 * side :]],
        axis=1,
    )
    sums = jnp.concatenate(
        [
            sums_ln1,
            sums_packed.reshape(2, width),
            sums_ln2,
            sums_dy,
            sums_fc1.reshape(4, width),
        ],
        axis=0,
    )
    later = gate(*fold(token[0], chain1, chain2, chain0a))
    sums = sums + later.astype(F32)
    sums = sums + core(sums)
    columns = 3 * side
    row_count = 3 * width // columns

    def owned(owner):
        vectors = lax.dynamic_slice(sums, (0, owner * share), (8, share)).reshape(-1)
        wide = lax.dynamic_slice(sums, (8 + owner, 0), (1, width)).reshape(-1)
        rows_here = jnp.concatenate([vectors, wide]).reshape(row_count, columns)
        return jnp.pad(rows_here, ((0, 64 - row_count), (0, 0))).astype(BF16)

    extra = [owned(me), owned(me ^ 2)]
    chain0b.fold(later, extra)
    going = [chain0b, chain0a, chain1, chain2]
    while any(one.active() for one in going):
        fold(0, *going)
    total2 = chain2.total.astype(F32)
    total1 = chain1.total.astype(F32)
    total_a = chain0a.total.astype(F32)
    total_b = chain0b.total.astype(F32)
    vectors = total_b[share : share + row_count].reshape(-1)
    mine = vectors[: 8 * share].reshape(8, share)
    fc1b = vectors[8 * share :]
    total_b = total_b[:share]
    qkv_grad = jnp.concatenate(
        [
            total[:, part * side : (part + 1) * side]
            for part in range(3)
            for total in (total_a, total_b)
        ],
        axis=1,
    )
    return (
        output.reshape(tokens.shape),
        in_grad.reshape(tokens.shape),
        mine[0],
        mine[1],
        qkv_grad,
        mine[2],
        mine[3],
        total_a[:, 3 * side :],
        mine[6],
        mine[4],
        mine[5],
        total1,
        fc1b,
        total2,
        mine[7],
    )


def solution(mesh):
    spread = P(("rep", "shard"), None, None)
    matrix = P("shard", None)
    vector = P("shard")
    return jax.shard_map(
        partial(on_device, mesh.shape["rep"]),
        mesh=mesh,
        in_specs=(
            spread, vector, vector, matrix, vector, vector, matrix, vector,
            vector, vector, matrix, vector, matrix, vector, spread,
        ),
        out_specs=(
            spread, spread, vector, vector, matrix, vector, vector, matrix,
            vector, vector, vector, matrix, vector, matrix, vector,
        ),
        check_vma=False,
    )
```

```python
from functools import partial
import math

import jax
import jax.numpy as jnp
from jax import lax
from jax.experimental import pallas as pl
from jax.experimental.pallas import tpu as pltpu
from jax.sharding import PartitionSpec as P

HEAD = 64
EPSILON = 1e-05
F32 = jnp.float32
BF16 = jnp.bfloat16
LIMIT = 56 * 1024 * 1024
TANH_SCALE = math.sqrt(2.0 / math.pi)


def dot_nn(left, right):
    return jnp.dot(left, right, preferred_element_type=F32)


def dot_nt(left, right):
    return lax.dot_general(left, right, (((1,), (1,)), ((), ())), preferred_element_type=F32)


def dot_tn(left, right):
    return lax.dot_general(left, right, (((0,), (0,)), ((), ())), preferred_element_type=F32)


def whole(shape):
    return pl.BlockSpec(shape, lambda *_: (0,) * len(shape))


HBM = pl.BlockSpec(memory_space=pl.ANY)
COST = 1e-9
UNROLL_A = 3
UNROLL_B = 3
VMEM = pl.BlockSpec(memory_space=pltpu.VMEM)
SMEM = pl.BlockSpec(memory_space=pltpu.SMEM)


def run(body, name, cost, inputs, outputs, scratch=(), deps=(), grid=()):
    count, hidden_inputs = len(inputs), len(deps)
    given = len(outputs)

    def kernel(*refs):
        first = True
        for axis in range(len(grid)):
            first = first & (pl.program_id(axis) == 0)
        token = refs[count + hidden_inputs + given]

        @pl.when(first)
        def _():
            token[0] = 0

        ins = refs[:count]
        outs = refs[count + hidden_inputs : count + hidden_inputs + given]
        body(*ins, *outs, *refs[count + hidden_inputs + given + 1 :])

    return pl.pallas_call(
        kernel,
        grid=grid,
        in_specs=[spec for _, spec in inputs] + [HBM] * hidden_inputs,
        out_specs=[spec for _, _, spec in outputs] + [SMEM],
        out_shape=[jax.ShapeDtypeStruct(shape, dtype) for shape, dtype, _ in outputs]
        + [jax.ShapeDtypeStruct((1,), jnp.int32)],
        scratch_shapes=list(scratch),
        compiler_params=pltpu.CompilerParams(
            vmem_limit_bytes=LIMIT,
            dimension_semantics=("arbitrary",) * len(grid) if grid else None,
        ),
        cost_estimate=pl.CostEstimate(
            flops=int(cost * COST), bytes_accessed=1, transcendentals=0
        ),
        name=name,
    )(*[value for value, _ in inputs], *deps)


def weight_copies(info, pieces, target, sems, start=0):
    me, half = info[0], info[1]
    block = pieces[0].shape[0]
    part = block // 2
    rows = [me * block, (me ^ 1) * block]
    for owner in (me ^ 2, me ^ 3):
        rows += [owner * block + half * part, owner * block + (1 - half) * part]
    columns = pl.ds(start, target.shape[1])
    copies = []
    for index, (piece, row) in enumerate(zip(pieces, rows)):
        size = piece.shape[0]
        row = pl.multiple_of(row, 16)
        source = piece if index < 2 else piece.at[:, columns]
        copies.append(
            pltpu.make_async_copy(source, target.at[pl.ds(row, size), :], sems.at[index])
        )
    return copies


def norm_parts(values):
    average = jnp.mean(values, axis=-1, keepdims=True)
    centred = values - average
    inverse = lax.rsqrt(jnp.mean(centred * centred, axis=-1, keepdims=True) + EPSILON)
    return centred * inverse, inverse


def triangle(block):
    return lax.broadcasted_iota(jnp.int32, (block, block), 0) <= lax.broadcasted_iota(
        jnp.int32, (block, block), 1
    )


def transpose_by_owner(info, source, target):
    block = source.shape[1] // 4
    for owner in range(4):
        turned = source[:, owner * block : (owner + 1) * block].T
        near = owner ^ info[0]
        slot = (near & 1) * 2 + near // 2
        target[pl.ds(pl.multiple_of(slot * block, 16), block), :] = turned


def norm_grad_rows(values, incoming, gain):
    white, inverse = norm_parts(values)
    scaled = incoming * gain
    inner = (
        scaled
        - jnp.mean(scaled, axis=-1, keepdims=True)
        - white * jnp.mean(scaled * white, axis=-1, keepdims=True)
    )
    return (
        inner * inverse,
        jnp.sum(incoming * white, axis=0, keepdims=True),
        jnp.sum(incoming, axis=0, keepdims=True),
    )


def copy_by_owner(me, source, target):
    block = source.shape[0] // 4
    for slot in range(4):
        owner = me ^ ((slot & 1) * 2 + slot // 2)
        target[slot * block : (slot + 1) * block, :] = source[
            pl.ds(pl.multiple_of(owner * block, 16), block), :
        ]


def project_kernel(info, tok, vec, *refs):
    pieces, (packed, turned, weight), (white_first, sems) = refs[:6], refs[6:9], refs[9:]
    rows, width = tok.shape
    copies = weight_copies(info, pieces, weight, sems)
    for copy in copies:
        copy.start()

    def norm_step(i, _):
        at = pl.ds(pl.multiple_of(i * 128, 128), 128)
        white, _inverse = norm_parts(tok[at, :].astype(F32))
        white_first[at, :] = (white * vec[0:1, :] + vec[1:2, :]).astype(BF16)
        return 0

    lax.fori_loop(0, rows // 128, norm_step, 0)
    transpose_by_owner(info, white_first, turned)
    for copy in copies:
        copy.wait()
    side = width // 2
    for part in range(3):
        value = dot_nn(white_first[...], weight[:, part * width : (part + 1) * width])
        if part == 0:
            value = (value + vec[2:3, :]).astype(BF16) * jnp.asarray(HEAD**-0.5, BF16)
        elif part == 2:
            value = (value + vec[3:4, :]).astype(BF16)
        else:
            value = value.astype(BF16)
        packed[:, part * side : (part + 1) * side] = value[:, :side]
        packed[:, (3 + part) * side : (4 + part) * side] = value[:, side:]


def project(info, tok, vec, pieces, deps):
    rows, width = tok.shape
    return run(
        project_kernel,
        "project",
        1e-9,
        [(info, SMEM), (tok, VMEM), (vec, VMEM)] + [(piece, HBM) for piece in pieces],
        [
            ((rows, 3 * width), BF16, VMEM),
            ((width, rows), BF16, VMEM),
            ((width, 3 * width), BF16, VMEM),
        ],
        [pltpu.VMEM((rows, width), BF16), pltpu.SemaphoreType.DMA((6,))],
        deps,
    )


def attend_kernel(length, packed, mixed, mixed_turned, logsum):
    side = packed.shape[1] // 3
    blocks = length // 128
    keep = triangle(128)

    def pair_step(pair, _):
        column = pair * 128
        query = packed[:, pl.ds(pl.multiple_of(column, 128), 128)]
        key = packed[:, pl.ds(pl.multiple_of(side + column, 128), 128)]
        value = packed[:, pl.ds(pl.multiple_of(2 * side + column, 128), 128)]
        lane = lax.broadcasted_iota(jnp.int32, query.shape, 1)
        halves = []
        for head in range(2):
            masked = jnp.where((lane < HEAD) == (head == 0), query, jnp.zeros_like(query))
            scores = [
                dot_nt(key[kb * 128 : (kb + 1) * 128], masked[kb * 128 :]) for kb in range(blocks)
            ]
            outs = []
            for qb in range(blocks):
                tiles = [
                    scores[kb][:, (qb - kb) * 128 : (qb - kb + 1) * 128] for kb in range(qb + 1)
                ]
                tiles[qb] = jnp.where(keep, tiles[qb], -1e30)
                highest = tiles[0]
                for tile in tiles[1:]:
                    highest = jnp.maximum(highest, tile)
                highest = jnp.max(highest, axis=0, keepdims=True)
                expo = [jnp.exp(tile - highest) for tile in tiles]
                total = expo[0]
                for tile in expo[1:]:
                    total = total + tile
                total = jnp.sum(total, axis=0, keepdims=True)
                scale = 1.0 / total
                probs = jnp.concatenate([(tile * scale).astype(BF16) for tile in expo], axis=0)
                outs.append(dot_tn(value[: (qb + 1) * 128], probs))
                logsum[0, pair * 2 + head, 0:1, qb * 128 : (qb + 1) * 128] = highest + jnp.log(
                    total
                )
            halves.append(outs)
        at = pl.ds(pl.multiple_of(column, 128), 128)
        for qb in range(blocks):
            both = jnp.concatenate([halves[0][qb][:HEAD], halves[1][qb][HEAD:]], axis=0)
            both = both.astype(BF16)
            mixed_turned[at, qb * 128 : (qb + 1) * 128] = both
            mixed[qb * 128 : (qb + 1) * 128, at] = both.T
        return 0

    lax.fori_loop(0, side // 128, pair_step, 0, unroll=UNROLL_A)


def attend(packed, length, deps):
    rows, columns = packed.shape
    width, seqs = columns // 3, rows // length
    side = width // 2
    heads = side // HEAD
    return run(
        partial(attend_kernel, length),
        "attend",
        13,
        [(packed, pl.BlockSpec((length, 3 * side), lambda s, g: (s, g)))],
        [
            ((rows, width), BF16, pl.BlockSpec((length, side), lambda s, g: (s, g))),
            ((width, rows), BF16, pl.BlockSpec((side, length), lambda s, g: (g, s))),
            (
                (seqs, 2 * heads, 1, length),
                F32,
                pl.BlockSpec((1, heads, 1, length), lambda s, g: (s, g, 0, 0)),
            ),
        ],
        deps=deps,
        grid=(seqs, 2),
    )


def feed_kernel(info, mixed, tok, vec, bias, *refs):
    far = refs[4:8]
    out_pieces, fc1_pieces = refs[:2] + far, refs[2:4] + far
    hidden, second_turned, act, slope, out_w, fc1_out, second, fc1_w, sems, out_sem = refs[8:]
    step = pl.program_id(0)
    rows, width = tok.shape
    chunk = act.shape[1]
    keep_fc1 = pltpu.make_async_copy(fc1_w, fc1_out, out_sem)

    @pl.when(step == 0)
    def _():
        out_copies = weight_copies(info, out_pieces, out_w, sems.at[0])
        fc1_copies = weight_copies(info, fc1_pieces, fc1_w, sems.at[1], width)
        for copy in out_copies + fc1_copies:
            copy.start()
        for copy in out_copies:
            copy.wait()

        def norm_step(i, _):
            at = pl.ds(pl.multiple_of(i * 256, 256), 256)
            value = tok[at, :].astype(F32) + dot_nn(mixed[at, :], out_w[...]) + vec[4:5, :]
            hidden[at, :] = value
            white, _inverse = norm_parts(value)
            second[at, :] = (white * vec[5:6, :] + vec[6:7, :]).astype(BF16)
            return 0

        lax.fori_loop(0, rows // 256, norm_step, 0)
        transpose_by_owner(info, second, second_turned)
        for copy in fc1_copies:
            copy.wait()
        keep_fc1.start()

    columns = pl.ds(pl.multiple_of(step * chunk, chunk), chunk)
    u = dot_nn(second[...], fc1_w[:, columns]) + bias[...]
    square = u * u
    t = jnp.tanh(u * (TANH_SCALE + (TANH_SCALE * 0.044715) * square))
    left = 0.5 + 0.5 * t
    act[...] = (u * left).astype(BF16)
    inner = 0.5 * TANH_SCALE + (1.5 * TANH_SCALE * 0.044715) * square
    slope[...] = (left + (u - u * t * t) * inner).astype(BF16)

    @pl.when(step == pl.num_programs(0) - 1)
    def _():
        keep_fc1.wait()


def feed(info, mixed, tok, vec, bias, pieces, deps):
    rows, width = tok.shape
    ff = bias.shape[1]
    chunk = 768
    by_column = pl.BlockSpec((rows, chunk), lambda j: (0, j))
    return run(
        feed_kernel,
        "feed",
        18,
        [
            (info, SMEM),
            (mixed, whole((rows, width))),
            (tok, whole((rows, width))),
            (vec, whole(vec.shape)),
            (bias, pl.BlockSpec((1, chunk), lambda j: (0, j))),
        ]
        + [(piece, HBM) for piece in pieces],
        [
            ((rows, width), F32, whole((rows, width))),
            ((width, rows), BF16, whole((width, rows))),
            ((rows, ff), BF16, by_column),
            ((rows, ff), BF16, by_column),
            ((width, width), BF16, whole((width, width))),
            ((width, ff), BF16, HBM),
        ],
        [
            pltpu.VMEM((rows, width), BF16),
            pltpu.VMEM((width, ff), BF16),
            pltpu.SemaphoreType.DMA((2, 6)),
            pltpu.SemaphoreType.DMA,
        ],
        deps,
        (ff // chunk,),
    )


def down_grad_kernel(sending, info, act, dy, *refs):
    if sending:
        pieces, (near, far, weight, held, mine, sems, piece_sems, out_sem) = refs[:6], refs[6:]
    else:
        near, far, sums, mine, sems = refs
    step = pl.program_id(0)
    block = near.shape[0]

    def fetch(index):
        owner = info[0] ^ (2 * index + (1 if sending else 0))
        columns = pl.ds(pl.multiple_of(owner * block, 128), block)
        return pltpu.make_async_copy(act.at[:, columns], mine.at[index], sems.at[index])

    if sending:
        copies = weight_copies(info, pieces, held, piece_sems)
        keep_weight = pltpu.make_async_copy(held, weight, out_sem)

    @pl.when(step == 0)
    def _():
        fetch(0).start()
        fetch(1).start()
        if sending:
            for copy in copies:
                copy.start()
        else:
            sums[...] = jnp.sum(dy[...].astype(F32), axis=0, keepdims=True)
        fetch(0).wait()
        near[...] = dot_nn(mine[0].T, dy[...]).astype(BF16)
        if sending:
            for copy in copies:
                copy.wait()
            keep_weight.start()

    @pl.when(step == 1)
    def _():
        fetch(1).wait()
        far[...] = dot_nn(mine[1].T, dy[...]).astype(BF16)
        if sending:
            keep_weight.wait()


def down_grad(info, act, dy, pieces, deps):
    rows, width = dy.shape
    ff = act.shape[1]
    block = ff // 4
    sending = len(pieces) > 0
    inputs = [(info, SMEM), (act, HBM), (dy, whole((rows, width)))]
    outputs = [((block, width), BF16, whole((block, width)))] * 2
    scratch = [pltpu.VMEM((2, rows, block), BF16), pltpu.SemaphoreType.DMA((2,))]
    if sending:
        inputs += [(piece, HBM) for piece in pieces]
        outputs += [((ff, width), BF16, HBM)]
        scratch = [pltpu.VMEM((ff, width), BF16)] + scratch
        scratch += [pltpu.SemaphoreType.DMA((6,)), pltpu.SemaphoreType.DMA]
    else:
        outputs += [((1, width), F32, whole((1, width)))]
    return run(
        partial(down_grad_kernel, sending), "down_grad", 6, inputs, outputs, scratch, deps, (2,)
    )


def up_grad_kernel(
    slope,
    dy,
    second_turned,
    fc1_w,
    fc2_w,
    hidden,
    vec,
    keep_near,
    keep_far,
    send_near,
    send_far,
    bias_sums,
    grad_hidden,
    branch,
    sums,
    total,
):
    step = pl.program_id(0)
    rows, width = dy.shape
    quarter = width // 4
    grad_act = dot_nt(dy[...], fc2_w[...])
    grad_pre = (grad_act * slope[...].astype(F32)).astype(BF16)
    bias_sums[...] = jnp.sum(grad_pre.astype(F32), axis=0, keepdims=True)
    grad = dot_nn(second_turned[...], grad_pre).astype(BF16)
    for slot, target in enumerate((keep_near, keep_far, send_near, send_far)):
        target[...] = grad[slot * quarter : (slot + 1) * quarter]
    part = dot_nt(grad_pre, fc1_w[...])

    @pl.when(step == 0)
    def _():
        total[...] = part

    @pl.when(step > 0)
    def _():
        total[...] += part

    @pl.when(step == pl.num_programs(0) - 1)
    def _():
        def norm_step(i, carry):
            at = pl.ds(pl.multiple_of(i * 128, 128), 128)
            through, gains, biases = norm_grad_rows(hidden[at, :], total[at, :], vec[5:6, :])
            value = dy[at, :].astype(F32) + through
            grad_hidden[at, :] = value
            rounded = value.astype(BF16)
            branch[at, :] = rounded
            return (
                carry[0] + gains,
                carry[1] + biases,
                carry[2] + jnp.sum(rounded.astype(F32), axis=0, keepdims=True),
            )

        zero = jnp.zeros((1, width), F32)
        gains, biases, outs = lax.fori_loop(0, rows // 128, norm_step, (zero, zero, zero))
        sums[0:1, :] = gains
        sums[1:2, :] = biases
        sums[2:3, :] = outs


def up_grad(slope, dy, second_turned, fc1_w, fc2_w, hidden, vec, deps):
    rows, width = dy.shape
    ff = slope.shape[1]
    chunk = 768
    square = whole((rows, width))
    split = ((width // 4, ff), BF16, pl.BlockSpec((width // 4, chunk), lambda j: (0, j)))
    return run(
        up_grad_kernel,
        "up_grad",
        22,
        [
            (slope, pl.BlockSpec((rows, chunk), lambda j: (0, j))),
            (dy, square),
            (second_turned, whole((width, rows))),
            (fc1_w, pl.BlockSpec((width, chunk), lambda j: (0, j))),
            (fc2_w, pl.BlockSpec((chunk, width), lambda j: (j, 0))),
            (hidden, square),
            (vec, whole(vec.shape)),
        ],
        [
            split,
            split,
            split,
            split,
            ((1, ff), F32, pl.BlockSpec((1, chunk), lambda j: (0, j))),
            ((rows, width), F32, square),
            ((rows, width), BF16, square),
            ((3, width), F32, whole((3, width))),
        ],
        [pltpu.VMEM((rows, width), F32)],
        deps,
        (ff // chunk,),
    )


def attend_grad_kernel(length, with_out, branch, weight, packed, logsum, first_turned, *refs):
    if with_out:
        info, mixed_turned = refs[:2]
        grad_packed, sums, grad_mixed, turned = refs[6:]
    else:
        grad_packed, sums, grad_mixed = refs[4:]
    targets = refs[2:6] if with_out else refs[:4]
    rows, width = branch.shape
    side = width // 2
    grad_mixed[...] = dot_nt(branch[...], weight[...]).astype(BF16)

    pairs = side // 128
    blocks = length // 128
    causal = triangle(128)

    def pair_step(it, _):
        seq = it // pairs
        pair = it % pairs
        base = seq * length
        column = pair * 128
        at = pl.ds(pl.multiple_of(base, 128), length)
        at_query = pl.ds(pl.multiple_of(column, 128), 128)
        at_key = pl.ds(pl.multiple_of(side + column, 128), 128)
        at_value = pl.ds(pl.multiple_of(2 * side + column, 128), 128)
        query, key, value = packed[at, at_query], packed[at, at_key], packed[at, at_value]
        incoming = grad_mixed[at, at_query]
        lane = lax.broadcasted_iota(jnp.int32, query.shape, 1)
        results = []
        for head in range(2):
            here = (lane < HEAD) == (head == 0)
            query_h = jnp.where(here, query, jnp.zeros_like(query))
            incoming_h = jnp.where(here, incoming, jnp.zeros_like(incoming))
            probs, grads = [], []
            for kb in range(blocks):
                rows_k = slice(kb * 128, (kb + 1) * 128)
                scores = dot_nt(key[rows_k], query_h[kb * 128 :])
                stats = logsum[seq, pair * 2 + head, 0:1, kb * 128 :]
                expo = jnp.exp(scores - stats)
                diagonal = jnp.where(causal, expo[:, :128], 0.0)
                if kb < blocks - 1:
                    expo = jnp.concatenate([diagonal, expo[:, 128:]], axis=1)
                else:
                    expo = diagonal
                probs.append(expo)
                grads.append(dot_nt(value[rows_k], incoming_h[kb * 128 :]))
            inner = []
            for qb in range(blocks):
                total = None
                for kb in range(qb + 1):
                    cut = slice((qb - kb) * 128, (qb - kb + 1) * 128)
                    term = probs[kb][:, cut] * grads[kb][:, cut]
                    total = term if total is None else total + term
                inner.append(jnp.sum(total, axis=0, keepdims=True))
            inner = jnp.concatenate(inner, axis=1)
            score_grads = [
                (probs[kb] * (grads[kb] - inner[:, kb * 128 :])).astype(BF16)
                for kb in range(blocks)
            ]
            grad_values = [
                dot_nn(probs[kb].astype(BF16), incoming[kb * 128 :]) for kb in range(blocks)
            ]
            grad_keys = [dot_nn(score_grads[kb], query[kb * 128 :]) for kb in range(blocks)]
            grad_query = []
            for qb in range(blocks):
                tiles = [
                    score_grads[kb][:, (qb - kb) * 128 : (qb - kb + 1) * 128]
                    for kb in range(qb + 1)
                ]
                grad_query.append(dot_tn(key[: (qb + 1) * 128], jnp.concatenate(tiles, axis=0)))
            results.append((grad_values, grad_keys, grad_query))
        left = lax.broadcasted_iota(jnp.int32, (128, 128), 1) < HEAD
        for b in range(blocks):
            to = pl.ds(pl.multiple_of(base + b * 128, 128), 128)
            grad_packed[to, at_value] = jnp.where(left, results[0][0][b], results[1][0][b]).astype(
                BF16
            )
            grad_packed[to, at_key] = jnp.where(left, results[0][1][b], results[1][1][b]).astype(
                BF16
            )
            both = jnp.concatenate([results[0][2][b][:HEAD], results[1][2][b][HEAD:]], axis=0)
            grad_packed[to, at_query] = (both * HEAD**-0.5).astype(BF16).T
        return 0

    lax.fori_loop(0, (rows // length) * pairs, pair_step, 0, unroll=UNROLL_B)

    quarter = width // 4

    def place(grad, start, stop):
        grad = grad.astype(BF16)
        for slot, target in enumerate(targets):
            target[:, start:stop] = grad[slot * quarter : (slot + 1) * quarter]

    place(dot_nn(first_turned[...], grad_packed[...]), 0, 3 * side)
    sums[...] = jnp.sum(grad_packed[...].astype(F32), axis=0, keepdims=True)
    if with_out:
        copy_by_owner(info[0], mixed_turned, turned)
        place(dot_nn(turned[...], branch[...]), 3 * side, 3 * side + width)


def attend_grad(half, branch, weight, packed, logsum, first_turned, extra, length, deps):
    rows, width = branch.shape
    side = width // 2
    heads = side // HEAD
    seqs = rows // length
    with_out = half == 0
    columns = 3 * side + (width if with_out else 0)
    inputs = [
        (branch, whole((rows, width))),
        (weight, pl.BlockSpec((side, width), lambda i: (half, 0))),
        (packed, pl.BlockSpec((rows, 3 * side), lambda i: (0, half))),
        (logsum, pl.BlockSpec((seqs, heads, 1, length), lambda i: (0, half, 0, 0))),
        (first_turned, whole((width, rows))),
    ]
    scratch = [pltpu.VMEM((rows, side), BF16)]
    if with_out:
        info, mixed_turned = extra
        inputs += [(info, SMEM), (mixed_turned, whole((width, rows)))]
        scratch += [pltpu.VMEM((width, rows), BF16)]
    split = (width // 4, columns)
    return run(
        partial(attend_grad_kernel, length, with_out),
        "attend_grad",
        13,
        inputs,
        [
            (split, BF16, whole(split)),
            (split, BF16, whole(split)),
            (split, BF16, whole(split)),
            (split, BF16, whole(split)),
            ((rows, 3 * side), BF16, whole((rows, 3 * side))),
            ((1, 3 * side), F32, whole((1, 3 * side))),
        ],
        scratch,
        deps,
        (1,),
    )


def finish_kernel(
    grad_a, grad_b, tok, grad_hidden, vec, weight, act, hidden, fc2_w, in_grad, sums, out
):
    step = pl.program_id(0)

    @pl.when(step == 0)
    def _():
        sums[...] = jnp.zeros_like(sums)

    side = grad_a.shape[1] // 3
    parts = []
    for part in range(3):
        for grad in (grad_a, grad_b):
            parts.append(grad[:, part * side : (part + 1) * side])
    grad_first = dot_nt(jnp.concatenate(parts, axis=1), weight[...])
    through, gains, biases = norm_grad_rows(tok[...].astype(F32), grad_first, vec[0:1, :])
    in_grad[...] = (grad_hidden[...] + through).astype(BF16)
    sums[0:1, :] += gains
    sums[1:2, :] += biases
    out[...] = (hidden[...] + dot_nn(act[...], fc2_w[...]) + vec[7:8, :]).astype(BF16)


def finish(grad_a, grad_b, tok, grad_hidden, vec, weight, act, hidden, fc2_w, deps):
    rows, width = tok.shape
    ff = act.shape[1]
    block = 256
    by_row = pl.BlockSpec((block, width), lambda i: (i, 0))
    part = pl.BlockSpec((block, 3 * width // 2), lambda i: (i, 0))
    return run(
        finish_kernel,
        "finish",
        1e20,
        [
            (grad_a, part),
            (grad_b, part),
            (tok, by_row),
            (grad_hidden, by_row),
            (vec, whole(vec.shape)),
            (weight, whole(weight.shape)),
            (act, pl.BlockSpec((block, ff), lambda i: (i, 0))),
            (hidden, by_row),
            (fc2_w, whole(fc2_w.shape)),
        ],
        [
            ((rows, width), BF16, by_row),
            ((2, width), F32, whole((2, width))),
            ((rows, width), BF16, by_row),
        ],
        deps=deps,
        grid=(rows // block,),
    )


def assemble_kernel(grad_a, grad_b, qkv_grad, out_grad, vectors):
    rows = qkv_grad.shape[0]
    side = grad_b.shape[1] // 3
    for part in range(3):
        at = slice(part * side, (part + 1) * side)
        start = 2 * part * side
        qkv_grad[:, start : start + side] = grad_a[:, at].astype(F32)
        qkv_grad[:, start + side : start + 2 * side] = grad_b[:rows, at].astype(F32)
    out_grad[...] = grad_a[:, 3 * side :].astype(F32)
    vectors[...] = grad_b[rows : rows + 16, :].astype(F32)


def assemble(grad_a, grad_b):
    rows, columns = grad_a.shape
    wide = grad_b.shape[1]
    return run(
        assemble_kernel,
        "assemble",
        1,
        [(grad_a, VMEM), (grad_b, VMEM)],
        [
            ((rows, 2 * wide), F32, VMEM),
            ((rows, columns - wide), F32, VMEM),
            ((16, wide), F32, VMEM),
        ],
    )[:3]


def swap(value, axis, size, bit):
    return lax.ppermute(value, axis, [(i, i ^ bit) for i in range(size)])


def gate(*values):
    return run(lambda: None, "gate", 1, [], [], deps=values)[0][0]


def hold(values, after):
    count = len(values)
    shapes = [jax.ShapeDtypeStruct(value.shape, value.dtype) for value in values]
    return pl.pallas_call(
        lambda *_: None,
        in_specs=[HBM] * (count + len(after)),
        out_specs=[HBM] * count,
        out_shape=shapes,
        input_output_aliases={index: index for index in range(count)},
        cost_estimate=pl.CostEstimate(flops=1, bytes_accessed=1, transcendentals=0),
        name="hold",
    )(*values, *after)


def half_rows(block, half):
    part = block.shape[0] // 2
    return lax.dynamic_slice_in_dim(block, half * part, part, 0)


class Chain:
    def __init__(self, keep, send, rep, reps):
        self.rep, self.reps = rep, reps
        self.levels = list(range(reps.bit_length() - 1))
        self.back = self.levels[-2::-1]
        self.terms, self.far = [keep[0]], keep[1]
        self.got_far = swap(send[1], "shard", 4, 1)
        self.got = swap(send[0], "shard", 4, 1)
        self.total = None
        self.done = False

    def active(self):
        return not self.done

    def fold(self, token, extra=None):
        self.terms = self.terms + [self.got]
        if self.far is not None:
            total = jnp.where(token == 0, self.far.astype(F32) + self.got_far.astype(F32), 0.0)
            self.operand, self.far = total.astype(BF16), None
            if extra is not None:
                near = (self.terms[0].astype(F32) + self.got.astype(F32)).astype(BF16)
                self.terms = [jnp.concatenate([near, extra[0]], axis=0)]
                self.operand = jnp.concatenate([self.operand, extra[1]], axis=0)
            self.got = swap(self.operand, "shard", 4, 2)
        elif len(self.levels) > 1:
            level = self.levels.pop(0)
            bit = ((self.rep >> level) & 1) + token
            size = self.terms[0].shape[0] // 2
            self.operand = self.cut((1 - bit) * size, size)
            self.terms = [self.cut(bit * size, size)]
            self.got = swap(self.operand, "rep", self.reps, 1 << level)
        elif self.levels:
            level = self.levels.pop(0)
            self.operand = self.add(token)
            self.terms = [self.operand]
            self.got = swap(self.operand, "rep", self.reps, 1 << level)
        else:
            if self.total is None:
                self.total = self.add(token)
            else:
                first = ((self.rep >> self.level) & 1) + token == 0
                self.total = jnp.where(
                    first,
                    jnp.concatenate([self.total, self.got], axis=0),
                    jnp.concatenate([self.got, self.total], axis=0),
                )
            self.operand = self.total
            if self.back:
                self.level = self.back.pop(0)
                self.got = swap(self.total, "rep", self.reps, 1 << self.level)
            else:
                self.done = True
        return self.operand

    def add(self, token):
        total = sum(term.astype(F32) for term in self.terms)
        return jnp.where(token == 0, total, 0.0).astype(BF16)

    def cut(self, start, size):
        total = 0.0
        for term in self.terms:
            total = total + lax.dynamic_slice_in_dim(term, start, size, 0).astype(F32)
        return total.astype(BF16)


def on_device(
    reps,
    tokens,
    ln1_gain,
    ln1_bias,
    qkv_weight,
    query_bias,
    value_bias,
    out_weight,
    out_bias,
    ln2_gain,
    ln2_bias,
    fc1_weight,
    fc1_bias,
    fc2_weight,
    fc2_bias,
    cotangent,
):
    seqs_here, length, width = tokens.shape
    rows = seqs_here * length
    share = width // 4
    me = lax.axis_index("shard").astype(jnp.int32)
    rep = lax.axis_index("rep").astype(jnp.int32)
    half = rep & 1
    info = jnp.stack([me, half])
    tok = tokens.reshape(rows, width)
    dy = cotangent.reshape(rows, width)

    core = lambda value: swap(value, "shard", 4, 1)
    chip_x = lambda value: swap(value, "shard", 4, 2)
    chip_y = lambda value: swap(value, "rep", reps, 1)

    qkv_mine = half_rows(qkv_weight, half)
    qkv_far = chip_x(qkv_mine)
    early = gate(qkv_mine).astype(F32)
    small = jnp.concatenate(
        [
            v.reshape(-1, share).astype(F32) + early
            for v in (
                ln1_gain,
                ln1_bias,
                query_bias,
                value_bias,
                out_bias,
                ln2_gain,
                ln2_bias,
                fc2_bias,
                fc1_bias,
            )
        ],
        axis=0,
    )
    pair = jnp.stack([small, core(small)], axis=0)
    near = jnp.concatenate([pair, chip_x(pair)], axis=0)
    near = jnp.where((me & 1) == 0, near, near[jnp.array([1, 0, 3, 2])])
    near = jnp.where((me & 2) == 0, near, near[jnp.array([2, 3, 0, 1])])
    vec = near[:, :8].transpose(1, 0, 2).reshape(8, width)
    bias = near[:, 8:].reshape(1, -1)

    token = gate(qkv_far)
    joint_mine = jnp.concatenate(
        [half_rows(out_weight, half + token), half_rows(fc1_weight, half + token)], axis=1
    )
    joint_far = chip_x(joint_mine)
    qkv_far_b = chip_y(qkv_far)
    qkv = (qkv_weight, core(qkv_weight), qkv_far, qkv_far_b, core(qkv_far), core(qkv_far_b))
    packed, first_turned, qkv_full, token = project(info, tok, vec, qkv, [joint_mine, bias])

    fc2_mine = half_rows(fc2_weight, half)
    joint_far, fc2_mine = hold([joint_far, fc2_mine], [packed])
    joint_far_b = chip_y(joint_far)
    fc2_far = chip_x(fc2_mine)
    mixed, mixed_turned, logsum, token = attend(packed, length, [joint_far, fc2_mine])

    joint_far_b, fc2_far = hold([joint_far_b, fc2_far], [mixed])
    fc2_far_b = chip_y(fc2_far)
    joint = (
        out_weight,
        core(out_weight),
        fc1_weight,
        core(fc1_weight),
        joint_far,
        joint_far_b,
        core(joint_far),
        core(joint_far_b),
    )
    hidden, second_turned, act, slope, out_full, fc1_full, token = feed(
        info, mixed, tok, vec, bias, joint, [fc2_far]
    )

    def fold(token, *chains):
        return [one.fold(token) for one in chains if one.active()]

    (fc2_far_b,) = hold([fc2_far_b], [hidden])
    fc2 = (fc2_weight, core(fc2_weight), fc2_far, fc2_far_b, core(fc2_far), core(fc2_far_b))
    *send, fc2_full, token = down_grad(info, act, dy, fc2, [])
    *keep, sums_dy, token = down_grad(info, act, dy, (), send)
    chain2 = Chain(keep, send, rep, reps)
    sent = fold(token[0], chain2)
    *parts, sums_fc1, grad_hidden, branch, sums_ln2, token = up_grad(
        slope, dy, second_turned, fc1_full, fc2_full, hidden, vec, sent
    )
    chain1 = Chain(parts[:2], parts[2:], rep, reps)
    sent = fold(token[0], chain2)
    sent += fold(gate(*sent), chain1)
    *parts, grad_a, sums_qa, token = attend_grad(
        0, branch, out_full, packed, logsum, first_turned, (info, mixed_turned), length, sent
    )
    chain0a = Chain(parts[:2], parts[2:], rep, reps)
    sent = fold(token[0], chain2)
    *parts, grad_b, sums_qb, token = attend_grad(
        1, branch, out_full, packed, logsum, first_turned, None, length, sent
    )
    chain0b = Chain(parts[:2], parts[2:], rep, reps)
    sent = fold(token[0], chain1)
    sent += fold(gate(*sent), chain2, chain0a)
    in_grad, sums_ln1, output, token = finish(
        grad_a, grad_b, tok, grad_hidden, vec, qkv_full, act, hidden, fc2_full, sent
    )
    side = width // 2
    sums_packed = jnp.concatenate(
        [sums_qa[:, :side], sums_qb[:, :side], sums_qa[:, 2 * side :], sums_qb[:, 2 * side :]],
        axis=1,
    )
    sums = jnp.concatenate(
        [
            sums_ln1,
            sums_packed.reshape(2, width),
            sums_ln2,
            sums_dy,
            sums_fc1.reshape(4, width),
        ],
        axis=0,
    )
    later = gate(*fold(token[0], chain0a))
    later = gate(*fold(later, chain2, chain1))
    sums = sums + later.astype(F32)
    sums = sums + core(sums)
    columns = 3 * side
    row_count = 3 * width // columns

    def owned(owner):
        vectors = lax.dynamic_slice(sums, (0, owner * share), (8, share)).reshape(-1)
        wide = lax.dynamic_slice(sums, (8 + owner, 0), (1, width)).reshape(-1)
        rows_here = jnp.concatenate([vectors, wide]).reshape(row_count, columns)
        return jnp.pad(rows_here, ((0, 64 - row_count), (0, 0))).astype(BF16)

    extra = [owned(me), owned(me ^ 2)]
    chain0b.fold(later, extra)
    fold(0, chain0a, chain1, chain2)
    fold(gate(chain0b.fold(0)), chain0a, chain1)
    going = [chain0b, chain0a, chain1, chain2]
    while any(one.active() for one in going):
        fold(0, *going)
    total2 = chain2.total.astype(F32)
    total1 = chain1.total.astype(F32)
    qkv_grad, out_grad, vectors = assemble(chain0a.total, chain0b.total)
    vectors = vectors[:row_count].reshape(-1)
    mine = vectors[: 8 * share].reshape(8, share)
    fc1b = vectors[8 * share :]
    return (
        output.reshape(tokens.shape),
        in_grad.reshape(tokens.shape),
        mine[0],
        mine[1],
        qkv_grad,
        mine[2],
        mine[3],
        out_grad,
        mine[6],
        mine[4],
        mine[5],
        total1,
        fc1b,
        total2,
        mine[7],
    )


def solution(mesh):
    spread = P(("rep", "shard"), None, None)
    matrix = P("shard", None)
    vector = P("shard")
    return jax.shard_map(
        partial(on_device, mesh.shape["rep"]),
        mesh=mesh,
        in_specs=(
            spread, vector, vector, matrix, vector, vector, matrix, vector,
            vector, vector, matrix, vector, matrix, vector, spread,
        ),
        out_specs=(
            spread, spread, vector, vector, matrix, vector, vector, matrix,
            vector, vector, vector, matrix, vector, matrix, vector,
        ),
        check_vma=False,
    )
```

```python
from functools import partial
import math

import jax
import jax.numpy as jnp
from jax import lax
from jax.experimental import pallas as pl
from jax.experimental.pallas import tpu as pltpu
from jax.sharding import PartitionSpec as P

HEAD = 64
EPSILON = 1e-05
F32 = jnp.float32
BF16 = jnp.bfloat16
LIMIT = 56 * 1024 * 1024
TANH_SCALE = math.sqrt(2.0 / math.pi)


def dot_nn(left, right):
    return jnp.dot(left, right, preferred_element_type=F32)


def dot_nt(left, right):
    return lax.dot_general(left, right, (((1,), (1,)), ((), ())), preferred_element_type=F32)


def dot_tn(left, right):
    return lax.dot_general(left, right, (((0,), (0,)), ((), ())), preferred_element_type=F32)


def whole(shape):
    return pl.BlockSpec(shape, lambda *_: (0,) * len(shape))


HBM = pl.BlockSpec(memory_space=pl.ANY)
COST = 1e-9
UNROLL_A = 3
UNROLL_B = 3
VMEM = pl.BlockSpec(memory_space=pltpu.VMEM)
SMEM = pl.BlockSpec(memory_space=pltpu.SMEM)


def run(body, name, cost, inputs, outputs, scratch=(), deps=(), grid=()):
    count, hidden_inputs = len(inputs), len(deps)
    given = len(outputs)

    def kernel(*refs):
        first = True
        for axis in range(len(grid)):
            first = first & (pl.program_id(axis) == 0)
        token = refs[count + hidden_inputs + given]

        @pl.when(first)
        def _():
            token[0] = 0

        ins = refs[:count]
        outs = refs[count + hidden_inputs : count + hidden_inputs + given]
        body(*ins, *outs, *refs[count + hidden_inputs + given + 1 :])

    return pl.pallas_call(
        kernel,
        grid=grid,
        in_specs=[spec for _, spec in inputs] + [HBM] * hidden_inputs,
        out_specs=[spec for _, _, spec in outputs] + [SMEM],
        out_shape=[jax.ShapeDtypeStruct(shape, dtype) for shape, dtype, _ in outputs]
        + [jax.ShapeDtypeStruct((1,), jnp.int32)],
        scratch_shapes=list(scratch),
        compiler_params=pltpu.CompilerParams(
            vmem_limit_bytes=LIMIT,
            dimension_semantics=("arbitrary",) * len(grid) if grid else None,
        ),
        cost_estimate=pl.CostEstimate(
            flops=int(cost * COST), bytes_accessed=1, transcendentals=0
        ),
        name=name,
    )(*[value for value, _ in inputs], *deps)


def weight_copies(info, pieces, target, sems, start=0):
    me, half = info[0], info[1]
    block = pieces[0].shape[0]
    part = block // 2
    rows = [me * block, (me ^ 1) * block]
    for owner in (me ^ 2, me ^ 3):
        rows += [owner * block + half * part, owner * block + (1 - half) * part]
    columns = pl.ds(start, target.shape[1])
    copies = []
    for index, (piece, row) in enumerate(zip(pieces, rows)):
        size = piece.shape[0]
        row = pl.multiple_of(row, 16)
        source = piece if index < 2 else piece.at[:, columns]
        copies.append(
            pltpu.make_async_copy(source, target.at[pl.ds(row, size), :], sems.at[index])
        )
    return copies


def norm_parts(values):
    average = jnp.mean(values, axis=-1, keepdims=True)
    centred = values - average
    inverse = lax.rsqrt(jnp.mean(centred * centred, axis=-1, keepdims=True) + EPSILON)
    return centred * inverse, inverse


def triangle(block):
    return lax.broadcasted_iota(jnp.int32, (block, block), 0) <= lax.broadcasted_iota(
        jnp.int32, (block, block), 1
    )


def transpose_by_owner(info, source, target):
    block = source.shape[1] // 4
    for owner in range(4):
        turned = source[:, owner * block : (owner + 1) * block].T
        near = owner ^ info[0]
        slot = (near & 1) * 2 + near // 2
        target[pl.ds(pl.multiple_of(slot * block, 16), block), :] = turned


def norm_grad_rows(values, incoming, gain):
    white, inverse = norm_parts(values)
    scaled = incoming * gain
    inner = (
        scaled
        - jnp.mean(scaled, axis=-1, keepdims=True)
        - white * jnp.mean(scaled * white, axis=-1, keepdims=True)
    )
    return (
        inner * inverse,
        jnp.sum(incoming * white, axis=0, keepdims=True),
        jnp.sum(incoming, axis=0, keepdims=True),
    )


def copy_by_owner(me, source, target):
    block = source.shape[0] // 4
    for slot in range(4):
        owner = me ^ ((slot & 1) * 2 + slot // 2)
        target[slot * block : (slot + 1) * block, :] = source[
            pl.ds(pl.multiple_of(owner * block, 16), block), :
        ]


def project_kernel(info, tok, vec, *refs):
    pieces, (packed, turned, weight), (white_first, sems) = refs[:6], refs[6:9], refs[9:]
    rows, width = tok.shape
    copies = weight_copies(info, pieces, weight, sems)
    for copy in copies:
        copy.start()

    def norm_step(i, _):
        at = pl.ds(pl.multiple_of(i * 128, 128), 128)
        white, _inverse = norm_parts(tok[at, :].astype(F32))
        white_first[at, :] = (white * vec[0:1, :] + vec[1:2, :]).astype(BF16)
        return 0

    lax.fori_loop(0, rows // 128, norm_step, 0)
    transpose_by_owner(info, white_first, turned)
    for copy in copies:
        copy.wait()
    side = width // 2
    for part in range(3):
        value = dot_nn(white_first[...], weight[:, part * width : (part + 1) * width])
        if part == 0:
            value = (value + vec[2:3, :]).astype(BF16) * jnp.asarray(HEAD**-0.5, BF16)
        elif part == 2:
            value = (value + vec[3:4, :]).astype(BF16)
        else:
            value = value.astype(BF16)
        packed[:, part * side : (part + 1) * side] = value[:, :side]
        packed[:, (3 + part) * side : (4 + part) * side] = value[:, side:]


def project(info, tok, vec, pieces, deps):
    rows, width = tok.shape
    return run(
        project_kernel,
        "project",
        1e-9,
        [(info, SMEM), (tok, VMEM), (vec, VMEM)] + [(piece, HBM) for piece in pieces],
        [
            ((rows, 3 * width), BF16, VMEM),
            ((width, rows), BF16, VMEM),
            ((width, 3 * width), BF16, VMEM),
        ],
        [pltpu.VMEM((rows, width), BF16), pltpu.SemaphoreType.DMA((6,))],
        deps,
    )


def attend_kernel(length, packed, mixed, mixed_turned, logsum):
    side = packed.shape[1] // 3
    blocks = length // 128
    keep = triangle(128)

    def pair_step(pair, _):
        column = pair * 128
        query = packed[:, pl.ds(pl.multiple_of(column, 128), 128)]
        key = packed[:, pl.ds(pl.multiple_of(side + column, 128), 128)]
        value = packed[:, pl.ds(pl.multiple_of(2 * side + column, 128), 128)]
        lane = lax.broadcasted_iota(jnp.int32, query.shape, 1)
        halves = []
        for head in range(2):
            masked = jnp.where((lane < HEAD) == (head == 0), query, jnp.zeros_like(query))
            scores = [
                dot_nt(key[kb * 128 : (kb + 1) * 128], masked[kb * 128 :]) for kb in range(blocks)
            ]
            outs = []
            for qb in range(blocks):
                tiles = [
                    scores[kb][:, (qb - kb) * 128 : (qb - kb + 1) * 128] for kb in range(qb + 1)
                ]
                tiles[qb] = jnp.where(keep, tiles[qb], -1e30)
                highest = tiles[0]
                for tile in tiles[1:]:
                    highest = jnp.maximum(highest, tile)
                highest = jnp.max(highest, axis=0, keepdims=True)
                expo = [jnp.exp(tile - highest) for tile in tiles]
                total = expo[0]
                for tile in expo[1:]:
                    total = total + tile
                total = jnp.sum(total, axis=0, keepdims=True)
                scale = 1.0 / total
                probs = jnp.concatenate([(tile * scale).astype(BF16) for tile in expo], axis=0)
                outs.append(dot_tn(value[: (qb + 1) * 128], probs))
                logsum[0, pair * 2 + head, 0:1, qb * 128 : (qb + 1) * 128] = highest + jnp.log(
                    total
                )
            halves.append(outs)
        at = pl.ds(pl.multiple_of(column, 128), 128)
        for qb in range(blocks):
            both = jnp.concatenate([halves[0][qb][:HEAD], halves[1][qb][HEAD:]], axis=0)
            both = both.astype(BF16)
            mixed_turned[at, qb * 128 : (qb + 1) * 128] = both
            mixed[qb * 128 : (qb + 1) * 128, at] = both.T
        return 0

    lax.fori_loop(0, side // 128, pair_step, 0, unroll=UNROLL_A)


def attend(packed, length, deps):
    rows, columns = packed.shape
    width, seqs = columns // 3, rows // length
    side = width // 2
    heads = side // HEAD
    return run(
        partial(attend_kernel, length),
        "attend",
        13,
        [(packed, pl.BlockSpec((length, 3 * side), lambda s, g: (s, g)))],
        [
            ((rows, width), BF16, pl.BlockSpec((length, side), lambda s, g: (s, g))),
            ((width, rows), BF16, pl.BlockSpec((side, length), lambda s, g: (g, s))),
            (
                (seqs, 2 * heads, 1, length),
                F32,
                pl.BlockSpec((1, heads, 1, length), lambda s, g: (s, g, 0, 0)),
            ),
        ],
        deps=deps,
        grid=(seqs, 2),
    )


def feed_kernel(info, mixed, tok, vec, bias, *refs):
    far = refs[4:8]
    out_pieces, fc1_pieces = refs[:2] + far, refs[2:4] + far
    hidden, second_turned, act, slope, out_w, fc1_out, second, fc1_w, sems, out_sem = refs[8:]
    step = pl.program_id(0)
    rows, width = tok.shape
    chunk = act.shape[1]
    keep_fc1 = pltpu.make_async_copy(fc1_w, fc1_out, out_sem)

    @pl.when(step == 0)
    def _():
        out_copies = weight_copies(info, out_pieces, out_w, sems.at[0])
        fc1_copies = weight_copies(info, fc1_pieces, fc1_w, sems.at[1], width)
        for copy in out_copies + fc1_copies:
            copy.start()
        for copy in out_copies:
            copy.wait()

        def norm_step(i, _):
            at = pl.ds(pl.multiple_of(i * 256, 256), 256)
            value = tok[at, :].astype(F32) + dot_nn(mixed[at, :], out_w[...]) + vec[4:5, :]
            hidden[at, :] = value
            white, _inverse = norm_parts(value)
            second[at, :] = (white * vec[5:6, :] + vec[6:7, :]).astype(BF16)
            return 0

        lax.fori_loop(0, rows // 256, norm_step, 0)
        transpose_by_owner(info, second, second_turned)
        for copy in fc1_copies:
            copy.wait()
        keep_fc1.start()

    columns = pl.ds(pl.multiple_of(step * chunk, chunk), chunk)
    u = dot_nn(second[...], fc1_w[:, columns]) + bias[...]
    square = u * u
    t = jnp.tanh(u * (TANH_SCALE + (TANH_SCALE * 0.044715) * square))
    left = 0.5 + 0.5 * t
    act[...] = (u * left).astype(BF16)
    inner = 0.5 * TANH_SCALE + (1.5 * TANH_SCALE * 0.044715) * square
    slope[...] = (left + (u - u * t * t) * inner).astype(BF16)

    @pl.when(step == pl.num_programs(0) - 1)
    def _():
        keep_fc1.wait()


def feed(info, mixed, tok, vec, bias, pieces, deps):
    rows, width = tok.shape
    ff = bias.shape[1]
    chunk = 768
    by_column = pl.BlockSpec((rows, chunk), lambda j: (0, j))
    return run(
        feed_kernel,
        "feed",
        18,
        [
            (info, SMEM),
            (mixed, whole((rows, width))),
            (tok, whole((rows, width))),
            (vec, whole(vec.shape)),
            (bias, pl.BlockSpec((1, chunk), lambda j: (0, j))),
        ]
        + [(piece, HBM) for piece in pieces],
        [
            ((rows, width), F32, whole((rows, width))),
            ((width, rows), BF16, whole((width, rows))),
            ((rows, ff), BF16, by_column),
            ((rows, ff), BF16, by_column),
            ((width, width), BF16, whole((width, width))),
            ((width, ff), BF16, HBM),
        ],
        [
            pltpu.VMEM((rows, width), BF16),
            pltpu.VMEM((width, ff), BF16),
            pltpu.SemaphoreType.DMA((2, 6)),
            pltpu.SemaphoreType.DMA,
        ],
        deps,
        (ff // chunk,),
    )


def down_grad_kernel(sending, info, act, dy, *refs):
    if sending:
        pieces, (near, far, weight, held, mine, sems, piece_sems, out_sem) = refs[:6], refs[6:]
    else:
        near, far, sums, mine, sems = refs
    step = pl.program_id(0)
    block = near.shape[0]

    def fetch(index):
        owner = info[0] ^ (2 * index + (1 if sending else 0))
        columns = pl.ds(pl.multiple_of(owner * block, 128), block)
        return pltpu.make_async_copy(act.at[:, columns], mine.at[index], sems.at[index])

    if sending:
        copies = weight_copies(info, pieces, held, piece_sems)
        keep_weight = pltpu.make_async_copy(held, weight, out_sem)

    @pl.when(step == 0)
    def _():
        fetch(0).start()
        fetch(1).start()
        if sending:
            for copy in copies:
                copy.start()
        else:
            sums[...] = jnp.sum(dy[...].astype(F32), axis=0, keepdims=True)
        fetch(0).wait()
        near[...] = dot_nn(mine[0].T, dy[...]).astype(BF16)
        if sending:
            for copy in copies:
                copy.wait()
            keep_weight.start()

    @pl.when(step == 1)
    def _():
        fetch(1).wait()
        far[...] = dot_nn(mine[1].T, dy[...]).astype(BF16)
        if sending:
            keep_weight.wait()


def down_grad(info, act, dy, pieces, deps):
    rows, width = dy.shape
    ff = act.shape[1]
    block = ff // 4
    sending = len(pieces) > 0
    inputs = [(info, SMEM), (act, HBM), (dy, whole((rows, width)))]
    outputs = [((block, width), BF16, whole((block, width)))] * 2
    scratch = [pltpu.VMEM((2, rows, block), BF16), pltpu.SemaphoreType.DMA((2,))]
    if sending:
        inputs += [(piece, HBM) for piece in pieces]
        outputs += [((ff, width), BF16, HBM)]
        scratch = [pltpu.VMEM((ff, width), BF16)] + scratch
        scratch += [pltpu.SemaphoreType.DMA((6,)), pltpu.SemaphoreType.DMA]
    else:
        outputs += [((1, width), F32, whole((1, width)))]
    return run(
        partial(down_grad_kernel, sending), "down_grad", 6, inputs, outputs, scratch, deps, (2,)
    )


def up_grad_kernel(
    slope,
    dy,
    second_turned,
    fc1_w,
    fc2_w,
    hidden,
    vec,
    keep_near,
    keep_far,
    send_near,
    send_far,
    bias_sums,
    grad_hidden,
    branch,
    sums,
    total,
):
    step = pl.program_id(0)
    rows, width = dy.shape
    quarter = width // 4
    grad_act = dot_nt(dy[...], fc2_w[...])
    grad_pre = (grad_act * slope[...].astype(F32)).astype(BF16)
    bias_sums[...] = jnp.sum(grad_pre.astype(F32), axis=0, keepdims=True)
    grad = dot_nn(second_turned[...], grad_pre).astype(BF16)
    for slot, target in enumerate((keep_near, keep_far, send_near, send_far)):
        target[...] = grad[slot * quarter : (slot + 1) * quarter]
    part = dot_nt(grad_pre, fc1_w[...])

    @pl.when(step == 0)
    def _():
        total[...] = part

    @pl.when(step > 0)
    def _():
        total[...] += part

    @pl.when(step == pl.num_programs(0) - 1)
    def _():
        def norm_step(i, carry):
            at = pl.ds(pl.multiple_of(i * 128, 128), 128)
            through, gains, biases = norm_grad_rows(hidden[at, :], total[at, :], vec[5:6, :])
            value = dy[at, :].astype(F32) + through
            grad_hidden[at, :] = value
            rounded = value.astype(BF16)
            branch[at, :] = rounded
            return (
                carry[0] + gains,
                carry[1] + biases,
                carry[2] + jnp.sum(rounded.astype(F32), axis=0, keepdims=True),
            )

        zero = jnp.zeros((1, width), F32)
        gains, biases, outs = lax.fori_loop(0, rows // 128, norm_step, (zero, zero, zero))
        sums[0:1, :] = gains
        sums[1:2, :] = biases
        sums[2:3, :] = outs


def up_grad(slope, dy, second_turned, fc1_w, fc2_w, hidden, vec, deps):
    rows, width = dy.shape
    ff = slope.shape[1]
    chunk = 768
    square = whole((rows, width))
    split = ((width // 4, ff), BF16, pl.BlockSpec((width // 4, chunk), lambda j: (0, j)))
    return run(
        up_grad_kernel,
        "up_grad",
        22,
        [
            (slope, pl.BlockSpec((rows, chunk), lambda j: (0, j))),
            (dy, square),
            (second_turned, whole((width, rows))),
            (fc1_w, pl.BlockSpec((width, chunk), lambda j: (0, j))),
            (fc2_w, pl.BlockSpec((chunk, width), lambda j: (j, 0))),
            (hidden, square),
            (vec, whole(vec.shape)),
        ],
        [
            split,
            split,
            split,
            split,
            ((1, ff), F32, pl.BlockSpec((1, chunk), lambda j: (0, j))),
            ((rows, width), F32, square),
            ((rows, width), BF16, square),
            ((3, width), F32, whole((3, width))),
        ],
        [pltpu.VMEM((rows, width), F32)],
        deps,
        (ff // chunk,),
    )


def attend_grad_kernel(length, with_out, branch, weight, packed, logsum, first_turned, *refs):
    if with_out:
        info, mixed_turned = refs[:2]
        grad_packed, sums, grad_mixed, turned = refs[6:]
    else:
        grad_packed, sums, grad_mixed = refs[4:]
    targets = refs[2:6] if with_out else refs[:4]
    rows, width = branch.shape
    side = width // 2
    grad_mixed[...] = dot_nt(branch[...], weight[...]).astype(BF16)

    pairs = side // 128
    blocks = length // 128
    causal = triangle(128)

    def pair_step(it, _):
        seq = it // pairs
        pair = it % pairs
        base = seq * length
        column = pair * 128
        at = pl.ds(pl.multiple_of(base, 128), length)
        at_query = pl.ds(pl.multiple_of(column, 128), 128)
        at_key = pl.ds(pl.multiple_of(side + column, 128), 128)
        at_value = pl.ds(pl.multiple_of(2 * side + column, 128), 128)
        query, key, value = packed[at, at_query], packed[at, at_key], packed[at, at_value]
        incoming = grad_mixed[at, at_query]
        lane = lax.broadcasted_iota(jnp.int32, query.shape, 1)
        results = []
        for head in range(2):
            here = (lane < HEAD) == (head == 0)
            query_h = jnp.where(here, query, jnp.zeros_like(query))
            incoming_h = jnp.where(here, incoming, jnp.zeros_like(incoming))
            probs, grads = [], []
            for kb in range(blocks):
                rows_k = slice(kb * 128, (kb + 1) * 128)
                scores = dot_nt(key[rows_k], query_h[kb * 128 :])
                stats = logsum[seq, pair * 2 + head, 0:1, kb * 128 :]
                expo = jnp.exp(scores - stats)
                diagonal = jnp.where(causal, expo[:, :128], 0.0)
                if kb < blocks - 1:
                    expo = jnp.concatenate([diagonal, expo[:, 128:]], axis=1)
                else:
                    expo = diagonal
                probs.append(expo)
                grads.append(dot_nt(value[rows_k], incoming_h[kb * 128 :]))
            inner = []
            for qb in range(blocks):
                total = None
                for kb in range(qb + 1):
                    cut = slice((qb - kb) * 128, (qb - kb + 1) * 128)
                    term = probs[kb][:, cut] * grads[kb][:, cut]
                    total = term if total is None else total + term
                inner.append(jnp.sum(total, axis=0, keepdims=True))
            inner = jnp.concatenate(inner, axis=1)
            score_grads = [
                (probs[kb] * (grads[kb] - inner[:, kb * 128 :])).astype(BF16)
                for kb in range(blocks)
            ]
            grad_values = [
                dot_nn(probs[kb].astype(BF16), incoming[kb * 128 :]) for kb in range(blocks)
            ]
            grad_keys = [dot_nn(score_grads[kb], query[kb * 128 :]) for kb in range(blocks)]
            grad_query = []
            for qb in range(blocks):
                tiles = [
                    score_grads[kb][:, (qb - kb) * 128 : (qb - kb + 1) * 128]
                    for kb in range(qb + 1)
                ]
                grad_query.append(dot_tn(key[: (qb + 1) * 128], jnp.concatenate(tiles, axis=0)))
            results.append((grad_values, grad_keys, grad_query))
        left = lax.broadcasted_iota(jnp.int32, (128, 128), 1) < HEAD
        for b in range(blocks):
            to = pl.ds(pl.multiple_of(base + b * 128, 128), 128)
            grad_packed[to, at_value] = jnp.where(left, results[0][0][b], results[1][0][b]).astype(
                BF16
            )
            grad_packed[to, at_key] = jnp.where(left, results[0][1][b], results[1][1][b]).astype(
                BF16
            )
            both = jnp.concatenate([results[0][2][b][:HEAD], results[1][2][b][HEAD:]], axis=0)
            grad_packed[to, at_query] = (both * HEAD**-0.5).astype(BF16).T
        return 0

    lax.fori_loop(0, (rows // length) * pairs, pair_step, 0, unroll=UNROLL_B)

    quarter = width // 4

    def place(grad, start, stop):
        grad = grad.astype(BF16)
        for slot, target in enumerate(targets):
            target[:, start:stop] = grad[slot * quarter : (slot + 1) * quarter]

    place(dot_nn(first_turned[...], grad_packed[...]), 0, 3 * side)
    sums[...] = jnp.sum(grad_packed[...].astype(F32), axis=0, keepdims=True)
    if with_out:
        copy_by_owner(info[0], mixed_turned, turned)
        place(dot_nn(turned[...], branch[...]), 3 * side, 3 * side + width)


def attend_grad(half, branch, weight, packed, logsum, first_turned, extra, length, deps):
    rows, width = branch.shape
    side = width // 2
    heads = side // HEAD
    seqs = rows // length
    with_out = half == 0
    columns = 3 * side + (width if with_out else 0)
    inputs = [
        (branch, whole((rows, width))),
        (weight, pl.BlockSpec((side, width), lambda i: (half, 0))),
        (packed, pl.BlockSpec((rows, 3 * side), lambda i: (0, half))),
        (logsum, pl.BlockSpec((seqs, heads, 1, length), lambda i: (0, half, 0, 0))),
        (first_turned, whole((width, rows))),
    ]
    scratch = [pltpu.VMEM((rows, side), BF16)]
    if with_out:
        info, mixed_turned = extra
        inputs += [(info, SMEM), (mixed_turned, whole((width, rows)))]
        scratch += [pltpu.VMEM((width, rows), BF16)]
    split = (width // 4, columns)
    return run(
        partial(attend_grad_kernel, length, with_out),
        "attend_grad",
        13,
        inputs,
        [
            (split, BF16, whole(split)),
            (split, BF16, whole(split)),
            (split, BF16, whole(split)),
            (split, BF16, whole(split)),
            ((rows, 3 * side), BF16, whole((rows, 3 * side))),
            ((1, 3 * side), F32, whole((1, 3 * side))),
        ],
        scratch,
        deps,
        (1,),
    )


def finish_kernel(
    grad_a, grad_b, tok, grad_hidden, vec, weight, act, hidden, fc2_w, in_grad, sums, out
):
    step = pl.program_id(0)

    @pl.when(step == 0)
    def _():
        sums[...] = jnp.zeros_like(sums)

    side = grad_a.shape[1] // 3
    parts = []
    for part in range(3):
        for grad in (grad_a, grad_b):
            parts.append(grad[:, part * side : (part + 1) * side])
    grad_first = dot_nt(jnp.concatenate(parts, axis=1), weight[...])
    through, gains, biases = norm_grad_rows(tok[...].astype(F32), grad_first, vec[0:1, :])
    in_grad[...] = (grad_hidden[...] + through).astype(BF16)
    sums[0:1, :] += gains
    sums[1:2, :] += biases
    out[...] = (hidden[...] + dot_nn(act[...], fc2_w[...]) + vec[7:8, :]).astype(BF16)


def finish(grad_a, grad_b, tok, grad_hidden, vec, weight, act, hidden, fc2_w, deps):
    rows, width = tok.shape
    ff = act.shape[1]
    block = 256
    by_row = pl.BlockSpec((block, width), lambda i: (i, 0))
    part = pl.BlockSpec((block, 3 * width // 2), lambda i: (i, 0))
    return run(
        finish_kernel,
        "finish",
        1e20,
        [
            (grad_a, part),
            (grad_b, part),
            (tok, by_row),
            (grad_hidden, by_row),
            (vec, whole(vec.shape)),
            (weight, whole(weight.shape)),
            (act, pl.BlockSpec((block, ff), lambda i: (i, 0))),
            (hidden, by_row),
            (fc2_w, whole(fc2_w.shape)),
        ],
        [
            ((rows, width), BF16, by_row),
            ((2, width), F32, whole((2, width))),
            ((rows, width), BF16, by_row),
        ],
        deps=deps,
        grid=(rows // block,),
    )


def assemble_kernel(grad_a, grad_b, qkv_grad, out_grad, vectors):
    rows = qkv_grad.shape[0]
    side = grad_b.shape[1] // 3
    for part in range(3):
        at = slice(part * side, (part + 1) * side)
        start = 2 * part * side
        qkv_grad[:, start : start + side] = grad_a[:, at].astype(F32)
        qkv_grad[:, start + side : start + 2 * side] = grad_b[:rows, at].astype(F32)
    out_grad[...] = grad_a[:, 3 * side :].astype(F32)
    vectors[...] = grad_b[rows : rows + 16, :].astype(F32)


def assemble(grad_a, grad_b):
    rows, columns = grad_a.shape
    wide = grad_b.shape[1]
    return run(
        assemble_kernel,
        "assemble",
        1,
        [(grad_a, VMEM), (grad_b, VMEM)],
        [
            ((rows, 2 * wide), F32, VMEM),
            ((rows, columns - wide), F32, VMEM),
            ((16, wide), F32, VMEM),
        ],
    )[:3]


def swap(value, axis, size, bit):
    return lax.ppermute(value, axis, [(i, i ^ bit) for i in range(size)])


def gate(*values):
    return run(lambda: None, "gate", 1, [], [], deps=values)[0][0]


def hold(values, after):
    count = len(values)
    shapes = [jax.ShapeDtypeStruct(value.shape, value.dtype) for value in values]
    return pl.pallas_call(
        lambda *_: None,
        in_specs=[HBM] * (count + len(after)),
        out_specs=[HBM] * count,
        out_shape=shapes,
        input_output_aliases={index: index for index in range(count)},
        cost_estimate=pl.CostEstimate(flops=1, bytes_accessed=1, transcendentals=0),
        name="hold",
    )(*values, *after)


def half_rows(block, half):
    part = block.shape[0] // 2
    return lax.dynamic_slice_in_dim(block, half * part, part, 0)


class Chain:
    def __init__(self, keep, send, rep, reps):
        self.rep, self.reps = rep, reps
        self.levels = list(range(reps.bit_length() - 1))
        self.back = self.levels[-2::-1]
        self.terms, self.far = [keep[0]], keep[1]
        self.got_far = swap(send[1], "shard", 4, 1)
        self.got = swap(send[0], "shard", 4, 1)
        self.total = None
        self.done = False

    def active(self):
        return not self.done

    def fold(self, token, extra=None):
        self.terms = self.terms + [self.got]
        if self.far is not None:
            total = jnp.where(token == 0, self.far.astype(F32) + self.got_far.astype(F32), 0.0)
            self.operand, self.far = total.astype(BF16), None
            if extra is not None:
                near = (self.terms[0].astype(F32) + self.got.astype(F32)).astype(BF16)
                self.terms = [jnp.concatenate([near, extra[0]], axis=0)]
                self.operand = jnp.concatenate([self.operand, extra[1]], axis=0)
            self.got = swap(self.operand, "shard", 4, 2)
        elif len(self.levels) > 1:
            level = self.levels.pop(0)
            bit = ((self.rep >> level) & 1) + token
            size = self.terms[0].shape[0] // 2
            self.operand = self.cut((1 - bit) * size, size)
            self.terms = [self.cut(bit * size, size)]
            self.got = swap(self.operand, "rep", self.reps, 1 << level)
        elif self.levels:
            level = self.levels.pop(0)
            self.operand = self.add(token)
            self.terms = [self.operand]
            self.got = swap(self.operand, "rep", self.reps, 1 << level)
        else:
            if self.total is None:
                self.total = self.add(token)
            else:
                first = ((self.rep >> self.level) & 1) + token == 0
                self.total = jnp.where(
                    first,
                    jnp.concatenate([self.total, self.got], axis=0),
                    jnp.concatenate([self.got, self.total], axis=0),
                )
            self.operand = self.total
            if self.back:
                self.level = self.back.pop(0)
                self.got = swap(self.total, "rep", self.reps, 1 << self.level)
            else:
                self.done = True
        return self.operand

    def add(self, token):
        total = sum(term.astype(F32) for term in self.terms)
        return jnp.where(token == 0, total, 0.0).astype(BF16)

    def cut(self, start, size):
        total = 0.0
        for term in self.terms:
            total = total + lax.dynamic_slice_in_dim(term, start, size, 0).astype(F32)
        return total.astype(BF16)


def on_device(
    reps,
    tokens,
    ln1_gain,
    ln1_bias,
    qkv_weight,
    query_bias,
    value_bias,
    out_weight,
    out_bias,
    ln2_gain,
    ln2_bias,
    fc1_weight,
    fc1_bias,
    fc2_weight,
    fc2_bias,
    cotangent,
):
    seqs_here, length, width = tokens.shape
    rows = seqs_here * length
    share = width // 4
    me = lax.axis_index("shard").astype(jnp.int32)
    rep = lax.axis_index("rep").astype(jnp.int32)
    half = rep & 1
    info = jnp.stack([me, half])
    tok = tokens.reshape(rows, width)
    dy = cotangent.reshape(rows, width)

    core = lambda value: swap(value, "shard", 4, 1)
    chip_x = lambda value: swap(value, "shard", 4, 2)
    chip_y = lambda value: swap(value, "rep", reps, 1)

    qkv_mine = half_rows(qkv_weight, half)
    qkv_far = chip_x(qkv_mine)
    early = gate(qkv_mine).astype(F32)
    small = jnp.concatenate(
        [
            v.reshape(-1, share).astype(F32) + early
            for v in (
                ln1_gain,
                ln1_bias,
                query_bias,
                value_bias,
                out_bias,
                ln2_gain,
                ln2_bias,
                fc2_bias,
                fc1_bias,
            )
        ],
        axis=0,
    )
    pair = jnp.stack([small, core(small)], axis=0)
    near = jnp.concatenate([pair, chip_x(pair)], axis=0)
    near = jnp.where((me & 1) == 0, near, near[jnp.array([1, 0, 3, 2])])
    near = jnp.where((me & 2) == 0, near, near[jnp.array([2, 3, 0, 1])])
    vec = near[:, :8].transpose(1, 0, 2).reshape(8, width)
    bias = near[:, 8:].reshape(1, -1)

    token = gate(qkv_far)
    joint_mine = jnp.concatenate(
        [half_rows(out_weight, half + token), half_rows(fc1_weight, half + token)], axis=1
    )
    joint_far = chip_x(joint_mine)
    qkv_far_b = chip_y(qkv_far)
    qkv = (qkv_weight, core(qkv_weight), qkv_far, qkv_far_b, core(qkv_far), core(qkv_far_b))
    packed, first_turned, qkv_full, token = project(info, tok, vec, qkv, [joint_mine, bias])

    fc2_mine = half_rows(fc2_weight, half)
    joint_far, fc2_mine = hold([joint_far, fc2_mine], [packed])
    joint_far_b = chip_y(joint_far)
    fc2_far = chip_x(fc2_mine)
    mixed, mixed_turned, logsum, token = attend(packed, length, [joint_far, fc2_mine])

    joint_far_b, fc2_far = hold([joint_far_b, fc2_far], [mixed])
    fc2_far_b = chip_y(fc2_far)
    joint = (
        out_weight,
        core(out_weight),
        fc1_weight,
        core(fc1_weight),
        joint_far,
        joint_far_b,
        core(joint_far),
        core(joint_far_b),
    )
    hidden, second_turned, act, slope, out_full, fc1_full, token = feed(
        info, mixed, tok, vec, bias, joint, [fc2_far]
    )

    def fold(token, *chains):
        return [one.fold(token) for one in chains if one.active()]

    (fc2_far_b,) = hold([fc2_far_b], [hidden])
    fc2 = (fc2_weight, core(fc2_weight), fc2_far, fc2_far_b, core(fc2_far), core(fc2_far_b))
    *send, fc2_full, token = down_grad(info, act, dy, fc2, [])
    *keep, sums_dy, token = down_grad(info, act, dy, (), send)
    chain2 = Chain(keep, send, rep, reps)
    sent = fold(token[0], chain2)
    *parts, sums_fc1, grad_hidden, branch, sums_ln2, token = up_grad(
        slope, dy, second_turned, fc1_full, fc2_full, hidden, vec, sent
    )
    chain1 = Chain(parts[:2], parts[2:], rep, reps)
    sent = fold(token[0], chain2)
    sent += fold(gate(*sent), chain1)
    *parts, grad_a, sums_qa, token = attend_grad(
        0, branch, out_full, packed, logsum, first_turned, (info, mixed_turned), length, sent
    )
    chain0a = Chain(parts[:2], parts[2:], rep, reps)
    sent = fold(token[0], chain2)
    *parts, grad_b, sums_qb, token = attend_grad(
        1, branch, out_full, packed, logsum, first_turned, None, length, sent
    )
    chain0b = Chain(parts[:2], parts[2:], rep, reps)
    sent = fold(token[0], chain1)
    sent += fold(gate(*sent), chain2, chain0a)
    in_grad, sums_ln1, output, token = finish(
        grad_a, grad_b, tok, grad_hidden, vec, qkv_full, act, hidden, fc2_full, sent
    )
    side = width // 2
    sums_packed = jnp.concatenate(
        [sums_qa[:, :side], sums_qb[:, :side], sums_qa[:, 2 * side :], sums_qb[:, 2 * side :]],
        axis=1,
    )
    sums = jnp.concatenate(
        [
            sums_ln1,
            sums_packed.reshape(2, width),
            sums_ln2,
            sums_dy,
            sums_fc1.reshape(4, width),
        ],
        axis=0,
    )
    later = gate(*fold(token[0], chain0a))
    later = gate(*fold(later, chain2, chain1))
    sums = sums + later.astype(F32)
    sums = sums + core(sums)
    columns = 3 * side
    row_count = 3 * width // columns

    def owned(owner):
        vectors = lax.dynamic_slice(sums, (0, owner * share), (8, share)).reshape(-1)
        wide = lax.dynamic_slice(sums, (8 + owner, 0), (1, width)).reshape(-1)
        rows_here = jnp.concatenate([vectors, wide]).reshape(row_count, columns)
        return jnp.pad(rows_here, ((0, 32 - row_count), (0, 0))).astype(BF16)

    extra = [owned(me), owned(me ^ 2)]
    chain0b.fold(later, extra)
    fold(0, chain0a, chain1, chain2)
    fold(gate(chain0b.fold(0)), chain0a, chain1)
    going = [chain0b, chain0a, chain1, chain2]
    while any(one.active() for one in going):
        fold(0, *going)
    total2 = chain2.total.astype(F32)
    total1 = chain1.total.astype(F32)
    qkv_grad, out_grad, vectors = assemble(chain0a.total, chain0b.total)
    vectors = vectors[:row_count].reshape(-1)
    mine = vectors[: 8 * share].reshape(8, share)
    fc1b = vectors[8 * share :]
    return (
        output.reshape(tokens.shape),
        in_grad.reshape(tokens.shape),
        mine[0],
        mine[1],
        qkv_grad,
        mine[2],
        mine[3],
        out_grad,
        mine[6],
        mine[4],
        mine[5],
        total1,
        fc1b,
        total2,
        mine[7],
    )


def solution(mesh):
    spread = P(("rep", "shard"), None, None)
    matrix = P("shard", None)
    vector = P("shard")
    return jax.shard_map(
        partial(on_device, mesh.shape["rep"]),
        mesh=mesh,
        in_specs=(
            spread, vector, vector, matrix, vector, vector, matrix, vector,
            vector, vector, matrix, vector, matrix, vector, spread,
        ),
        out_specs=(
            spread, spread, vector, vector, matrix, vector, vector, matrix,
            vector, vector, vector, matrix, vector, matrix, vector,
        ),
        check_vma=False,
    )
```
